32 devices in a mesh: gx: 8 (over y, x, core), gy: 4 (over z).
Axes of the slice: x: 2, y: 2, z: 4, core: 2. Of those that a mesh axis runs over, the one named last changes fastest.
Arguments:
- volume: bfloat16 [64, 16, 64, 128], P(None, 'gx', 'gy'), may hold values from -6 to 6
- kernel: bfloat16 [4, 4, 4, 32, 64], replicated, may hold values from -0.25 to 0.25
- cotangent: bfloat16 [2, 2, 2, 32, 16, 64, 128], P(None, None, None, None, 'gx', 'gy'), may hold values from -6 to 6
Outputs:
- activation: bfloat16 [2, 2, 2, 32, 16, 64, 128], P(None, None, None, None, 'gx', 'gy')
- input_grad: bfloat16 [64, 16, 64, 128], P(None, 'gx', 'gy')
- weight_grad: float32 [4, 4, 4, 32, 64], replicated
The draws below stay inside these ranges and needn't reach their ends.
All inputs are finite; a program needn't handle non-finite values.
Results may differ from the reference program's by a relative error of at most 0.0049.
Values may be sent and summed in bfloat16 or wider, within the bound.
No kernel may reach another device: no remote copies, remote signals or barrier semaphores. Data moves between devices by JAX's collectives and lax.ppermute only.
A program may use at most 192 MiB of HBM per device.

```python
import math
import jax
import jax.numpy as jnp

CI = 64
CO = 32
K = 4
NZ = 128
NX = 16
NY = 64


def levels(key, extent, split, least, top_value):
    level, own = 1.0, jax.random.fold_in(key, 6)
    for position, blocks in split:
        steps = jnp.exp(jax.random.uniform(jax.random.fold_in(own, position), (blocks,), jnp.float32, least / len(split), top_value / len(split)))
        level = level * jnp.repeat(steps, extent[position] // blocks).reshape([-1 if axis == position else 1 for axis in range(len(extent))])
    return level


def scatter_about(own_key, dims, scale, bound, pieces=(), dtype=jnp.bfloat16):
    result = scale * jax.random.normal(own_key, dims, jnp.float32)
    if pieces:
        result = result * levels(own_key, dims, pieces, -0.22, 0.18)
    return jnp.clip(result, -bound, bound).astype(dtype)


def setup_inputs(seed: int = 0) -> dict:
    key_list = jax.random.split(jax.random.key(seed), 4)
    return {
        "volume": scatter_about(key_list[0], (CI, NX, NY, NZ), 1.0, 6.0, ((1, 8), (2, 4))),
        "kernel": scatter_about(key_list[1], (K, K, K, CO, CI), (8 * CI) ** -0.5, 0.25),
        "cotangent": scatter_about(key_list[2], (2, 2, 2, CO, NX, NY, NZ), 1.0, 6.0, ((4, 8), (5, 4))),
    }


FORWARD_TAPS = (((1, 0), (3, -1)), ((2, 0), (0, 1)))
BACK_TAPS = ((1, -1), (0, 0), (1, 0), (0, 1))

def silu_pair(before):
    sigmoid = jax.nn.sigmoid(before)
    return (before * sigmoid, sigmoid * (1.0 + before * (1.0 - sigmoid)))

def reference(volume, kernel, cotangent):
    cells = NX * NY * NZ
    padded = jnp.pad(volume, ((0, 0), (1, 1), (1, 1), (1, 1)))
    act_phases = []
    grad_phases = []
    for phase_x in range(2):
        for phase_y in range(2):
            for phase_z in range(2):
                running = jnp.zeros((CO, cells), jnp.float32)
                for tap_x, shift_x in FORWARD_TAPS[phase_x]:
                    for tap_y, shift_y in FORWARD_TAPS[phase_y]:
                        for tap_z, shift_z in FORWARD_TAPS[phase_z]:
                            sliced = padded[:, 1 + shift_x:1 + shift_x + NX, 1 + shift_y:1 + shift_y + NY, 1 + shift_z:1 + shift_z + NZ].reshape(CI, cells)
                            running = running + jnp.dot(kernel[tap_x, tap_y, tap_z], sliced, preferred_element_type=jnp.float32)
                values, slopes = silu_pair(running)
                act_phases.append(values.astype(jnp.bfloat16).reshape(CO, NX, NY, NZ))
                cot_phase = cotangent[phase_x, phase_y, phase_z].reshape(CO, cells)
                grad_phase = (cot_phase.astype(jnp.float32) * slopes).astype(jnp.bfloat16)
                grad_phases.append(jnp.pad(grad_phase.reshape(CO, NX, NY, NZ), ((0, 0), (1, 1), (1, 1), (1, 1))))
    activation = jnp.stack(act_phases).reshape(2, 2, 2, CO, NX, NY, NZ)
    flat_volume = volume.reshape(CI, cells)
    back_sum = jnp.zeros((CI, cells), jnp.float32)
    weight_parts = []
    for tap_x in range(K):
        for tap_y in range(K):
            for tap_z in range(K):
                phase_x, shift_x = BACK_TAPS[tap_x]
                phase_y, shift_y = BACK_TAPS[tap_y]
                phase_z, shift_z = BACK_TAPS[tap_z]
                source = grad_phases[4 * phase_x + 2 * phase_y + phase_z]
                sliced = source[:, 1 + shift_x:1 + shift_x + NX, 1 + shift_y:1 + shift_y + NY, 1 + shift_z:1 + shift_z + NZ].reshape(CO, cells)
                back_sum = back_sum + jnp.dot(kernel[tap_x, tap_y, tap_z].T, sliced, preferred_element_type=jnp.float32)
                weight_parts.append(jnp.dot(sliced, flat_volume.T, preferred_element_type=jnp.float32))
    scaling = 1.0 / math.sqrt(NX * NY * NZ)
    weight_grad = jnp.stack(weight_parts).reshape(K, K, K, CO, CI) * scaling
    input_grad = back_sum.astype(jnp.bfloat16).reshape(CI, NX, NY, NZ)
    return (activation, input_grad, weight_grad)
```

```python
import functools
import math

import jax
import jax.numpy as jnp
from jax import lax
from jax.experimental import pallas as pl
from jax.experimental.pallas import tpu as pltpu
from jax.sharding import PartitionSpec as P

F32 = jnp.float32
BF16 = jnp.bfloat16


def forward_kernel(nx, ny, nz, ci, co, chunk, ext, xlo, xhi, w, cot, act, g, wg, vm, ga, gb):
    half = 4 * ci
    rows = 8 * co

    def plain(x, lanes):
        if x == 0:
            return xlo[0, :, lanes]
        if x == nx + 1:
            return xhi[0, :, lanes]
        return ext[x - 1, :, lanes]

    def corners(get, i, j0, j1):
        return jnp.concatenate(
            [
                get(i + 1 - ex, slice((j0 + 1 - ey) * nz, (j1 + 1 - ey) * nz))
                for ex in range(2)
                for ey in range(2)
            ],
            axis=0,
        )

    def rolled(x, lanes):
        return vm[x, :, lanes]

    for x in range(nx + 2):
        for y in range(ny + 2):
            lanes = slice(y * nz, (y + 1) * nz)
            vm[x, :, lanes] = pltpu.roll(plain(x, lanes).astype(F32), 1, 1).astype(BF16)

    first = lax.broadcasted_iota(jnp.int32, (co, nz), 1) == 0
    zeros = jnp.zeros((2 * co, nz), BF16)

    for i in range(nx + 1):
        for j0 in range(0, ny + 1, chunk):
            j1 = min(j0 + chunk, ny + 1)
            back = jnp.dot(w[:, half:], corners(rolled, i, j0, j1), preferred_element_type=F32)
            here = jnp.dot(w[:, :half], corners(plain, i, j0, j1), preferred_element_type=F32)
            for j in range(j0, j1):
                cols = slice((j - j0) * nz, (j - j0 + 1) * nz)
                wide = slice(j * nz, (j + 1) * nz)
                for tx in range(2):
                    for ty in range(2):
                        sx, sy = 1 - tx, 1 - ty
                        m, n = i - sx, j - sy
                        base = (2 * tx + ty) * 2 * co
                        if not (0 <= m < nx and 0 <= n < ny):
                            g[i, base : base + 2 * co, wide] = zeros
                            ga[i, base : base + 2 * co, wide] = zeros
                            gb[i, base : base + 2 * co, wide] = zeros
                            continue
                        out = slice(n * nz, (n + 1) * nz)
                        for tz in range(2):
                            sz = 1 - tz
                            r = slice(base + tz * co, base + (tz + 1) * co)
                            low, high = back[r, cols], here[r, cols]
                            if sz == 1:
                                before = low + jnp.where(first, 0.0, high)
                                before = pltpu.roll(before, nz - 1, 1)
                            else:
                                before = jnp.where(first, 0.0, low) + high
                            q = ((2 * sx + sy) * 2 + sz) * co
                            sig = 0.5 * jnp.tanh(0.5 * before) + 0.5
                            value = before * sig
                            act[m, q : q + co, out] = value.astype(BF16)
                            slope = sig + value * (1.0 - sig)
                            grad = cot[m, q : q + co, out].astype(F32) * slope
                            if sz == 1:
                                grad = pltpu.roll(grad, 1, 1)
                            whole = grad.astype(BF16)
                            cut = jnp.where(first, 0.0, grad).astype(BF16)
                            g[i, r, wide] = whole
                            ga[i, r, wide] = cut if sz == 0 else whole
                            gb[i, r, wide] = cut if sz == 1 else whole

    nt = (((1,), (1,)), ((), ()))
    for part, (grads, get) in enumerate(((gb, plain), (ga, rolled))):
        total = None
        for i in range(nx + 1):
            term = lax.dot_general(
                grads[i], corners(get, i, 0, ny + 1), nt, preferred_element_type=F32
            )
            total = term if total is None else total + term
        wg[:, part * half : (part + 1) * half] = total


def backward_kernel(nx, ny, nz, ci, co, chunk, g, wt, ig, u):
    half = 4 * ci
    rows = 8 * co
    shape = (rows, nz)
    first = lax.broadcasted_iota(jnp.int32, shape, 1) == 0
    phase = (lax.broadcasted_iota(jnp.int32, shape, 0) // co) % 2
    cut_a = first & (phase == 1)
    cut_b = first & (phase == 0)
    for i in range(nx + 1):
        for j0 in range(0, ny + 1, chunk):
            j1 = min(j0 + chunk, ny + 1)
            lefts, rights = [], []
            for j in range(j0, j1):
                piece = g[i, :, j * nz : (j + 1) * nz].astype(F32)
                lefts.append(jnp.where(cut_a, 0.0, piece).astype(BF16))
                rights.append(jnp.where(cut_b, 0.0, piece).astype(BF16))
            back = jnp.dot(wt[half:], jnp.concatenate(lefts, axis=1), preferred_element_type=F32)
            here = jnp.dot(wt[:half], jnp.concatenate(rights, axis=1), preferred_element_type=F32)
            for j in range(j0, j1):
                cols = slice((j - j0) * nz, (j - j0 + 1) * nz)
                u[i, :, j * nz : (j + 1) * nz] = here[:, cols] + pltpu.roll(
                    back[:, cols], nz - 1, 1
                )
    for m in range(-1, nx + 1):
        for y in range(-1, ny + 1):
            total = None
            for ex in range(2):
                for ey in range(2):
                    i, j = m + ex, y + ey
                    if 0 <= i <= nx and 0 <= j <= ny:
                        r = (2 * ex + ey) * ci
                        term = u[i, r : r + ci, j * nz : (j + 1) * nz]
                        total = term if total is None else total + term
            ig[m + 1, :, (y + 1) * nz : (y + 2) * nz] = total


def neighbours(axis):
    count = lax.axis_size(axis)
    up = [(i, i + 1) for i in range(count - 1)]
    return up, [(b, a) for a, b in up]


def on_device(volume, kernel, cotangent):
    ci, nx, ny, nz = volume.shape
    co = kernel.shape[3]
    gx_up, gx_down = neighbours("gx")
    gy_up, gy_down = neighbours("gy")
    devices = lax.axis_size("gx") * lax.axis_size("gy")
    cells = nx * lax.axis_size("gx") * ny * lax.axis_size("gy") * nz

    flat = volume.transpose(1, 0, 2, 3).reshape(nx, ci, ny * nz)
    ylo = lax.ppermute(flat[:, :, (ny - 1) * nz :], "gy", gy_up)
    yhi = lax.ppermute(flat[:, :, :nz], "gy", gy_down)
    ext = jnp.concatenate([ylo, flat, yhi], axis=2)
    xlo = lax.ppermute(ext[nx - 1 :], "gx", gx_up)
    xhi = lax.ppermute(ext[:1], "gx", gx_down)

    taps = kernel.reshape(2, 2, 2, 2, 2, 2, co, ci)
    w = taps.transpose(1, 3, 5, 6, 4, 0, 2, 7).reshape(8 * co, 8 * ci)
    wt = w.T
    cot = (
        cotangent.reshape(8 * co, nx, ny, nz).transpose(1, 0, 2, 3).reshape(nx, 8 * co, ny * nz)
    )

    vmem = pl.BlockSpec(memory_space=pltpu.VMEM)
    chunk = 4
    act, g, wg = pl.pallas_call(
        functools.partial(forward_kernel, nx, ny, nz, ci, co, chunk),
        out_shape=(
            jax.ShapeDtypeStruct((nx, 8 * co, ny * nz), BF16),
            jax.ShapeDtypeStruct((nx + 1, 8 * co, (ny + 1) * nz), BF16),
            jax.ShapeDtypeStruct((8 * co, 8 * ci), F32),
        ),
        in_specs=[vmem] * 5,
        out_specs=(vmem,) * 3,
        scratch_shapes=[
            pltpu.VMEM((nx + 2, ci, (ny + 2) * nz), BF16),
            pltpu.VMEM((nx + 1, 8 * co, (ny + 1) * nz), BF16),
            pltpu.VMEM((nx + 1, 8 * co, (ny + 1) * nz), BF16),
        ],
        compiler_params=pltpu.CompilerParams(vmem_limit_bytes=48 * 1024 * 1024),
    )(ext, xlo, xhi, w, cot)

    shares = wg.astype(BF16).reshape(devices, 8 * co * 8 * ci // devices // 128, 128)
    mine = lax.all_to_all(shares, ("gx", "gy"), 0, 0, tiled=True)
    scale = 1.0 / math.sqrt(cells)
    summed = (jnp.sum(mine.astype(F32), axis=0) * scale).astype(F32)
    spread = jnp.broadcast_to(summed[None], (devices,) + summed.shape)
    gathered = lax.all_to_all(spread, ("gx", "gy"), 0, 0, tiled=True)
    weight_grad = (
        gathered.reshape(2, 2, 2, co, 2, 2, 2, ci)
        .transpose(5, 0, 6, 1, 4, 2, 3, 7)
        .reshape(4, 4, 4, co, ci)
    )

    ig = pl.pallas_call(
        functools.partial(backward_kernel, nx, ny, nz, ci, co, chunk),
        out_shape=jax.ShapeDtypeStruct((nx + 2, ci, (ny + 2) * nz), F32),
        in_specs=[vmem] * 2,
        out_specs=vmem,
        scratch_shapes=[pltpu.VMEM((nx + 1, 4 * ci, (ny + 1) * nz), F32)],
        compiler_params=pltpu.CompilerParams(vmem_limit_bytes=48 * 1024 * 1024),
    )(g, wt)
    from_low = lax.ppermute(ig[nx + 1 :].astype(BF16), "gx", gx_up).astype(F32)
    from_high = lax.ppermute(ig[:1].astype(BF16), "gx", gx_down).astype(F32)
    zero = jnp.zeros((nx - 1,) + from_low.shape[1:], F32)
    mid = (
        ig[1 : nx + 1]
        + jnp.concatenate([from_low, zero], axis=0)
        + jnp.concatenate([zero, from_high], axis=0)
    )
    y_low = lax.ppermute(mid[:, :, (ny + 1) * nz :].astype(BF16), "gy", gy_up).astype(F32)
    y_high = lax.ppermute(mid[:, :, :nz].astype(BF16), "gy", gy_down).astype(F32)
    gap = jnp.zeros((nx, ci, (ny - 1) * nz), F32)
    full = (
        mid[:, :, nz : (ny + 1) * nz]
        + jnp.concatenate([y_low, gap], axis=2)
        + jnp.concatenate([gap, y_high], axis=2)
    )
    input_grad = full.astype(BF16).reshape(nx, ci, ny, nz).transpose(1, 0, 2, 3)
    activation = (
        act.reshape(nx, 8 * co, ny, nz).transpose(1, 0, 2, 3).reshape(cotangent.shape)
    )
    return activation, input_grad, weight_grad


def solution(mesh):
    placed = (P(None, "gx", "gy", None), P(), P(None, None, None, None, "gx", "gy", None))
    return jax.shard_map(
        on_device,
        mesh=mesh,
        in_specs=placed,
        out_specs=(placed[2], placed[0], P()),
        check_vma=False,
    )
```

```python
import functools
import math

import jax
import jax.numpy as jnp
from jax import lax
from jax.experimental import pallas as pl
from jax.experimental.pallas import tpu as pltpu
from jax.sharding import PartitionSpec as P

F32 = jnp.float32
BF16 = jnp.bfloat16


def forward_kernel(nx, ny, nz, ci, co, chunk, ext, xlo, xhi, w, cot, act, g, wg, vm, ga, gb):
    half = 4 * ci
    rows = 8 * co

    def plain(x, lanes):
        if x == 0:
            return xlo[0, :, lanes]
        if x == nx + 1:
            return xhi[0, :, lanes]
        return ext[x - 1, :, lanes]

    def corners(get, i, j0, j1):
        return jnp.concatenate(
            [
                get(i + 1 - ex, slice((j0 + 1 - ey) * nz, (j1 + 1 - ey) * nz))
                for ex in range(2)
                for ey in range(2)
            ],
            axis=0,
        )

    def rolled(x, lanes):
        return vm[x, :, lanes]

    for x in range(nx + 2):
        for y in range(ny + 2):
            lanes = slice(y * nz, (y + 1) * nz)
            vm[x, :, lanes] = pltpu.roll(plain(x, lanes).astype(F32), 1, 1).astype(BF16)

    first = lax.broadcasted_iota(jnp.int32, (co, nz), 1) == 0
    zeros = jnp.zeros((2 * co, nz), BF16)

    for i in range(nx + 1):
        for j0 in range(0, ny + 1, chunk):
            j1 = min(j0 + chunk, ny + 1)
            back = jnp.dot(w[:, half:], corners(rolled, i, j0, j1), preferred_element_type=F32)
            here = jnp.dot(w[:, :half], corners(plain, i, j0, j1), preferred_element_type=F32)
            for j in range(j0, j1):
                cols = slice((j - j0) * nz, (j - j0 + 1) * nz)
                wide = slice(j * nz, (j + 1) * nz)
                for tx in range(2):
                    for ty in range(2):
                        sx, sy = 1 - tx, 1 - ty
                        m, n = i - sx, j - sy
                        base = (2 * tx + ty) * 2 * co
                        if not (0 <= m < nx and 0 <= n < ny):
                            g[i, base : base + 2 * co, wide] = zeros
                            ga[i, base : base + 2 * co, wide] = zeros
                            gb[i, base : base + 2 * co, wide] = zeros
                            continue
                        out = slice(n * nz, (n + 1) * nz)
                        for tz in range(2):
                            sz = 1 - tz
                            r = slice(base + tz * co, base + (tz + 1) * co)
                            low, high = back[r, cols], here[r, cols]
                            if sz == 1:
                                before = low + jnp.where(first, 0.0, high)
                                before = pltpu.roll(before, nz - 1, 1)
                            else:
                                before = jnp.where(first, 0.0, low) + high
                            q = ((2 * sx + sy) * 2 + sz) * co
                            sig = 0.5 * jnp.tanh(0.5 * before) + 0.5
                            value = before * sig
                            act[m, q : q + co, out] = value.astype(BF16)
                            slope = sig + value * (1.0 - sig)
                            grad = cot[m, q : q + co, out].astype(F32) * slope
                            if sz == 1:
                                grad = pltpu.roll(grad, 1, 1)
                            whole = grad.astype(BF16)
                            cut = jnp.where(first, 0.0, grad).astype(BF16)
                            g[i, r, wide] = whole
                            ga[i, r, wide] = cut if sz == 0 else whole
                            gb[i, r, wide] = cut if sz == 1 else whole

    nt = (((1,), (1,)), ((), ()))
    for part, (grads, get) in enumerate(((gb, plain), (ga, rolled))):
        total = None
        for i in range(nx + 1):
            term = lax.dot_general(
                grads[i], corners(get, i, 0, ny + 1), nt, preferred_element_type=F32
            )
            total = term if total is None else total + term
        for ex in range(2):
            for tx in range(2):
                for ty in range(2):
                    for tz in range(2):
                        r = ((2 * tx + ty) * 2 + tz) * co
                        block = (((2 * ex + tx) * 2 + ty) * 2 + part) * 2 + tz
                        wg[block] = total[
                            r : r + co, ex * 2 * ci : (ex + 1) * 2 * ci
                        ].astype(BF16)


def backward_kernel(nx, ny, nz, ci, co, chunk, g, wt, ig, u):
    half = 4 * ci
    rows = 8 * co
    shape = (rows, nz)
    first = lax.broadcasted_iota(jnp.int32, shape, 1) == 0
    phase = (lax.broadcasted_iota(jnp.int32, shape, 0) // co) % 2
    cut_a = first & (phase == 1)
    cut_b = first & (phase == 0)
    for i in range(nx + 1):
        for j0 in range(0, ny + 1, chunk):
            j1 = min(j0 + chunk, ny + 1)
            lefts, rights = [], []
            for j in range(j0, j1):
                piece = g[i, :, j * nz : (j + 1) * nz].astype(F32)
                lefts.append(jnp.where(cut_a, 0.0, piece).astype(BF16))
                rights.append(jnp.where(cut_b, 0.0, piece).astype(BF16))
            back = jnp.dot(wt[half:], jnp.concatenate(lefts, axis=1), preferred_element_type=F32)
            here = jnp.dot(wt[:half], jnp.concatenate(rights, axis=1), preferred_element_type=F32)
            for j in range(j0, j1):
                cols = slice((j - j0) * nz, (j - j0 + 1) * nz)
                u[i, :, j * nz : (j + 1) * nz] = here[:, cols] + pltpu.roll(
                    back[:, cols], nz - 1, 1
                )
    for m in range(-1, nx + 1):
        for y in range(-1, ny + 1):
            total = None
            for ex in range(2):
                for ey in range(2):
                    i, j = m + ex, y + ey
                    if 0 <= i <= nx and 0 <= j <= ny:
                        r = (2 * ex + ey) * ci
                        term = u[i, r : r + ci, j * nz : (j + 1) * nz]
                        total = term if total is None else total + term
            ig[m + 1, :, (y + 1) * nz : (y + 2) * nz] = total


def sum_kernel(scale, shares, *refs):
    out = refs[2] if len(refs) > 1 else refs[0]
    total = shares[0].astype(F32)
    for k in range(1, shares.shape[0]):
        total = total + shares[k].astype(F32)
    rounded = (total * scale).astype(BF16)
    for k in range(out.shape[0]):
        out[k] = rounded


def unpack_kernel(co, ci, packed, out):
    for ex in range(2):
        for tx in range(2):
            for ty in range(2):
                for ez in range(2):
                    for tz in range(2):
                        block = (((2 * ex + tx) * 2 + ty) * 2 + ez) * 2 + tz
                        pair = packed[block].astype(F32)
                        for ey in range(2):
                            out[2 * ex + tx, 2 * ey + ty, 2 * ez + tz] = pair[
                                :, ey * ci : (ey + 1) * ci
                            ]


def neighbours(axis):
    count = lax.axis_size(axis)
    up = [(i, i + 1) for i in range(count - 1)]
    return up, [(b, a) for a, b in up]


def on_device(volume, kernel, cotangent):
    ci, nx, ny, nz = volume.shape
    co = kernel.shape[3]
    gx_up, gx_down = neighbours("gx")
    gy_up, gy_down = neighbours("gy")
    devices = lax.axis_size("gx") * lax.axis_size("gy")
    cells = nx * lax.axis_size("gx") * ny * lax.axis_size("gy") * nz

    flat = volume.transpose(1, 0, 2, 3).reshape(nx, ci, ny * nz)
    ylo = lax.ppermute(flat[:, :, (ny - 1) * nz :], "gy", gy_up)
    yhi = lax.ppermute(flat[:, :, :nz], "gy", gy_down)
    ext = jnp.concatenate([ylo, flat, yhi], axis=2)
    xlo = lax.ppermute(ext[nx - 1 :], "gx", gx_up)
    xhi = lax.ppermute(ext[:1], "gx", gx_down)

    taps = kernel.reshape(2, 2, 2, 2, 2, 2, co, ci)
    w = taps.transpose(1, 3, 5, 6, 4, 0, 2, 7).reshape(8 * co, 8 * ci)
    wt = w.T
    cot = (
        cotangent.reshape(8 * co, nx, ny, nz).transpose(1, 0, 2, 3).reshape(nx, 8 * co, ny * nz)
    )

    vmem = pl.BlockSpec(memory_space=pltpu.VMEM)
    anywhere = pl.BlockSpec(memory_space=pl.ANY)
    chunk = 4
    act, g, wg = pl.pallas_call(
        functools.partial(forward_kernel, nx, ny, nz, ci, co, chunk),
        out_shape=(
            jax.ShapeDtypeStruct((nx, 8 * co, ny * nz), BF16),
            jax.ShapeDtypeStruct((nx + 1, 8 * co, (ny + 1) * nz), BF16),
            jax.ShapeDtypeStruct((32, co, 2 * ci), BF16),
        ),
        in_specs=[vmem] * 5,
        out_specs=(vmem,) * 3,
        scratch_shapes=[
            pltpu.VMEM((nx + 2, ci, (ny + 2) * nz), BF16),
            pltpu.VMEM((nx + 1, 8 * co, (ny + 1) * nz), BF16),
            pltpu.VMEM((nx + 1, 8 * co, (ny + 1) * nz), BF16),
        ],
        compiler_params=pltpu.CompilerParams(vmem_limit_bytes=48 * 1024 * 1024),
    )(ext, xlo, xhi, w, cot)

    scale = 1.0 / math.sqrt(cells)
    wide = lax.axis_size("gx")
    tall = lax.axis_size("gy")
    piece = 8 * co * 4 // wide
    first = lax.all_to_all(wg.reshape(wide, piece, 2 * ci), "gx", 0, 0, tiled=True)

    ig = pl.pallas_call(
        functools.partial(backward_kernel, nx, ny, nz, ci, co, chunk),
        out_shape=jax.ShapeDtypeStruct((nx + 2, ci, (ny + 2) * nz), F32),
        in_specs=[vmem] * 2,
        out_specs=vmem,
        scratch_shapes=[pltpu.VMEM((nx + 1, 4 * ci, (ny + 1) * nz), F32)],
        compiler_params=pltpu.CompilerParams(vmem_limit_bytes=48 * 1024 * 1024),
    )(g, wt)
    send_up = ig[nx + 1 :].astype(BF16)
    send_down = ig[:1].astype(BF16)
    part, send_up, send_down = pl.pallas_call(
        functools.partial(sum_kernel, 1.0),
        out_shape=(
            jax.ShapeDtypeStruct((tall, piece, 2 * ci), BF16),
            jax.ShapeDtypeStruct(send_up.shape, BF16),
            jax.ShapeDtypeStruct(send_down.shape, BF16),
        ),
        in_specs=[vmem, anywhere, anywhere],
        out_specs=(vmem, anywhere, anywhere),
        input_output_aliases={1: 1, 2: 2},
    )(first, send_up, send_down)
    second = lax.all_to_all(part, "gy", 0, 0, tiled=True)
    from_low = lax.ppermute(send_up, "gx", gx_up).astype(F32)
    from_high = lax.ppermute(send_down, "gx", gx_down).astype(F32)
    total = pl.pallas_call(
        functools.partial(sum_kernel, scale),
        out_shape=jax.ShapeDtypeStruct((wide, piece, 2 * ci), BF16),
        in_specs=[vmem],
        out_specs=vmem,
    )(second)
    third = lax.all_to_all(total, "gx", 0, 0, tiled=True)
    weight_grad = pl.pallas_call(
        functools.partial(unpack_kernel, co, ci),
        out_shape=jax.ShapeDtypeStruct((4, 4, 4, co, ci), F32),
        in_specs=[vmem],
        out_specs=vmem,
    )(third.reshape(32, co, 2 * ci))
    zero = jnp.zeros((nx - 1,) + from_low.shape[1:], F32)
    mid = (
        ig[1 : nx + 1]
        + jnp.concatenate([from_low, zero], axis=0)
        + jnp.concatenate([zero, from_high], axis=0)
    )
    y_low = lax.ppermute(mid[:, :, (ny + 1) * nz :].astype(BF16), "gy", gy_up).astype(F32)
    y_high = lax.ppermute(mid[:, :, :nz].astype(BF16), "gy", gy_down).astype(F32)
    gap = jnp.zeros((nx, ci, (ny - 1) * nz), F32)
    full = (
        mid[:, :, nz : (ny + 1) * nz]
        + jnp.concatenate([y_low, gap], axis=2)
        + jnp.concatenate([gap, y_high], axis=2)
    )
    input_grad = full.astype(BF16).reshape(nx, ci, ny, nz).transpose(1, 0, 2, 3)
    activation = (
        act.reshape(nx, 8 * co, ny, nz).transpose(1, 0, 2, 3).reshape(cotangent.shape)
    )
    return activation, input_grad, weight_grad


def solution(mesh):
    placed = (P(None, "gx", "gy", None), P(), P(None, None, None, None, "gx", "gy", None))
    return jax.shard_map(
        on_device,
        mesh=mesh,
        in_specs=placed,
        out_specs=(placed[2], placed[0], P()),
        check_vma=False,
    )
```

```python
import functools
import math

import jax
import jax.numpy as jnp
from jax import lax
from jax.experimental import pallas as pl
from jax.experimental.pallas import tpu as pltpu
from jax.sharding import PartitionSpec as P

F32 = jnp.float32
BF16 = jnp.bfloat16
GROUP = 16


def swap_matrix(outer, inner):
    size = outer * inner
    row = lax.broadcasted_iota(jnp.int32, (size, size), 0)
    col = lax.broadcasted_iota(jnp.int32, (size, size), 1)
    return jnp.where(col == (row % outer) * inner + row // outer, 1.0, 0.0).astype(BF16)


def brick_pass(dims, chunk, duals, block, cot, w, wt, act_out, wg_add, ig_add, scratch):
    nx, ny, nz, ci, co = dims
    vm, ga, gb, cots, vals, staged, sems = scratch
    half = 4 * ci
    slot = {i: k for k, i in enumerate(duals)}
    planes = sorted({i + 1 - e for i in duals for e in range(2)})
    place = {x: k for k, x in enumerate(planes)}
    split = co // GROUP

    for x in planes:
        for y in range(ny + 2):
            lanes = slice(y * nz, (y + 1) * nz)
            vm[place[x], :, lanes] = pltpu.roll(block(x, y).astype(F32), 1, 1).astype(BF16)

    def rolled(x, y):
        return vm[place[x], :, y * nz : (y + 1) * nz]

    def corners(get, i, j0, j1):
        return jnp.concatenate(
            [
                jnp.concatenate([get(i + 1 - ex, j + 1 - ey) for j in range(j0, j1)], axis=1)
                for ex in range(2)
                for ey in range(2)
            ],
            axis=0,
        )

    pairs = [
        (i, sx, i - sx, sy, sz)
        for i in duals
        for sx in range(2)
        if 0 <= i - sx < nx
        for sy in range(2)
        for sz in range(2)
    ]

    to_y = swap_matrix(GROUP, ny)
    for i, sx, m, sy, sz in pairs:
        q = (2 * sx + sy) * 2 + sz
        raw = jnp.concatenate(
            [
                cot[q, k * GROUP : (k + 1) * GROUP, m].reshape(GROUP * ny, nz)
                for k in range(split)
            ],
            axis=1,
        )
        moved = jnp.dot(to_y, raw, preferred_element_type=F32).astype(BF16)
        for y in range(ny):
            for k in range(split):
                cots[
                    slot[i],
                    q * co + k * GROUP : q * co + (k + 1) * GROUP,
                    y * nz : (y + 1) * nz,
                ] = moved[y * GROUP : (y + 1) * GROUP, k * nz : (k + 1) * nz]

    first = lax.broadcasted_iota(jnp.int32, (co, nz), 1) == 0
    zeros = jnp.zeros((2 * co, nz), BF16)
    started = set()

    for i in duals:
        s = slot[i]
        for j0 in range(0, ny + 1, chunk):
            j1 = min(j0 + chunk, ny + 1)
            back = jnp.dot(w[:, half:], corners(rolled, i, j0, j1), preferred_element_type=F32)
            here = jnp.dot(w[:, :half], corners(block, i, j0, j1), preferred_element_type=F32)
            for j in range(j0, j1):
                cols = slice((j - j0) * nz, (j - j0 + 1) * nz)
                wide = slice(j * nz, (j + 1) * nz)
                for tx in range(2):
                    for ty in range(2):
                        sx, sy = 1 - tx, 1 - ty
                        m, n = i - sx, j - sy
                        base = (2 * tx + ty) * 2 * co
                        if not (0 <= m < nx and 0 <= n < ny):
                            ga[s, base : base + 2 * co, wide] = zeros
                            gb[s, base : base + 2 * co, wide] = zeros
                            continue
                        out = slice(n * nz, (n + 1) * nz)
                        for tz in range(2):
                            sz = 1 - tz
                            r = slice(base + tz * co, base + (tz + 1) * co)
                            low, high = back[r, cols], here[r, cols]
                            if sz == 1:
                                before = low + jnp.where(first, 0.0, high)
                                before = pltpu.roll(before, nz - 1, 1)
                            else:
                                before = jnp.where(first, 0.0, low) + high
                            q = ((2 * sx + sy) * 2 + sz) * co
                            sig = 0.5 * jnp.tanh(0.5 * before) + 0.5
                            value = before * sig
                            vals[s, q : q + co, out] = value.astype(BF16)
                            slope = sig + value * (1.0 - sig)
                            grad = cots[s, q : q + co, out].astype(F32) * slope
                            if sz == 1:
                                grad = pltpu.roll(grad, 1, 1)
                            whole = grad.astype(BF16)
                            cut = jnp.where(first, 0.0, grad).astype(BF16)
                            ga[s, r, wide] = cut if sz == 0 else whole
                            gb[s, r, wide] = cut if sz == 1 else whole

    to_c = swap_matrix(ny, GROUP)
    copies = []
    for count, (i, sx, m, sy, sz) in enumerate(pairs):
        q = (2 * sx + sy) * 2 + sz
        mixed = jnp.concatenate(
            [
                jnp.concatenate(
                    [
                        vals[
                            slot[i],
                            q * co + k * GROUP : q * co + (k + 1) * GROUP,
                            y * nz : (y + 1) * nz,
                        ]
                        for y in range(ny)
                    ],
                    axis=0,
                )
                for k in range(split)
            ],
            axis=1,
        )
        moved = jnp.dot(to_c, mixed, preferred_element_type=F32).astype(BF16)
        for k in range(split):
            staged[count, k * GROUP : (k + 1) * GROUP] = moved[
                :, k * nz : (k + 1) * nz
            ].reshape(GROUP, ny, nz)
        copy = pltpu.make_async_copy(staged.at[count], act_out.at[q, :, m], sems.at[count])
        copy.start()
        copies.append(copy)

    nt = (((1,), (1,)), ((), ()))
    for part, (grads, get) in enumerate(((gb, block), (ga, rolled))):
        total = None
        for i in duals:
            term = lax.dot_general(
                grads[slot[i]], corners(get, i, 0, ny + 1), nt, preferred_element_type=F32
            )
            total = term if total is None else total + term
        wg_add(part, total)

    for i in duals:
        s = slot[i]
        for j0 in range(0, ny + 1, chunk):
            j1 = min(j0 + chunk, ny + 1)
            wide = slice(j0 * nz, j1 * nz)
            back = jnp.dot(wt[half:], ga[s, :, wide], preferred_element_type=F32)
            here = jnp.dot(wt[:half], gb[s, :, wide], preferred_element_type=F32)
            for j in range(j0, j1):
                cols = slice((j - j0) * nz, (j - j0 + 1) * nz)
                both = here[:, cols] + pltpu.roll(back[:, cols], nz - 1, 1)
                for ex in range(2):
                    for ey in range(2):
                        r = (2 * ex + ey) * ci
                        cell = (i - ex, j - ey)
                        ig_add(cell[0], cell[1], both[r : r + ci], cell not in started)
                        started.add(cell)

    for copy in copies:
        copy.wait()


def inner_kernel(dims, chunk, flat, ylo, yhi, w, wt, cot, act_out, wg, ig, *scratch):
    nx, ny, nz, ci, co = dims
    half = 4 * ci

    def block(x, y):
        if y == 0:
            return ylo[x - 1]
        if y == ny + 1:
            return yhi[x - 1]
        return flat[x - 1, :, (y - 1) * nz : y * nz]

    def wg_add(part, total):
        wg[:, part * half : (part + 1) * half] = total

    def ig_add(m, y, value, fresh):
        lanes = slice((y + 1) * nz, (y + 2) * nz)
        ig[m, :, lanes] = value if fresh else ig[m, :, lanes] + value

    brick_pass(
        dims, chunk, range(1, nx), block, cot, w, wt, act_out, wg_add, ig_add, scratch
    )


def outer_kernel(
    dims,
    chunk,
    core,
    flat,
    ylo,
    yhi,
    xlo,
    xhi,
    w,
    wt,
    cot,
    wg_in,
    ig_in,
    act_in,
    act_out,
    keep,
    send,
    own,
    yface,
    up,
    down,
    full,
    faces,
    *scratch,
):
    del act_in
    nx, ny, nz, ci, co = dims
    half = 4 * ci

    def block(x, y):
        lanes = slice(y * nz, (y + 1) * nz)
        if x == 0:
            return xlo[0, :, lanes]
        if x == nx + 1:
            return xhi[0, :, lanes]
        if y == 0:
            return ylo[x - 1]
        if y == ny + 1:
            return yhi[x - 1]
        return flat[x - 1, :, (y - 1) * nz : y * nz]

    def wg_add(part, total):
        total = total + wg_in[:, part * half : (part + 1) * half]
        for ex in range(2):
            for row in range(8):
                tx, ty, tz = row // 4, row // 2 % 2, row % 2
                index = ((tx * 2 + ty) * 2 + part) * 2 + tz
                full[ex, index] = total[
                    row * co : (row + 1) * co, ex * 2 * ci : (ex + 1) * 2 * ci
                ]

    def ig_add(m, y, value, fresh):
        lanes = slice((y + 1) * nz, (y + 2) * nz)
        if m < 0 or m >= nx:
            side = 0 if m < 0 else 1
            faces[side, :, lanes] = value if fresh else faces[side, :, lanes] + value
            return
        if y < 0 or y >= ny:
            side = 0 if y < 0 else 1
            base = ig_in[m, :, lanes] if fresh else yface[side, m]
            yface[side, m] = base + value
            return
        inner = slice(y * nz, (y + 1) * nz)
        base = ig_in[m, :, lanes] if fresh else own[m, :, inner]
        own[m, :, inner] = base + value

    for m in range(1, nx - 1):
        own[m] = ig_in[m, :, nz : (ny + 1) * nz]
        yface[0, m] = ig_in[m, :, :nz]
        yface[1, m] = ig_in[m, :, (ny + 1) * nz :]
    brick_pass(dims, chunk, (0, nx), block, cot, w, wt, act_out, wg_add, ig_add, scratch)
    c = core[0]
    keep[...] = full[c]
    send[...] = full[1 - c].astype(BF16)
    down[0] = faces[0].astype(BF16)
    up[0] = faces[1].astype(BF16)


def unpack_kernel(co, ci, core, mine, other, out, full):
    c = core[0]
    full[c] = mine[...].astype(F32)
    full[1 - c] = other[...].astype(F32)
    for ex in range(2):
        for tx in range(2):
            for ty in range(2):
                for ez in range(2):
                    for tz in range(2):
                        index = ((tx * 2 + ty) * 2 + ez) * 2 + tz
                        pair = full[ex, index]
                        for ey in range(2):
                            out[2 * ex + tx, 2 * ey + ty, 2 * ez + tz] = pair[
                                :, ey * ci : (ey + 1) * ci
                            ]


def neighbours(axis):
    count = lax.axis_size(axis)
    up = [(i, i + 1) for i in range(count - 1)]
    return up, [(b, a) for a, b in up]


def on_device(volume, kernel, cotangent):
    ci, nx, ny, nz = volume.shape
    co = kernel.shape[3]
    gx, gy = lax.axis_size("gx"), lax.axis_size("gy")
    gx_up, gx_down = neighbours("gx")
    gy_up, gy_down = neighbours("gy")
    cells = nx * gx * ny * gy * nz
    dims = (nx, ny, nz, ci, co)
    core = (lax.axis_index("gx") % 2).astype(jnp.int32).reshape(1)

    flat = volume.transpose(1, 0, 2, 3).reshape(nx, ci, ny * nz)
    ylo = lax.ppermute(flat[:, :, (ny - 1) * nz :], "gy", gy_up)
    yhi = lax.ppermute(flat[:, :, :nz], "gy", gy_down)
    top = jnp.concatenate([ylo[nx - 1 :], flat[nx - 1 :], yhi[nx - 1 :]], axis=2)
    low = jnp.concatenate([ylo[:1], flat[:1], yhi[:1]], axis=2)
    xlo = lax.ppermute(top, "gx", gx_up)
    xhi = lax.ppermute(low, "gx", gx_down)

    taps = kernel.reshape(2, 2, 2, 2, 2, 2, co, ci)
    w = taps.transpose(1, 3, 5, 6, 4, 0, 2, 7).reshape(8 * co, 8 * ci)
    wt = w.T
    cot = cotangent.reshape(8, co, nx, ny, nz)

    vmem = pl.BlockSpec(memory_space=pltpu.VMEM)
    smem = pl.BlockSpec(memory_space=pltpu.SMEM)
    anywhere = pl.BlockSpec(memory_space=pl.ANY)
    chunk = 4

    def scratch(duals, planes, pairs):
        return [
            pltpu.VMEM((planes, ci, (ny + 2) * nz), BF16),
            pltpu.VMEM((duals, 8 * co, (ny + 1) * nz), BF16),
            pltpu.VMEM((duals, 8 * co, (ny + 1) * nz), BF16),
            pltpu.VMEM((duals, 8 * co, ny * nz), BF16),
            pltpu.VMEM((duals, 8 * co, ny * nz), BF16),
            pltpu.VMEM((pairs, co, ny, nz), BF16),
            pltpu.SemaphoreType.DMA((pairs,)),
        ]

    params = pltpu.CompilerParams(vmem_limit_bytes=40 * 1024 * 1024)
    act, wg_part, ig_part = pl.pallas_call(
        functools.partial(inner_kernel, dims, chunk),
        out_shape=(
            jax.ShapeDtypeStruct(cot.shape, BF16),
            jax.ShapeDtypeStruct((8 * co, 8 * ci), F32),
            jax.ShapeDtypeStruct((nx, ci, (ny + 2) * nz), F32),
        ),
        in_specs=[vmem] * 6,
        out_specs=(anywhere, vmem, vmem),
        scratch_shapes=scratch(nx - 1, nx, 8 * (nx - 1)),
        compiler_params=params,
    )(flat, ylo, yhi, w, wt, cot)
    act, keep, send, own, yface, up, down = pl.pallas_call(
        functools.partial(outer_kernel, dims, chunk),
        out_shape=(
            jax.ShapeDtypeStruct(cot.shape, BF16),
            jax.ShapeDtypeStruct((16, co, 2 * ci), F32),
            jax.ShapeDtypeStruct((16, co, 2 * ci), BF16),
            jax.ShapeDtypeStruct((nx, ci, ny * nz), F32),
            jax.ShapeDtypeStruct((2, nx, ci, nz), F32),
            jax.ShapeDtypeStruct((1, ci, (ny + 2) * nz), BF16),
            jax.ShapeDtypeStruct((1, ci, (ny + 2) * nz), BF16),
        ),
        in_specs=[smem] + [vmem] * 10 + [anywhere],
        out_specs=(anywhere,) + (vmem,) * 6,
        input_output_aliases={11: 0},
        scratch_shapes=[
            pltpu.VMEM((2, 16, co, 2 * ci), F32),
            pltpu.VMEM((2, ci, (ny + 2) * nz), F32),
        ]
        + scratch(2, min(nx + 2, 4), 8),
        compiler_params=params,
    )(core, flat, ylo, yhi, xlo, xhi, w, wt, cot, wg_part, ig_part, act)

    scale = 1.0 / math.sqrt(cells)
    swap = [(i, i ^ 1) for i in range(gx)]
    pairs = gx // 2
    groups = [[2 * i + b for i in range(pairs)] for b in range(2)]
    piece = 16 * co // pairs
    half = keep + lax.ppermute(send, "gx", swap).astype(F32)
    shares = half.astype(BF16).reshape(pairs, piece, 2 * ci)
    shares = lax.all_to_all(shares, "gx", 0, 0, axis_index_groups=groups, tiled=True)
    part = jnp.sum(shares.astype(F32), axis=0).astype(BF16)
    rows = lax.all_to_all(
        jnp.broadcast_to(part[None], (gy,) + part.shape), "gy", 0, 0, tiled=True
    )
    total = (jnp.sum(rows.astype(F32), axis=0) * scale).astype(BF16)
    mine = lax.all_to_all(
        jnp.broadcast_to(total[None], (pairs,) + total.shape),
        "gx",
        0,
        0,
        axis_index_groups=groups,
        tiled=True,
    ).reshape(16, co, 2 * ci)
    other = lax.ppermute(mine, "gx", swap)
    weight_grad = pl.pallas_call(
        functools.partial(unpack_kernel, co, ci),
        out_shape=jax.ShapeDtypeStruct((4, 4, 4, co, ci), F32),
        in_specs=[smem, vmem, vmem],
        out_specs=vmem,
        scratch_shapes=[pltpu.VMEM((2, 16, co, 2 * ci), F32)],
    )(core, mine, other)

    from_low = lax.ppermute(up, "gx", gx_up).astype(F32)
    from_high = lax.ppermute(down, "gx", gx_down).astype(F32)

    def add_x(array, lanes):
        lead = (nx - 1,) + from_low[:, :, lanes].shape[1:]
        zero = jnp.zeros(lead, F32)
        return (
            array
            + jnp.concatenate([from_low[:, :, lanes], zero], axis=0)
            + jnp.concatenate([zero, from_high[:, :, lanes]], axis=0)
        )

    send_low = add_x(yface[0], slice(0, nz)).astype(BF16)
    send_high = add_x(yface[1], slice((ny + 1) * nz, None)).astype(BF16)
    y_low = lax.ppermute(send_high, "gy", gy_up).astype(F32)
    y_high = lax.ppermute(send_low, "gy", gy_down).astype(F32)
    gap = jnp.zeros((nx, ci, (ny - 1) * nz), F32)
    total_ig = (
        add_x(own, slice(nz, (ny + 1) * nz))
        + jnp.concatenate([y_low, gap], axis=2)
        + jnp.concatenate([gap, y_high], axis=2)
    )
    input_grad = total_ig.astype(BF16).reshape(nx, ci, ny, nz).transpose(1, 0, 2, 3)
    return act.reshape(cotangent.shape), input_grad, weight_grad


def solution(mesh):
    placed = (P(None, "gx", "gy", None), P(), P(None, None, None, None, "gx", "gy", None))
    return jax.shard_map(
        on_device,
        mesh=mesh,
        in_specs=placed,
        out_specs=(placed[2], placed[0], P()),
        check_vma=False,
    )
```

```python
import functools
import math

import jax
import jax.numpy as jnp
from jax import lax
from jax.experimental import pallas as pl
from jax.experimental.pallas import tpu as pltpu
from jax.sharding import PartitionSpec as P

F32 = jnp.float32
BF16 = jnp.bfloat16
GROUP = 16


def swap_matrix(outer, inner):
    size = outer * inner
    row = lax.broadcasted_iota(jnp.int32, (size, size), 0)
    col = lax.broadcasted_iota(jnp.int32, (size, size), 1)
    return jnp.where(col == (row % outer) * inner + row // outer, 1.0, 0.0).astype(BF16)


def turn(matrix, pieces, nz):
    flat = [p.reshape(p.shape[0] * p.shape[1], nz) for p in pieces]
    moved = jnp.dot(matrix, jnp.concatenate(flat, axis=1), preferred_element_type=F32)
    return moved.astype(BF16)


def bring_plane(to_y, raw, ny, nz, put):
    for k in range(0, raw.count, 2):
        moved = turn(to_y, [raw(k), raw(k + 1)], nz)
        for y in range(ny):
            rows = slice(y * GROUP, (y + 1) * GROUP)
            put(k, y, moved[rows, :nz])
            put(k + 1, y, moved[rows, nz:])


class Tiles:
    def __init__(self, count, get):
        self.count, self.get = count, get

    def __call__(self, k):
        return self.get(k)


def columns_pass(dims, chunk, columns, block, rolled, w, wt, cot_at, put_value, wg_add, ig_add, ga, gb):
    nx, ny, nz, ci, co = dims
    half = 4 * ci
    first = lax.broadcasted_iota(jnp.int32, (co, nz), 1) == 0
    zeros = jnp.zeros((2 * co, nz), BF16)

    def corners(get, some):
        return jnp.concatenate(
            [
                jnp.concatenate([get(i + 1 - ex, j + 1 - ey) for i, j in some], axis=1)
                for ex in range(2)
                for ey in range(2)
            ],
            axis=0,
        )

    starts = range(0, len(columns), chunk)
    for c0 in starts:
        some = columns[c0 : c0 + chunk]
        back = jnp.dot(w[:, half:], corners(rolled, some), preferred_element_type=F32)
        here = jnp.dot(w[:, :half], corners(block, some), preferred_element_type=F32)
        for k, (i, j) in enumerate(some):
            cols = slice(k * nz, (k + 1) * nz)
            wide = slice((c0 + k) * nz, (c0 + k + 1) * nz)
            for tx in range(2):
                for ty in range(2):
                    sx, sy = 1 - tx, 1 - ty
                    m, n = i - sx, j - sy
                    base = (2 * tx + ty) * 2 * co
                    if not (0 <= m < nx and 0 <= n < ny):
                        ga[base : base + 2 * co, wide] = zeros
                        gb[base : base + 2 * co, wide] = zeros
                        continue
                    for tz in range(2):
                        sz = 1 - tz
                        r = slice(base + tz * co, base + (tz + 1) * co)
                        low, high = back[r, cols], here[r, cols]
                        if sz == 1:
                            before = low + jnp.where(first, 0.0, high)
                            before = pltpu.roll(before, nz - 1, 1)
                        else:
                            before = jnp.where(first, 0.0, low) + high
                        q = (2 * sx + sy) * 2 + sz
                        sig = 0.5 * jnp.tanh(0.5 * before) + 0.5
                        value = before * sig
                        put_value(q, m, n, value.astype(BF16))
                        slope = sig + value * (1.0 - sig)
                        grad = cot_at(q, m, n).astype(F32) * slope
                        if sz == 1:
                            grad = pltpu.roll(grad, 1, 1)
                        whole = grad.astype(BF16)
                        cut = jnp.where(first, 0.0, grad).astype(BF16)
                        ga[r, wide] = cut if sz == 0 else whole
                        gb[r, wide] = cut if sz == 1 else whole

    started = set()
    for c0 in starts:
        some = columns[c0 : c0 + chunk]
        wide = slice(c0 * nz, (c0 + len(some)) * nz)
        back = jnp.dot(wt[half:], ga[:, wide], preferred_element_type=F32)
        here = jnp.dot(wt[:half], gb[:, wide], preferred_element_type=F32)
        for k, (i, j) in enumerate(some):
            cols = slice(k * nz, (k + 1) * nz)
            both = here[:, cols] + pltpu.roll(back[:, cols], nz - 1, 1)
            for ex in range(2):
                for ey in range(2):
                    r = (2 * ex + ey) * ci
                    cell = (i - ex, j - ey)
                    ig_add(cell[0], cell[1], both[r : r + ci], cell not in started)
                    started.add(cell)

    nt = (((1,), (1,)), ((), ()))
    for part, (grads, get) in enumerate(((gb, block), (ga, rolled))):
        wg_add(
            part,
            lax.dot_general(grads[...], corners(get, columns), nt, preferred_element_type=F32),
        )
    return started


def edge_row(q, ny):
    return (ny - 1) if q // 2 % 2 else 0


def inner_kernel(
    dims, chunk, vol, taps, cot, flat, w, wt, vals, cot_edge, wg, ig, vm, ga, gb, cots
):
    nx, ny, nz, ci, co = dims
    half = 4 * ci
    to_y = swap_matrix(GROUP, ny)

    for tx in range(2):
        for ty in range(2):
            for tz in range(2):
                r = ((2 * tx + ty) * 2 + tz) * co
                for ez in range(2):
                    for ex in range(2):
                        pair = [taps[2 * ex + tx, 2 * ey + ty, 2 * ez + tz] for ey in range(2)]
                        c = (2 * ez + ex) * 2 * ci
                        w[r : r + co, c : c + 2 * ci] = jnp.concatenate(pair, axis=1)
    wt[...] = w[...].T

    for x in range(nx):

        def put(k, y, rows, x=x):
            r = slice(k * GROUP, (k + 1) * GROUP)
            lanes = slice(y * nz, (y + 1) * nz)
            flat[x, r, lanes] = rows
            vm[x, r, lanes] = pltpu.roll(rows.astype(F32), 1, 1).astype(BF16)

        tiles = Tiles(
            ci // GROUP, lambda k, x=x: vol[k * GROUP : (k + 1) * GROUP, x]
        )
        bring_plane(to_y, tiles, ny, nz, put)

    for i in range(1, nx):
        for q in range(8):
            m = i - q // 4

            def put(k, y, rows, i=i, q=q):
                r = slice(q * co + k * GROUP, q * co + (k + 1) * GROUP)
                cots[i - 1, r, y * nz : (y + 1) * nz] = rows
                if y == edge_row(q, ny):
                    cot_edge[i - 1, r] = rows

            tiles = Tiles(
                co // GROUP, lambda k, q=q, m=m: cot[q, k * GROUP : (k + 1) * GROUP, m]
            )
            bring_plane(to_y, tiles, ny, nz, put)

    def block(x, y):
        return flat[x - 1, :, (y - 1) * nz : y * nz]

    def rolled(x, y):
        return vm[x - 1, :, (y - 1) * nz : y * nz]

    def cot_at(q, m, n):
        return cots[m + q // 4 - 1, q * co : (q + 1) * co, n * nz : (n + 1) * nz]

    def put_value(q, m, n, value):
        vals[m + q // 4 - 1, q * co : (q + 1) * co, n * nz : (n + 1) * nz] = value

    def wg_add(part, total):
        wg[:, part * half : (part + 1) * half] = total

    def ig_add(m, y, value, fresh):
        lanes = slice(y * nz, (y + 1) * nz)
        ig[m, :, lanes] = value if fresh else ig[m, :, lanes] + value

    columns = [(i, j) for i in range(1, nx) for j in range(1, ny)]
    columns_pass(
        dims, chunk, columns, block, rolled, w, wt, cot_at, put_value, wg_add, ig_add, ga, gb
    )


def outer_kernel(
    dims,
    chunk,
    core,
    flat,
    xlo,
    xhi,
    ylo,
    yhi,
    w,
    wt,
    cot,
    vals_in,
    cot_edge,
    wg_in,
    ig_in,
    act_out,
    own_out,
    keep,
    send,
    yface,
    up,
    down,
    full,
    faces,
    own,
    xs,
    vm,
    ga,
    gb,
    cots,
    vals,
    val_edge,
    staged,
    sems,
):
    nx, ny, nz, ci, co = dims
    half = 4 * ci
    to_y = swap_matrix(GROUP, ny)
    to_c = swap_matrix(ny, GROUP)

    for side, plane in enumerate((xlo, xhi)):

        def put(k, y, rows, side=side):
            xs[side, k * GROUP : (k + 1) * GROUP, y * nz : (y + 1) * nz] = rows

        tiles = Tiles(
            ci // GROUP, lambda k, plane=plane: plane[k * GROUP : (k + 1) * GROUP, 0]
        )
        bring_plane(to_y, tiles, ny, nz, put)

    for side in range(2):
        for q in range(4 * side, 4 * side + 4):

            def put(k, y, rows, q=q):
                r = slice(q * co + k * GROUP, q * co + (k + 1) * GROUP)
                cots[r, y * nz : (y + 1) * nz] = rows

            tiles = Tiles(
                co // GROUP,
                lambda k, q=q, side=side: cot[
                    q, k * GROUP : (k + 1) * GROUP, side * (nx - 1)
                ],
            )
            bring_plane(to_y, tiles, ny, nz, put)

    def block(x, y):
        if y == 0:
            return ylo[x]
        if y == ny + 1:
            return yhi[x]
        lanes = slice((y - 1) * nz, y * nz)
        if x == 0:
            return xs[0, :, lanes]
        if x == nx + 1:
            return xs[1, :, lanes]
        return flat[x - 1, :, lanes]

    for x in range(nx + 2):
        for y in range(ny + 2):
            vm[x, :, y * nz : (y + 1) * nz] = pltpu.roll(block(x, y).astype(F32), 1, 1).astype(
                BF16
            )

    def rolled(x, y):
        return vm[x, :, y * nz : (y + 1) * nz]

    def inner(q, m):
        return 1 <= m + q // 4 < nx

    def cot_at(q, m, n):
        r = slice(q * co, (q + 1) * co)
        if inner(q, m):
            return cot_edge[m + q // 4 - 1, r]
        return cots[r, n * nz : (n + 1) * nz]

    def put_value(q, m, n, value):
        r = slice(q * co, (q + 1) * co)
        if inner(q, m):
            val_edge[m + q // 4 - 1, r] = value
        else:
            vals[r, n * nz : (n + 1) * nz] = value

    def wg_add(part, total):
        total = total + wg_in[:, part * half : (part + 1) * half]
        for ex in range(2):
            for row in range(8):
                tx, ty, tz = row // 4, row // 2 % 2, row % 2
                index = ((tx * 2 + ty) * 2 + part) * 2 + tz
                full[ex, index] = total[
                    row * co : (row + 1) * co, ex * 2 * ci : (ex + 1) * 2 * ci
                ]

    def ig_add(m, y, value, fresh):
        if m < 0 or m >= nx:
            side = 0 if m < 0 else 1
            lanes = slice((y + 1) * nz, (y + 2) * nz)
            faces[side, :, lanes] = value if fresh else faces[side, :, lanes] + value
        elif y < 0 or y >= ny:
            side = 0 if y < 0 else 1
            yface[side, m] = value if fresh else yface[side, m] + value
        else:
            lanes = slice(y * nz, (y + 1) * nz)
            own[m, :, lanes] = (ig_in if fresh else own)[m, :, lanes] + value

    columns = [(i, j) for i in (0, nx) for j in range(ny + 1)]
    columns += [(i, j) for i in range(1, nx) for j in (0, ny)]
    started = columns_pass(
        dims, chunk, columns, block, rolled, w, wt, cot_at, put_value, wg_add, ig_add, ga, gb
    )
    for m in range(nx):
        for y in range(ny):
            if (m, y) not in started:
                lanes = slice(y * nz, (y + 1) * nz)
                own[m, :, lanes] = ig_in[m, :, lanes]
    c = core[0]
    keep[...] = full[c]
    send[...] = full[1 - c].astype(BF16)
    down[0] = faces[0].astype(BF16)
    up[0] = faces[1].astype(BF16)
    copies = [pltpu.make_async_copy(own, own_out, sems.at[8 * nx])]
    copies[0].start()

    for m in range(nx):
        for q in range(8):
            tiles = []
            for k in range(co // GROUP):
                r = slice(q * co + k * GROUP, q * co + (k + 1) * GROUP)
                rows = []
                for y in range(ny):
                    lanes = slice(y * nz, (y + 1) * nz)
                    if not inner(q, m):
                        rows.append(vals[r, lanes])
                    elif y == edge_row(q, ny):
                        rows.append(val_edge[m + q // 4 - 1, r])
                    else:
                        rows.append(vals_in[m + q // 4 - 1, r, lanes])
                tiles.append(jnp.concatenate(rows, axis=0).reshape(ny, GROUP, nz))
            moved = turn(to_c, tiles, nz)
            spot = m * 8 + q
            for k in range(co // GROUP):
                staged[spot, k * GROUP : (k + 1) * GROUP] = moved[
                    :, k * nz : (k + 1) * nz
                ].reshape(GROUP, ny, nz)
            copy = pltpu.make_async_copy(staged.at[spot], act_out.at[q, :, m], sems.at[spot])
            copy.start()
            copies.append(copy)
    for copy in copies:
        copy.wait()


def unpack_kernel(co, ci, core, mine, other, out, full):
    c = core[0]
    full[c] = mine[...].astype(F32)
    full[1 - c] = other[...].astype(F32)
    for ex in range(2):
        for tx in range(2):
            for ty in range(2):
                for ez in range(2):
                    for tz in range(2):
                        index = ((tx * 2 + ty) * 2 + ez) * 2 + tz
                        pair = full[ex, index]
                        for ey in range(2):
                            out[2 * ex + tx, 2 * ey + ty, 2 * ez + tz] = pair[
                                :, ey * ci : (ey + 1) * ci
                            ]


def neighbours(axis):
    count = lax.axis_size(axis)
    up = [(i, i + 1) for i in range(count - 1)]
    return up, [(b, a) for a, b in up]


def on_device(volume, kernel, cotangent):
    ci, nx, ny, nz = volume.shape
    co = kernel.shape[3]
    gx, gy = lax.axis_size("gx"), lax.axis_size("gy")
    gx_up, gx_down = neighbours("gx")
    gy_up, gy_down = neighbours("gy")
    cells = nx * gx * ny * gy * nz
    dims = (nx, ny, nz, ci, co)
    core = (lax.axis_index("gx") % 2).astype(jnp.int32).reshape(1)

    xlo = lax.ppermute(volume[:, nx - 1 :], "gx", gx_up)
    xhi = lax.ppermute(volume[:, :1], "gx", gx_down)
    cot = cotangent.reshape(8, co, nx, ny, nz)

    vmem = pl.BlockSpec(memory_space=pltpu.VMEM)
    smem = pl.BlockSpec(memory_space=pltpu.SMEM)
    anywhere = pl.BlockSpec(memory_space=pl.ANY)
    params = pltpu.CompilerParams(vmem_limit_bytes=28 * 1024 * 1024)
    n_in = (nx - 1) * (ny - 1)
    n_out = 2 * (ny + 1) + 2 * (nx - 1)
    flat, w, wt, vals, cot_edge, wg_part, ig_part = pl.pallas_call(
        functools.partial(inner_kernel, dims, 5),
        out_shape=(
            jax.ShapeDtypeStruct((nx, ci, ny * nz), BF16),
            jax.ShapeDtypeStruct((8 * co, 8 * ci), BF16),
            jax.ShapeDtypeStruct((8 * ci, 8 * co), BF16),
            jax.ShapeDtypeStruct((nx - 1, 8 * co, ny * nz), BF16),
            jax.ShapeDtypeStruct((nx - 1, 8 * co, nz), BF16),
            jax.ShapeDtypeStruct((8 * co, 8 * ci), F32),
            jax.ShapeDtypeStruct((nx, ci, ny * nz), F32),
        ),
        in_specs=[vmem] * 3,
        out_specs=(vmem,) * 7,
        scratch_shapes=[
            pltpu.VMEM((nx, ci, ny * nz), BF16),
            pltpu.VMEM((8 * co, n_in * nz), BF16),
            pltpu.VMEM((8 * co, n_in * nz), BF16),
            pltpu.VMEM((nx - 1, 8 * co, ny * nz), BF16),
        ],
        compiler_params=params,
    )(volume, kernel, cot)

    def y_row(y):
        rows = jnp.concatenate([xlo[:, :, y], volume[:, :, y], xhi[:, :, y]], axis=1)
        return rows.transpose(1, 0, 2)

    ylo = lax.ppermute(y_row(ny - 1), "gy", gy_up)
    yhi = lax.ppermute(y_row(0), "gy", gy_down)
    act, own, keep, send, yface, up, down = pl.pallas_call(
        functools.partial(outer_kernel, dims, 4),
        out_shape=(
            jax.ShapeDtypeStruct(cot.shape, BF16),
            jax.ShapeDtypeStruct((nx, ci, ny * nz), F32),
            jax.ShapeDtypeStruct((16, co, 2 * ci), F32),
            jax.ShapeDtypeStruct((16, co, 2 * ci), BF16),
            jax.ShapeDtypeStruct((2, nx, ci, nz), F32),
            jax.ShapeDtypeStruct((1, ci, (ny + 2) * nz), BF16),
            jax.ShapeDtypeStruct((1, ci, (ny + 2) * nz), BF16),
        ),
        in_specs=[smem] + [vmem] * 12,
        out_specs=(anywhere, anywhere) + (vmem,) * 5,
        scratch_shapes=[
            pltpu.VMEM((2, 16, co, 2 * ci), F32),
            pltpu.VMEM((2, ci, (ny + 2) * nz), F32),
            pltpu.VMEM((nx, ci, ny * nz), F32),
            pltpu.VMEM((2, ci, ny * nz), BF16),
            pltpu.VMEM((nx + 2, ci, (ny + 2) * nz), BF16),
            pltpu.VMEM((8 * co, n_out * nz), BF16),
            pltpu.VMEM((8 * co, n_out * nz), BF16),
            pltpu.VMEM((8 * co, ny * nz), BF16),
            pltpu.VMEM((8 * co, ny * nz), BF16),
            pltpu.VMEM((nx - 1, 8 * co, nz), BF16),
            pltpu.VMEM((8 * nx, co, ny, nz), BF16),
            pltpu.SemaphoreType.DMA((8 * nx + 1,)),
        ],
        compiler_params=params,
    )(core, flat, xlo, xhi, ylo, yhi, w, wt, cot, vals, cot_edge, wg_part, ig_part)

    scale = 1.0 / math.sqrt(cells)
    place = lax.axis_index("gx")
    bits = [1 << b for b in range(1, gx.bit_length() - 1)]

    def trade(array, axis, count, distance):
        return lax.ppermute(array, axis, [(k, k ^ distance) for k in range(count)])

    part = (keep + trade(send, "gx", gx, 1).astype(F32)).reshape(16 * co, 2 * ci)
    for bit in bits:
        upper = (place & bit) != 0
        rows = part.shape[0] // 2
        kept = jnp.where(upper, part[rows:], part[:rows])
        sent = jnp.where(upper, part[:rows], part[rows:]).astype(BF16)
        part = kept + trade(sent, "gx", gx, bit).astype(F32)
    distance = 1
    while distance < gy:
        part = part + trade(part, "gy", gy, distance)
        distance *= 2
    total = (part * scale).astype(BF16)
    for bit in reversed(bits):
        upper = (place & bit) != 0
        others = trade(total, "gx", gx, bit)
        total = jnp.where(
            upper,
            jnp.concatenate([others, total], axis=0),
            jnp.concatenate([total, others], axis=0),
        )
    mine = total.reshape(16, co, 2 * ci)
    other = trade(mine, "gx", gx, 1)
    weight_grad = pl.pallas_call(
        functools.partial(unpack_kernel, co, ci),
        out_shape=jax.ShapeDtypeStruct((4, 4, 4, co, ci), F32),
        in_specs=[smem, vmem, vmem],
        out_specs=vmem,
        scratch_shapes=[pltpu.VMEM((2, 16, co, 2 * ci), F32)],
        compiler_params=pltpu.CompilerParams(vmem_limit_bytes=8 * 1024 * 1024),
    )(core, mine, other)

    from_low = lax.ppermute(up, "gx", gx_up).astype(F32)
    from_high = lax.ppermute(down, "gx", gx_down).astype(F32)

    def add_x(array, lanes):
        lead = (nx - 1,) + from_low[:, :, lanes].shape[1:]
        zero = jnp.zeros(lead, F32)
        return (
            array
            + jnp.concatenate([from_low[:, :, lanes], zero], axis=0)
            + jnp.concatenate([zero, from_high[:, :, lanes]], axis=0)
        )

    send_low = add_x(yface[0], slice(0, nz)).astype(BF16)
    send_high = add_x(yface[1], slice((ny + 1) * nz, None)).astype(BF16)
    y_low = lax.ppermute(send_high, "gy", gy_up).astype(F32)
    y_high = lax.ppermute(send_low, "gy", gy_down).astype(F32)
    gap = jnp.zeros((nx, ci, (ny - 1) * nz), F32)
    total_ig = (
        add_x(own, slice(nz, (ny + 1) * nz))
        + jnp.concatenate([y_low, gap], axis=2)
        + jnp.concatenate([gap, y_high], axis=2)
    )
    input_grad = total_ig.astype(BF16).reshape(nx, ci, ny, nz).transpose(1, 0, 2, 3)
    return act.reshape(cotangent.shape), input_grad, weight_grad


def solution(mesh):
    placed = (P(None, "gx", "gy", None), P(), P(None, None, None, None, "gx", "gy", None))
    return jax.shard_map(
        on_device,
        mesh=mesh,
        in_specs=placed,
        out_specs=(placed[2], placed[0], P()),
        check_vma=False,
    )
```

```python
import functools
import math

import jax
import jax.numpy as jnp
from jax import lax
from jax.experimental import pallas as pl
from jax.experimental.pallas import tpu as pltpu
from jax.sharding import PartitionSpec as P

F32 = jnp.float32
BF16 = jnp.bfloat16
GROUP = 16


def swap_matrix(outer, inner):
    size = outer * inner
    row = lax.broadcasted_iota(jnp.int32, (size, size), 0)
    col = lax.broadcasted_iota(jnp.int32, (size, size), 1)
    return jnp.where(col == (row % outer) * inner + row // outer, 1.0, 0.0).astype(BF16)


def turn(matrix, pieces, nz):
    flat = [p.reshape(p.shape[0] * p.shape[1], nz) for p in pieces]
    moved = jnp.dot(matrix, jnp.concatenate(flat, axis=1), preferred_element_type=F32)
    return moved.astype(BF16)


def bring_plane(to_y, raw, ny, nz, put):
    for k in range(0, raw.count, 2):
        moved = turn(to_y, [raw(k), raw(k + 1)], nz)
        for y in range(ny):
            rows = slice(y * GROUP, (y + 1) * GROUP)
            put(k, y, moved[rows, :nz])
            put(k + 1, y, moved[rows, nz:])


class Tiles:
    def __init__(self, count, get):
        self.count, self.get = count, get

    def __call__(self, k):
        return self.get(k)


def columns_pass(dims, chunk, columns, block, rolled, w, wt, cot_at, put_value, wg_add, ig_add, ga, gb):
    nx, ny, nz, ci, co = dims
    half = 4 * ci
    first = lax.broadcasted_iota(jnp.int32, (co, nz), 1) == 0
    zeros = jnp.zeros((2 * co, nz), BF16)

    def corners(get, some):
        return jnp.concatenate(
            [
                jnp.concatenate([get(i + 1 - ex, j + 1 - ey) for i, j in some], axis=1)
                for ex in range(2)
                for ey in range(2)
            ],
            axis=0,
        )

    starts = range(0, len(columns), chunk)
    for c0 in starts:
        some = columns[c0 : c0 + chunk]
        back = jnp.dot(w[:, half:], corners(rolled, some), preferred_element_type=F32)
        here = jnp.dot(w[:, :half], corners(block, some), preferred_element_type=F32)
        for k, (i, j) in enumerate(some):
            cols = slice(k * nz, (k + 1) * nz)
            wide = slice((c0 + k) * nz, (c0 + k + 1) * nz)
            for tx in range(2):
                for ty in range(2):
                    sx, sy = 1 - tx, 1 - ty
                    m, n = i - sx, j - sy
                    base = (2 * tx + ty) * 2 * co
                    if not (0 <= m < nx and 0 <= n < ny):
                        ga[base : base + 2 * co, wide] = zeros
                        gb[base : base + 2 * co, wide] = zeros
                        continue
                    for tz in range(2):
                        sz = 1 - tz
                        r = slice(base + tz * co, base + (tz + 1) * co)
                        low, high = back[r, cols], here[r, cols]
                        if sz == 1:
                            before = low + jnp.where(first, 0.0, high)
                            before = pltpu.roll(before, nz - 1, 1)
                        else:
                            before = jnp.where(first, 0.0, low) + high
                        q = (2 * sx + sy) * 2 + sz
                        sig = 0.5 * jnp.tanh(0.5 * before) + 0.5
                        value = before * sig
                        put_value(q, m, n, value.astype(BF16))
                        slope = sig + value * (1.0 - sig)
                        grad = cot_at(q, m, n).astype(F32) * slope
                        if sz == 1:
                            grad = pltpu.roll(grad, 1, 1)
                        whole = grad.astype(BF16)
                        cut = jnp.where(first, 0.0, grad).astype(BF16)
                        ga[r, wide] = cut if sz == 0 else whole
                        gb[r, wide] = cut if sz == 1 else whole

    started = set()
    for c0 in starts:
        some = columns[c0 : c0 + chunk]
        wide = slice(c0 * nz, (c0 + len(some)) * nz)
        back = jnp.dot(wt[half:], ga[:, wide], preferred_element_type=F32)
        here = jnp.dot(wt[:half], gb[:, wide], preferred_element_type=F32)
        for k, (i, j) in enumerate(some):
            cols = slice(k * nz, (k + 1) * nz)
            both = here[:, cols] + pltpu.roll(back[:, cols], nz - 1, 1)
            for ex in range(2):
                for ey in range(2):
                    r = (2 * ex + ey) * ci
                    cell = (i - ex, j - ey)
                    ig_add(cell[0], cell[1], both[r : r + ci], cell not in started)
                    started.add(cell)

    nt = (((1,), (1,)), ((), ()))
    for part, (grads, get) in enumerate(((gb, block), (ga, rolled))):
        wg_add(
            part,
            lax.dot_general(grads[...], corners(get, columns), nt, preferred_element_type=F32),
        )
    return started


def edge_row(q, ny):
    return (ny - 1) if q // 2 % 2 else 0


def inner_kernel(
    dims, chunk, vol, taps, cot, flat, w, wt, vals, cot_edge, wg, ig, vm, ga, gb, cots
):
    nx, ny, nz, ci, co = dims
    half = 4 * ci
    to_y = swap_matrix(GROUP, ny)

    for tx in range(2):
        for ty in range(2):
            for tz in range(2):
                r = ((2 * tx + ty) * 2 + tz) * co
                for ez in range(2):
                    for ex in range(2):
                        pair = [taps[2 * ex + tx, 2 * ey + ty, 2 * ez + tz] for ey in range(2)]
                        c = (2 * ez + ex) * 2 * ci
                        w[r : r + co, c : c + 2 * ci] = jnp.concatenate(pair, axis=1)
    wt[...] = w[...].T

    for x in range(nx):

        def put(k, y, rows, x=x):
            r = slice(k * GROUP, (k + 1) * GROUP)
            lanes = slice(y * nz, (y + 1) * nz)
            flat[x, r, lanes] = rows
            vm[x, r, lanes] = pltpu.roll(rows.astype(F32), 1, 1).astype(BF16)

        tiles = Tiles(
            ci // GROUP, lambda k, x=x: vol[k * GROUP : (k + 1) * GROUP, x]
        )
        bring_plane(to_y, tiles, ny, nz, put)

    for i in range(1, nx):
        for q in range(8):
            m = i - q // 4

            def put(k, y, rows, i=i, q=q):
                r = slice(q * co + k * GROUP, q * co + (k + 1) * GROUP)
                cots[i - 1, r, y * nz : (y + 1) * nz] = rows
                if y == edge_row(q, ny):
                    cot_edge[i - 1, r] = rows

            tiles = Tiles(
                co // GROUP, lambda k, q=q, m=m: cot[q, k * GROUP : (k + 1) * GROUP, m]
            )
            bring_plane(to_y, tiles, ny, nz, put)

    def block(x, y):
        return flat[x - 1, :, (y - 1) * nz : y * nz]

    def rolled(x, y):
        return vm[x - 1, :, (y - 1) * nz : y * nz]

    def cot_at(q, m, n):
        return cots[m + q // 4 - 1, q * co : (q + 1) * co, n * nz : (n + 1) * nz]

    def put_value(q, m, n, value):
        vals[m + q // 4 - 1, q * co : (q + 1) * co, n * nz : (n + 1) * nz] = value

    def wg_add(part, total):
        wg[:, part * half : (part + 1) * half] = total

    def ig_add(m, y, value, fresh):
        lanes = slice(y * nz, (y + 1) * nz)
        ig[m, :, lanes] = value if fresh else ig[m, :, lanes] + value

    columns = [(i, j) for i in range(1, nx) for j in range(1, ny)]
    columns_pass(
        dims, chunk, columns, block, rolled, w, wt, cot_at, put_value, wg_add, ig_add, ga, gb
    )


def outer_kernel(
    dims,
    chunk,
    flat,
    xlo_in,
    xhi_in,
    ylo_in,
    yhi_in,
    w,
    wt,
    cot,
    vals_in,
    cot_edge,
    wg_in,
    ig_in,
    act_out,
    own_out,
    up_out,
    down_out,
    wg,
    yface,
    sides,
    faces,
    own,
    xraw,
    yraw,
    xs,
    vm,
    ga,
    gb,
    cots,
    vals,
    val_edge,
    staged,
    sems,
):
    nx, ny, nz, ci, co = dims
    half = 4 * ci
    to_y = swap_matrix(GROUP, ny)
    to_c = swap_matrix(ny, GROUP)
    spots = 8 * nx
    arriving = [
        pltpu.make_async_copy(xlo_in, xraw.at[0], sems.at[spots]),
        pltpu.make_async_copy(xhi_in, xraw.at[1], sems.at[spots + 1]),
        pltpu.make_async_copy(ylo_in, yraw.at[0], sems.at[spots + 2]),
        pltpu.make_async_copy(yhi_in, yraw.at[1], sems.at[spots + 3]),
    ]
    for copy in arriving:
        copy.start()

    for side in range(2):
        for q in range(4 * side, 4 * side + 4):

            def put(k, y, rows, q=q):
                r = slice(q * co + k * GROUP, q * co + (k + 1) * GROUP)
                cots[r, y * nz : (y + 1) * nz] = rows

            tiles = Tiles(
                co // GROUP,
                lambda k, q=q, side=side: cot[
                    q, k * GROUP : (k + 1) * GROUP, side * (nx - 1)
                ],
            )
            bring_plane(to_y, tiles, ny, nz, put)

    for copy in arriving:
        copy.wait()
    for side in range(2):

        def put(k, y, rows, side=side):
            xs[side, k * GROUP : (k + 1) * GROUP, y * nz : (y + 1) * nz] = rows

        tiles = Tiles(
            ci // GROUP, lambda k, side=side: xraw[side, k * GROUP : (k + 1) * GROUP, 0]
        )
        bring_plane(to_y, tiles, ny, nz, put)

    def block(x, y):
        if y == 0:
            return yraw[0, x]
        if y == ny + 1:
            return yraw[1, x]
        lanes = slice((y - 1) * nz, y * nz)
        if x == 0:
            return xs[0, :, lanes]
        if x == nx + 1:
            return xs[1, :, lanes]
        return flat[x - 1, :, lanes]

    for x in range(nx + 2):
        for y in range(ny + 2):
            vm[x, :, y * nz : (y + 1) * nz] = pltpu.roll(block(x, y).astype(F32), 1, 1).astype(
                BF16
            )

    def rolled(x, y):
        return vm[x, :, y * nz : (y + 1) * nz]

    def inner(q, m):
        return 1 <= m + q // 4 < nx

    def cot_at(q, m, n):
        r = slice(q * co, (q + 1) * co)
        if inner(q, m):
            return cot_edge[m + q // 4 - 1, r]
        return cots[r, n * nz : (n + 1) * nz]

    def put_value(q, m, n, value):
        r = slice(q * co, (q + 1) * co)
        if inner(q, m):
            val_edge[m + q // 4 - 1, r] = value
        else:
            vals[r, n * nz : (n + 1) * nz] = value

    def wg_add(part, total):
        total = total + wg_in[:, part * half : (part + 1) * half]
        for ex in range(2):
            for row in range(8):
                tx, ty, tz = row // 4, row // 2 % 2, row % 2
                index = ((tx * 2 + ty) * 2 + part) * 2 + tz
                wg[ex * 16 + index] = total[
                    row * co : (row + 1) * co, ex * 2 * ci : (ex + 1) * 2 * ci
                ].astype(BF16)

    def ig_add(m, y, value, fresh):
        if m < 0 or m >= nx:
            side = 0 if m < 0 else 1
            lanes = slice((y + 1) * nz, (y + 2) * nz)
            faces[side, :, lanes] = value if fresh else faces[side, :, lanes] + value
        elif y < 0 or y >= ny:
            side = 0 if y < 0 else 1
            yface[side, m] = value if fresh else yface[side, m] + value
        else:
            lanes = slice(y * nz, (y + 1) * nz)
            own[m, :, lanes] = (ig_in if fresh else own)[m, :, lanes] + value

    columns = [(i, j) for i in (0, nx) for j in range(ny + 1)]
    columns += [(i, j) for i in range(1, nx) for j in (0, ny)]
    started = columns_pass(
        dims, chunk, columns, block, rolled, w, wt, cot_at, put_value, wg_add, ig_add, ga, gb
    )
    for m in range(nx):
        for y in range(ny):
            if (m, y) not in started:
                lanes = slice(y * nz, (y + 1) * nz)
                own[m, :, lanes] = ig_in[m, :, lanes]
    sides[...] = faces[...].astype(BF16)
    copies = [
        pltpu.make_async_copy(own, own_out, sems.at[spots]),
        pltpu.make_async_copy(sides.at[0], down_out, sems.at[spots + 1]),
        pltpu.make_async_copy(sides.at[1], up_out, sems.at[spots + 2]),
    ]
    for copy in copies:
        copy.start()

    for m in range(nx):
        for q in range(8):
            tiles = []
            for k in range(co // GROUP):
                r = slice(q * co + k * GROUP, q * co + (k + 1) * GROUP)
                rows = []
                for y in range(ny):
                    lanes = slice(y * nz, (y + 1) * nz)
                    if not inner(q, m):
                        rows.append(vals[r, lanes])
                    elif y == edge_row(q, ny):
                        rows.append(val_edge[m + q // 4 - 1, r])
                    else:
                        rows.append(vals_in[m + q // 4 - 1, r, lanes])
                tiles.append(jnp.concatenate(rows, axis=0).reshape(ny, GROUP, nz))
            moved = turn(to_c, tiles, nz)
            spot = m * 8 + q
            for k in range(co // GROUP):
                staged[spot, k * GROUP : (k + 1) * GROUP] = moved[
                    :, k * nz : (k + 1) * nz
                ].reshape(GROUP, ny, nz)
            copy = pltpu.make_async_copy(staged.at[spot], act_out.at[q, :, m], sems.at[spot])
            copy.start()
            copies.append(copy)
    for copy in copies:
        copy.wait()


def unpack_kernel(co, ci, packed, out):
    for ex in range(2):
        for tx in range(2):
            for ty in range(2):
                for ez in range(2):
                    for tz in range(2):
                        index = (((ex * 2 + tx) * 2 + ty) * 2 + ez) * 2 + tz
                        pair = packed[index].astype(F32)
                        for ey in range(2):
                            out[2 * ex + tx, 2 * ey + ty, 2 * ez + tz] = pair[
                                :, ey * ci : (ey + 1) * ci
                            ]


def neighbours(axis):
    count = lax.axis_size(axis)
    up = [(i, i + 1) for i in range(count - 1)]
    return up, [(b, a) for a, b in up]


def on_device(volume, kernel, cotangent):
    ci, nx, ny, nz = volume.shape
    co = kernel.shape[3]
    gx, gy = lax.axis_size("gx"), lax.axis_size("gy")
    gx_up, gx_down = neighbours("gx")
    gy_up, gy_down = neighbours("gy")
    cells = nx * gx * ny * gy * nz
    dims = (nx, ny, nz, ci, co)

    xlo = lax.ppermute(volume[:, nx - 1 :], "gx", gx_up)
    xhi = lax.ppermute(volume[:, :1], "gx", gx_down)
    cot = cotangent.reshape(8, co, nx, ny, nz)

    vmem = pl.BlockSpec(memory_space=pltpu.VMEM)
    smem = pl.BlockSpec(memory_space=pltpu.SMEM)
    anywhere = pl.BlockSpec(memory_space=pl.ANY)
    params = pltpu.CompilerParams(vmem_limit_bytes=28 * 1024 * 1024)
    n_in = (nx - 1) * (ny - 1)
    n_out = 2 * (ny + 1) + 2 * (nx - 1)
    flat, w, wt, vals, cot_edge, wg_part, ig_part = pl.pallas_call(
        functools.partial(inner_kernel, dims, 5),
        out_shape=(
            jax.ShapeDtypeStruct((nx, ci, ny * nz), BF16),
            jax.ShapeDtypeStruct((8 * co, 8 * ci), BF16),
            jax.ShapeDtypeStruct((8 * ci, 8 * co), BF16),
            jax.ShapeDtypeStruct((nx - 1, 8 * co, ny * nz), BF16),
            jax.ShapeDtypeStruct((nx - 1, 8 * co, nz), BF16),
            jax.ShapeDtypeStruct((8 * co, 8 * ci), F32),
            jax.ShapeDtypeStruct((nx, ci, ny * nz), F32),
        ),
        in_specs=[vmem] * 3,
        out_specs=(vmem,) * 7,
        scratch_shapes=[
            pltpu.VMEM((nx, ci, ny * nz), BF16),
            pltpu.VMEM((8 * co, n_in * nz), BF16),
            pltpu.VMEM((8 * co, n_in * nz), BF16),
            pltpu.VMEM((nx - 1, 8 * co, ny * nz), BF16),
        ],
        compiler_params=params,
    )(volume, kernel, cot)

    def y_row(y):
        return jnp.concatenate(
            [
                xlo[:, :, y].transpose(1, 0, 2),
                flat[:, :, y * nz : (y + 1) * nz],
                xhi[:, :, y].transpose(1, 0, 2),
            ],
            axis=0,
        )

    ylo = lax.ppermute(y_row(ny - 1), "gy", gy_up)
    yhi = lax.ppermute(y_row(0), "gy", gy_down)
    act, own, up, down, wg, yface = pl.pallas_call(
        functools.partial(outer_kernel, dims, 4),
        out_shape=(
            jax.ShapeDtypeStruct(cot.shape, BF16),
            jax.ShapeDtypeStruct((nx, ci, ny * nz), F32),
            jax.ShapeDtypeStruct((ci, (ny + 2) * nz), BF16),
            jax.ShapeDtypeStruct((ci, (ny + 2) * nz), BF16),
            jax.ShapeDtypeStruct((32, co, 2 * ci), BF16),
            jax.ShapeDtypeStruct((2, nx, ci, nz), F32),
        ),
        in_specs=[vmem] + [anywhere] * 4 + [vmem] * 7,
        out_specs=(anywhere,) * 4 + (vmem,) * 2,
        scratch_shapes=[
            pltpu.VMEM((2, ci, (ny + 2) * nz), BF16),
            pltpu.VMEM((2, ci, (ny + 2) * nz), F32),
            pltpu.VMEM((nx, ci, ny * nz), F32),
            pltpu.VMEM((2, ci, 1, ny, nz), BF16),
            pltpu.VMEM((2, nx + 2, ci, nz), BF16),
            pltpu.VMEM((2, ci, ny * nz), BF16),
            pltpu.VMEM((nx + 2, ci, (ny + 2) * nz), BF16),
            pltpu.VMEM((8 * co, n_out * nz), BF16),
            pltpu.VMEM((8 * co, n_out * nz), BF16),
            pltpu.VMEM((8 * co, ny * nz), BF16),
            pltpu.VMEM((8 * co, ny * nz), BF16),
            pltpu.VMEM((nx - 1, 8 * co, nz), BF16),
            pltpu.VMEM((8 * nx, co, ny, nz), BF16),
            pltpu.SemaphoreType.DMA((8 * nx + 4,)),
        ],
        compiler_params=params,
    )(flat, xlo, xhi, ylo, yhi, w, wt, cot, vals, cot_edge, wg_part, ig_part)

    scale = 1.0 / math.sqrt(cells)
    devices = gx * gy
    shares = wg.reshape(devices, 32 * co // devices, 2 * ci)
    shares = lax.all_to_all(shares, ("gx", "gy"), 0, 0, tiled=True)
    piece = (jnp.sum(shares.astype(F32), axis=0) * scale).astype(BF16)
    pieces = jnp.broadcast_to(piece[None], (devices,) + piece.shape)
    pieces = lax.all_to_all(pieces, ("gx", "gy"), 0, 0, tiled=True)
    weight_grad = pl.pallas_call(
        functools.partial(unpack_kernel, co, ci),
        out_shape=jax.ShapeDtypeStruct((4, 4, 4, co, ci), F32),
        in_specs=[vmem],
        out_specs=vmem,
        compiler_params=pltpu.CompilerParams(vmem_limit_bytes=8 * 1024 * 1024),
    )(pieces.reshape(32, co, 2 * ci))

    from_low = lax.ppermute(up, "gx", gx_up).astype(F32)[None]
    from_high = lax.ppermute(down, "gx", gx_down).astype(F32)[None]

    def add_x(array, lanes):
        lead = (nx - 1,) + from_low[:, :, lanes].shape[1:]
        zero = jnp.zeros(lead, F32)
        return (
            array
            + jnp.concatenate([from_low[:, :, lanes], zero], axis=0)
            + jnp.concatenate([zero, from_high[:, :, lanes]], axis=0)
        )

    send_low = add_x(yface[0], slice(0, nz)).astype(BF16)
    send_high = add_x(yface[1], slice((ny + 1) * nz, None)).astype(BF16)
    y_low = lax.ppermute(send_high, "gy", gy_up).astype(F32)
    y_high = lax.ppermute(send_low, "gy", gy_down).astype(F32)
    gap = jnp.zeros((nx, ci, (ny - 1) * nz), F32)
    total_ig = (
        add_x(own, slice(nz, (ny + 1) * nz))
        + jnp.concatenate([y_low, gap], axis=2)
        + jnp.concatenate([gap, y_high], axis=2)
    )
    input_grad = total_ig.astype(BF16).reshape(nx, ci, ny, nz).transpose(1, 0, 2, 3)
    return act.reshape(cotangent.shape), input_grad, weight_grad


def solution(mesh):
    placed = (P(None, "gx", "gy", None), P(), P(None, None, None, None, "gx", "gy", None))
    return jax.shard_map(
        on_device,
        mesh=mesh,
        in_specs=placed,
        out_specs=(placed[2], placed[0], P()),
        check_vma=False,
    )
```

```python
import functools
import math

import jax
import jax.numpy as jnp
from jax import lax
from jax.experimental import pallas as pl
from jax.experimental.pallas import tpu as pltpu
from jax.sharding import PartitionSpec as P

F32 = jnp.float32
BF16 = jnp.bfloat16
GROUP = 16


def swap_matrix(outer, inner):
    size = outer * inner
    row = lax.broadcasted_iota(jnp.int32, (size, size), 0)
    col = lax.broadcasted_iota(jnp.int32, (size, size), 1)
    return jnp.where(col == (row % outer) * inner + row // outer, 1.0, 0.0).astype(BF16)


def turn(matrix, pieces, nz):
    flat = [p.reshape(p.shape[0] * p.shape[1], nz) for p in pieces]
    moved = jnp.dot(matrix, jnp.concatenate(flat, axis=1), preferred_element_type=F32)
    return moved.astype(BF16)


def bring_plane(to_y, raw, ny, nz, put):
    for k in range(0, raw.count, 2):
        moved = turn(to_y, [raw(k), raw(k + 1)], nz)
        for y in range(ny):
            rows = slice(y * GROUP, (y + 1) * GROUP)
            put(k, y, moved[rows, :nz])
            put(k + 1, y, moved[rows, nz:])


class Tiles:
    def __init__(self, count, get):
        self.count, self.get = count, get

    def __call__(self, k):
        return self.get(k)


def columns_pass(dims, chunk, columns, block, rolled, w, wt, cot_at, put_value, wg_add, ig_add, ga, gb):
    nx, ny, nz, ci, co = dims
    half = 4 * ci
    first = lax.broadcasted_iota(jnp.int32, (co, nz), 1) == 0
    zeros = jnp.zeros((2 * co, nz), BF16)

    def corners(get, some):
        return jnp.concatenate(
            [
                jnp.concatenate([get(i + 1 - ex, j + 1 - ey) for i, j in some], axis=1)
                for ex in range(2)
                for ey in range(2)
            ],
            axis=0,
        )

    starts = range(0, len(columns), chunk)
    for c0 in starts:
        some = columns[c0 : c0 + chunk]
        back = jnp.dot(w[:, half:], corners(rolled, some), preferred_element_type=F32)
        here = jnp.dot(w[:, :half], corners(block, some), preferred_element_type=F32)
        for k, (i, j) in enumerate(some):
            cols = slice(k * nz, (k + 1) * nz)
            wide = slice((c0 + k) * nz, (c0 + k + 1) * nz)
            for tx in range(2):
                for ty in range(2):
                    sx, sy = 1 - tx, 1 - ty
                    m, n = i - sx, j - sy
                    base = (2 * tx + ty) * 2 * co
                    if not (0 <= m < nx and 0 <= n < ny):
                        ga[base : base + 2 * co, wide] = zeros
                        gb[base : base + 2 * co, wide] = zeros
                        continue
                    for tz in range(2):
                        sz = 1 - tz
                        r = slice(base + tz * co, base + (tz + 1) * co)
                        low, high = back[r, cols], here[r, cols]
                        if sz == 1:
                            before = low + jnp.where(first, 0.0, high)
                            before = pltpu.roll(before, nz - 1, 1)
                        else:
                            before = jnp.where(first, 0.0, low) + high
                        q = (2 * sx + sy) * 2 + sz
                        sig = 0.5 * jnp.tanh(0.5 * before) + 0.5
                        value = before * sig
                        put_value(q, m, n, value.astype(BF16))
                        slope = sig + value * (1.0 - sig)
                        grad = cot_at(q, m, n).astype(F32) * slope
                        if sz == 1:
                            grad = pltpu.roll(grad, 1, 1)
                        whole = grad.astype(BF16)
                        cut = jnp.where(first, 0.0, grad).astype(BF16)
                        ga[r, wide] = cut if sz == 0 else whole
                        gb[r, wide] = cut if sz == 1 else whole

    started = set()
    for c0 in starts:
        some = columns[c0 : c0 + chunk]
        wide = slice(c0 * nz, (c0 + len(some)) * nz)
        back = jnp.dot(wt[half:], ga[:, wide], preferred_element_type=F32)
        here = jnp.dot(wt[:half], gb[:, wide], preferred_element_type=F32)
        for k, (i, j) in enumerate(some):
            cols = slice(k * nz, (k + 1) * nz)
            both = here[:, cols] + pltpu.roll(back[:, cols], nz - 1, 1)
            for ex in range(2):
                for ey in range(2):
                    r = (2 * ex + ey) * ci
                    cell = (i - ex, j - ey)
                    ig_add(cell[0], cell[1], both[r : r + ci], cell not in started)
                    started.add(cell)

    nt = (((1,), (1,)), ((), ()))
    for part, (grads, get) in enumerate(((gb, block), (ga, rolled))):
        wg_add(
            part,
            lax.dot_general(grads[...], corners(get, columns), nt, preferred_element_type=F32),
        )
    return started


def edge_row(q, ny):
    return (ny - 1) if q // 2 % 2 else 0


def inner_kernel(
    dims,
    chunk,
    vol_in,
    taps_in,
    cot,
    flat,
    w,
    wt,
    vals,
    cot_edge,
    wg,
    ig,
    vol,
    taps,
    sems,
    vm,
    ga,
    gb,
    cots,
):
    nx, ny, nz, ci, co = dims
    half = 4 * ci
    to_y = swap_matrix(GROUP, ny)
    arriving = [
        pltpu.make_async_copy(vol_in, vol, sems.at[0]),
        pltpu.make_async_copy(taps_in, taps, sems.at[1]),
    ]
    for copy in arriving:
        copy.start()

    for i in range(1, nx):
        for q in range(8):
            m = i - q // 4

            def put(k, y, rows, i=i, q=q):
                r = slice(q * co + k * GROUP, q * co + (k + 1) * GROUP)
                cots[i - 1, r, y * nz : (y + 1) * nz] = rows
                if y == edge_row(q, ny):
                    cot_edge[i - 1, r] = rows

            tiles = Tiles(
                co // GROUP, lambda k, q=q, m=m: cot[q, k * GROUP : (k + 1) * GROUP, m]
            )
            bring_plane(to_y, tiles, ny, nz, put)

    for copy in arriving:
        copy.wait()
    for tx in range(2):
        for ty in range(2):
            for tz in range(2):
                r = ((2 * tx + ty) * 2 + tz) * co
                for ez in range(2):
                    for ex in range(2):
                        pair = [taps[2 * ex + tx, 2 * ey + ty, 2 * ez + tz] for ey in range(2)]
                        c = (2 * ez + ex) * 2 * ci
                        w[r : r + co, c : c + 2 * ci] = jnp.concatenate(pair, axis=1)
    wt[...] = w[...].T

    for x in range(nx):

        def put(k, y, rows, x=x):
            r = slice(k * GROUP, (k + 1) * GROUP)
            lanes = slice(y * nz, (y + 1) * nz)
            flat[x, r, lanes] = rows
            vm[x, r, lanes] = pltpu.roll(rows.astype(F32), 1, 1).astype(BF16)

        tiles = Tiles(
            ci // GROUP, lambda k, x=x: vol[k * GROUP : (k + 1) * GROUP, x]
        )
        bring_plane(to_y, tiles, ny, nz, put)

    def block(x, y):
        return flat[x - 1, :, (y - 1) * nz : y * nz]

    def rolled(x, y):
        return vm[x - 1, :, (y - 1) * nz : y * nz]

    def cot_at(q, m, n):
        return cots[m + q // 4 - 1, q * co : (q + 1) * co, n * nz : (n + 1) * nz]

    def put_value(q, m, n, value):
        vals[m + q // 4 - 1, q * co : (q + 1) * co, n * nz : (n + 1) * nz] = value

    def wg_add(part, total):
        wg[:, part * half : (part + 1) * half] = total

    def ig_add(m, y, value, fresh):
        lanes = slice(y * nz, (y + 1) * nz)
        ig[m, :, lanes] = value if fresh else ig[m, :, lanes] + value

    columns = [(i, j) for i in range(1, nx) for j in range(1, ny)]
    columns_pass(
        dims, chunk, columns, block, rolled, w, wt, cot_at, put_value, wg_add, ig_add, ga, gb
    )


def outer_kernel(
    dims,
    chunk,
    flat,
    xlo_in,
    xhi_in,
    ylo_in,
    yhi_in,
    w,
    wt,
    cot,
    vals_in,
    cot_edge,
    wg_in,
    ig_in,
    act_out,
    own_out,
    up_out,
    down_out,
    wg,
    yface,
    sides,
    faces,
    own,
    xraw,
    yraw,
    vm,
    ga,
    gb,
    cots,
    vals,
    val_edge,
    staged,
    sems,
):
    nx, ny, nz, ci, co = dims
    half = 4 * ci
    to_y = swap_matrix(GROUP, ny)
    to_c = swap_matrix(ny, GROUP)
    spots = 8 * nx
    arriving = [
        pltpu.make_async_copy(xlo_in, xraw.at[0], sems.at[spots]),
        pltpu.make_async_copy(xhi_in, xraw.at[1], sems.at[spots + 1]),
        pltpu.make_async_copy(ylo_in, yraw.at[0], sems.at[spots + 2]),
        pltpu.make_async_copy(yhi_in, yraw.at[1], sems.at[spots + 3]),
    ]
    for copy in arriving:
        copy.start()

    for side in range(2):
        for q in range(4 * side, 4 * side + 4):

            def put(k, y, rows, q=q):
                r = slice(q * co + k * GROUP, q * co + (k + 1) * GROUP)
                cots[r, y * nz : (y + 1) * nz] = rows

            tiles = Tiles(
                co // GROUP,
                lambda k, q=q, side=side: cot[
                    q, k * GROUP : (k + 1) * GROUP, side * (nx - 1)
                ],
            )
            bring_plane(to_y, tiles, ny, nz, put)

    for copy in arriving:
        copy.wait()
    def block(x, y):
        if y == 0:
            return yraw[0, x]
        if y == ny + 1:
            return yraw[1, x]
        if x == 0:
            return xraw[0, y - 1]
        if x == nx + 1:
            return xraw[1, y - 1]
        return flat[x - 1, :, (y - 1) * nz : y * nz]

    for x in range(nx + 2):
        for y in range(ny + 2):
            vm[x, :, y * nz : (y + 1) * nz] = pltpu.roll(block(x, y).astype(F32), 1, 1).astype(
                BF16
            )

    def rolled(x, y):
        return vm[x, :, y * nz : (y + 1) * nz]

    def inner(q, m):
        return 1 <= m + q // 4 < nx

    def cot_at(q, m, n):
        r = slice(q * co, (q + 1) * co)
        if inner(q, m):
            return cot_edge[m + q // 4 - 1, r]
        return cots[r, n * nz : (n + 1) * nz]

    def put_value(q, m, n, value):
        r = slice(q * co, (q + 1) * co)
        if inner(q, m):
            val_edge[m + q // 4 - 1, r] = value
        else:
            vals[r, n * nz : (n + 1) * nz] = value

    def wg_add(part, total):
        total = total + wg_in[:, part * half : (part + 1) * half]
        for ex in range(2):
            for row in range(8):
                tx, ty, tz = row // 4, row // 2 % 2, row % 2
                index = ((tx * 2 + ty) * 2 + part) * 2 + tz
                wg[ex * 16 + index] = total[
                    row * co : (row + 1) * co, ex * 2 * ci : (ex + 1) * 2 * ci
                ].astype(BF16)

    def ig_add(m, y, value, fresh):
        if m < 0 or m >= nx:
            side = 0 if m < 0 else 1
            lanes = slice((y + 1) * nz, (y + 2) * nz)
            faces[side, :, lanes] = value if fresh else faces[side, :, lanes] + value
        elif y < 0 or y >= ny:
            side = 0 if y < 0 else 1
            yface[side, m] = value if fresh else yface[side, m] + value
        else:
            lanes = slice(y * nz, (y + 1) * nz)
            own[m, :, lanes] = (ig_in if fresh else own)[m, :, lanes] + value

    columns = [(i, j) for i in (0, nx) for j in range(ny + 1)]
    columns += [(i, j) for i in range(1, nx) for j in (0, ny)]
    started = columns_pass(
        dims, chunk, columns, block, rolled, w, wt, cot_at, put_value, wg_add, ig_add, ga, gb
    )
    for m in range(nx):
        for y in range(ny):
            if (m, y) not in started:
                lanes = slice(y * nz, (y + 1) * nz)
                own[m, :, lanes] = ig_in[m, :, lanes]
    sides[...] = faces[...].astype(BF16)
    copies = [
        pltpu.make_async_copy(own, own_out, sems.at[spots]),
        pltpu.make_async_copy(sides.at[0], down_out, sems.at[spots + 1]),
        pltpu.make_async_copy(sides.at[1], up_out, sems.at[spots + 2]),
    ]
    for copy in copies:
        copy.start()

    for m in range(nx):
        for q in range(8):
            tiles = []
            for k in range(co // GROUP):
                r = slice(q * co + k * GROUP, q * co + (k + 1) * GROUP)
                rows = []
                for y in range(ny):
                    lanes = slice(y * nz, (y + 1) * nz)
                    if not inner(q, m):
                        rows.append(vals[r, lanes])
                    elif y == edge_row(q, ny):
                        rows.append(val_edge[m + q // 4 - 1, r])
                    else:
                        rows.append(vals_in[m + q // 4 - 1, r, lanes])
                tiles.append(jnp.concatenate(rows, axis=0).reshape(ny, GROUP, nz))
            moved = turn(to_c, tiles, nz)
            spot = m * 8 + q
            for k in range(co // GROUP):
                staged[spot, k * GROUP : (k + 1) * GROUP] = moved[
                    :, k * nz : (k + 1) * nz
                ].reshape(GROUP, ny, nz)
            copy = pltpu.make_async_copy(staged.at[spot], act_out.at[q, :, m], sems.at[spot])
            copy.start()
            copies.append(copy)
    for copy in copies:
        copy.wait()


def unpack_kernel(co, ci, packed, out):
    for ex in range(2):
        for tx in range(2):
            for ty in range(2):
                for ez in range(2):
                    for tz in range(2):
                        index = (((ex * 2 + tx) * 2 + ty) * 2 + ez) * 2 + tz
                        pair = packed[index].astype(F32)
                        for ey in range(2):
                            out[2 * ex + tx, 2 * ey + ty, 2 * ez + tz] = pair[
                                :, ey * ci : (ey + 1) * ci
                            ]


def neighbours(axis):
    count = lax.axis_size(axis)
    up = [(i, i + 1) for i in range(count - 1)]
    return up, [(b, a) for a, b in up]


def on_device(volume, kernel, cotangent):
    ci, nx, ny, nz = volume.shape
    co = kernel.shape[3]
    gx, gy = lax.axis_size("gx"), lax.axis_size("gy")
    gx_up, gx_down = neighbours("gx")
    gy_up, gy_down = neighbours("gy")
    cells = nx * gx * ny * gy * nz
    dims = (nx, ny, nz, ci, co)

    xlo = lax.ppermute(volume[:, nx - 1].transpose(1, 0, 2), "gx", gx_up)
    xhi = lax.ppermute(volume[:, 0].transpose(1, 0, 2), "gx", gx_down)
    cot = cotangent.reshape(8, co, nx, ny, nz)

    vmem = pl.BlockSpec(memory_space=pltpu.VMEM)
    smem = pl.BlockSpec(memory_space=pltpu.SMEM)
    anywhere = pl.BlockSpec(memory_space=pl.ANY)
    params = pltpu.CompilerParams(vmem_limit_bytes=28 * 1024 * 1024)
    n_in = (nx - 1) * (ny - 1)
    n_out = 2 * (ny + 1) + 2 * (nx - 1)
    flat, w, wt, vals, cot_edge, wg_part, ig_part = pl.pallas_call(
        functools.partial(inner_kernel, dims, 5),
        out_shape=(
            jax.ShapeDtypeStruct((nx, ci, ny * nz), BF16),
            jax.ShapeDtypeStruct((8 * co, 8 * ci), BF16),
            jax.ShapeDtypeStruct((8 * ci, 8 * co), BF16),
            jax.ShapeDtypeStruct((nx - 1, 8 * co, ny * nz), BF16),
            jax.ShapeDtypeStruct((nx - 1, 8 * co, nz), BF16),
            jax.ShapeDtypeStruct((8 * co, 8 * ci), F32),
            jax.ShapeDtypeStruct((nx, ci, ny * nz), F32),
        ),
        in_specs=[anywhere, anywhere, vmem],
        out_specs=(vmem,) * 7,
        scratch_shapes=[
            pltpu.VMEM(volume.shape, BF16),
            pltpu.VMEM(kernel.shape, BF16),
            pltpu.SemaphoreType.DMA((2,)),
            pltpu.VMEM((nx, ci, ny * nz), BF16),
            pltpu.VMEM((8 * co, n_in * nz), BF16),
            pltpu.VMEM((8 * co, n_in * nz), BF16),
            pltpu.VMEM((nx - 1, 8 * co, ny * nz), BF16),
        ],
        compiler_params=params,
    )(volume, kernel, cot)

    def y_row(y):
        return jnp.concatenate(
            [
                xlo[y : y + 1],
                flat[:, :, y * nz : (y + 1) * nz],
                xhi[y : y + 1],
            ],
            axis=0,
        )

    ylo = lax.ppermute(y_row(ny - 1), "gy", gy_up)
    yhi = lax.ppermute(y_row(0), "gy", gy_down)
    act, own, up, down, wg, yface = pl.pallas_call(
        functools.partial(outer_kernel, dims, 4),
        out_shape=(
            jax.ShapeDtypeStruct(cot.shape, BF16),
            jax.ShapeDtypeStruct((nx, ci, ny * nz), F32),
            jax.ShapeDtypeStruct((ci, (ny + 2) * nz), BF16),
            jax.ShapeDtypeStruct((ci, (ny + 2) * nz), BF16),
            jax.ShapeDtypeStruct((32, co, 2 * ci), BF16),
            jax.ShapeDtypeStruct((2, nx, ci, nz), F32),
        ),
        in_specs=[vmem] + [anywhere] * 4 + [vmem] * 7,
        out_specs=(anywhere,) * 4 + (vmem,) * 2,
        scratch_shapes=[
            pltpu.VMEM((2, ci, (ny + 2) * nz), BF16),
            pltpu.VMEM((2, ci, (ny + 2) * nz), F32),
            pltpu.VMEM((nx, ci, ny * nz), F32),
            pltpu.VMEM((2, ny, ci, nz), BF16),
            pltpu.VMEM((2, nx + 2, ci, nz), BF16),
            pltpu.VMEM((nx + 2, ci, (ny + 2) * nz), BF16),
            pltpu.VMEM((8 * co, n_out * nz), BF16),
            pltpu.VMEM((8 * co, n_out * nz), BF16),
            pltpu.VMEM((8 * co, ny * nz), BF16),
            pltpu.VMEM((8 * co, ny * nz), BF16),
            pltpu.VMEM((nx - 1, 8 * co, nz), BF16),
            pltpu.VMEM((8 * nx, co, ny, nz), BF16),
            pltpu.SemaphoreType.DMA((8 * nx + 4,)),
        ],
        compiler_params=params,
    )(flat, xlo, xhi, ylo, yhi, w, wt, cot, vals, cot_edge, wg_part, ig_part)

    scale = 1.0 / math.sqrt(cells)
    devices = gx * gy
    shares = wg.reshape(devices, 32 * co // devices, 2 * ci)
    shares = lax.all_to_all(shares, ("gx", "gy"), 0, 0, tiled=True)
    piece = (jnp.sum(shares.astype(F32), axis=0) * scale).astype(BF16)
    pieces = jnp.broadcast_to(piece[None], (devices,) + piece.shape)
    pieces = lax.all_to_all(pieces, ("gx", "gy"), 0, 0, tiled=True)
    weight_grad = pl.pallas_call(
        functools.partial(unpack_kernel, co, ci),
        out_shape=jax.ShapeDtypeStruct((4, 4, 4, co, ci), F32),
        in_specs=[vmem],
        out_specs=vmem,
        compiler_params=pltpu.CompilerParams(vmem_limit_bytes=8 * 1024 * 1024),
    )(pieces.reshape(32, co, 2 * ci))

    from_low = lax.ppermute(up, "gx", gx_up).astype(F32)[None]
    from_high = lax.ppermute(down, "gx", gx_down).astype(F32)[None]

    def add_x(array, lanes):
        lead = (nx - 1,) + from_low[:, :, lanes].shape[1:]
        zero = jnp.zeros(lead, F32)
        return (
            array
            + jnp.concatenate([from_low[:, :, lanes], zero], axis=0)
            + jnp.concatenate([zero, from_high[:, :, lanes]], axis=0)
        )

    later = 0.0 * piece[0, 0].astype(F32)
    send_low = (add_x(yface[0], slice(0, nz)) + later).astype(BF16)
    send_high = (add_x(yface[1], slice((ny + 1) * nz, None)) + later).astype(BF16)
    y_low = lax.ppermute(send_high, "gy", gy_up).astype(F32)
    y_high = lax.ppermute(send_low, "gy", gy_down).astype(F32)
    gap = jnp.zeros((nx, ci, (ny - 1) * nz), F32)
    total_ig = (
        add_x(own, slice(nz, (ny + 1) * nz))
        + jnp.concatenate([y_low, gap], axis=2)
        + jnp.concatenate([gap, y_high], axis=2)
    )
    input_grad = total_ig.astype(BF16).reshape(nx, ci, ny, nz).transpose(1, 0, 2, 3)
    return act.reshape(cotangent.shape), input_grad, weight_grad


def solution(mesh):
    placed = (P(None, "gx", "gy", None), P(), P(None, None, None, None, "gx", "gy", None))
    return jax.shard_map(
        on_device,
        mesh=mesh,
        in_specs=placed,
        out_specs=(placed[2], placed[0], P()),
        check_vma=False,
    )
```

```python
import functools
import math

import jax
import jax.numpy as jnp
from jax import lax
from jax.experimental import pallas as pl
from jax.experimental.pallas import tpu as pltpu
from jax.sharding import PartitionSpec as P

F32 = jnp.float32
BF16 = jnp.bfloat16
GROUP = 16


def swap_matrix(outer, inner):
    size = outer * inner
    row = lax.broadcasted_iota(jnp.int32, (size, size), 0)
    col = lax.broadcasted_iota(jnp.int32, (size, size), 1)
    return jnp.where(col == (row % outer) * inner + row // outer, 1.0, 0.0).astype(BF16)


def turn(matrix, pieces, nz):
    flat = [p.reshape(p.shape[0] * p.shape[1], nz) for p in pieces]
    moved = jnp.dot(matrix, jnp.concatenate(flat, axis=1), preferred_element_type=F32)
    return moved.astype(BF16)


def bring_plane(to_y, raw, ny, nz, put):
    for k in range(0, raw.count, 2):
        moved = turn(to_y, [raw(k), raw(k + 1)], nz)
        for y in range(ny):
            rows = slice(y * GROUP, (y + 1) * GROUP)
            put(k, y, moved[rows, :nz])
            put(k + 1, y, moved[rows, nz:])


class Tiles:
    def __init__(self, count, get):
        self.count, self.get = count, get

    def __call__(self, k):
        return self.get(k)


def columns_pass(dims, chunk, columns, block, rolled, w, cot_at, put_value, put_foreign, wg_add, ga, gb):
    nx, ny, nz, ci, co = dims
    half = 4 * ci
    first = lax.broadcasted_iota(jnp.int32, (co, nz), 1) == 0
    zeros = jnp.zeros((2 * co, nz), BF16)

    def corners(get, some):
        return jnp.concatenate(
            [
                jnp.concatenate([get(i + 1 - ex, j + 1 - ey) for i, j in some], axis=1)
                for ex in range(2)
                for ey in range(2)
            ],
            axis=0,
        )

    starts = range(0, len(columns), chunk)
    for c0 in starts:
        some = columns[c0 : c0 + chunk]
        back = jnp.dot(w[:, half:], corners(rolled, some), preferred_element_type=F32)
        here = jnp.dot(w[:, :half], corners(block, some), preferred_element_type=F32)
        for k, (i, j) in enumerate(some):
            cols = slice(k * nz, (k + 1) * nz)
            wide = slice((c0 + k) * nz, (c0 + k + 1) * nz)
            for tx in range(2):
                for ty in range(2):
                    sx, sy = 1 - tx, 1 - ty
                    m, n = i - sx, j - sy
                    base = (2 * tx + ty) * 2 * co
                    if not (0 <= m < nx and 0 <= n < ny):
                        ga[base : base + 2 * co, wide] = zeros
                        gb[base : base + 2 * co, wide] = zeros
                        r = slice(base, base + co)
                        put_foreign(
                            (i, j, tx, ty), 0, back[r, cols] + jnp.where(first, 0.0, here[r, cols])
                        )
                        r = slice(base + co, base + 2 * co)
                        put_foreign(
                            (i, j, tx, ty), 1, jnp.where(first, 0.0, back[r, cols]) + here[r, cols]
                        )
                        continue
                    for tz in range(2):
                        sz = 1 - tz
                        r = slice(base + tz * co, base + (tz + 1) * co)
                        low, high = back[r, cols], here[r, cols]
                        if sz == 1:
                            before = low + jnp.where(first, 0.0, high)
                            before = pltpu.roll(before, nz - 1, 1)
                        else:
                            before = jnp.where(first, 0.0, low) + high
                        q = (2 * sx + sy) * 2 + sz
                        sig = 0.5 * jnp.tanh(0.5 * before) + 0.5
                        value = before * sig
                        put_value(q, m, n, value.astype(BF16))
                        slope = sig + value * (1.0 - sig)
                        grad = cot_at(q, m, n).astype(F32) * slope
                        if sz == 1:
                            grad = pltpu.roll(grad, 1, 1)
                        whole = grad.astype(BF16)
                        cut = jnp.where(first, 0.0, grad).astype(BF16)
                        ga[r, wide] = cut if sz == 0 else whole
                        gb[r, wide] = cut if sz == 1 else whole

    nt = (((1,), (1,)), ((), ()))
    for part, (grads, get) in enumerate(((gb, block), (ga, rolled))):
        wg_add(
            part,
            lax.dot_general(grads[...], corners(get, columns), nt, preferred_element_type=F32),
        )


def input_pass(dims, chunk, columns, wt, cut_grads, ig_add):
    nx, ny, nz, ci, co = dims
    half = 4 * ci
    started = set()
    for c0 in range(0, len(columns), chunk):
        some = columns[c0 : c0 + chunk]
        left, right = cut_grads(c0, some)
        back = jnp.dot(wt[half:], left, preferred_element_type=F32)
        here = jnp.dot(wt[:half], right, preferred_element_type=F32)
        for k, (i, j) in enumerate(some):
            cols = slice(k * nz, (k + 1) * nz)
            both = here[:, cols] + pltpu.roll(back[:, cols], nz - 1, 1)
            for ex in range(2):
                for ey in range(2):
                    m, y = i - ex, j - ey
                    if 0 <= m < nx and 0 <= y < ny:
                        r = (2 * ex + ey) * ci
                        ig_add(m, y, both[r : r + ci], (m, y) not in started)
                        started.add((m, y))
    return started


def outer_columns(nx, ny):
    columns = [(i, j) for i in (0, nx) for j in range(ny + 1)]
    return columns + [(i, j) for i in range(1, nx) for j in (0, ny)]


def foreign_spots(nx, ny):
    spots = {}
    for i, j in outer_columns(nx, ny):
        for tx in range(2):
            for ty in range(2):
                m, n = i - 1 + tx, j - 1 + ty
                if not (0 <= m < nx and 0 <= n < ny):
                    spots[i, j, tx, ty] = len(spots)
    return spots


def is_inner(q, m, nx):
    return 1 <= m + q // 4 < nx


def edge_row(q, ny):
    return (ny - 1) if q // 2 % 2 else 0


def inner_kernel(
    dims,
    chunk,
    vol_in,
    taps_in,
    cot,
    flat,
    w,
    wt,
    vals_out,
    cot_edge,
    wg,
    ig_out,
    face_up,
    face_down,
    vals,
    ig,
    vol,
    taps,
    sems,
    vm,
    ga,
    gb,
    cots,
):
    nx, ny, nz, ci, co = dims
    half = 4 * ci
    to_y = swap_matrix(GROUP, ny)
    arriving = [
        pltpu.make_async_copy(vol_in, vol, sems.at[0]),
        pltpu.make_async_copy(taps_in, taps, sems.at[1]),
    ]
    leaving = [
        pltpu.make_async_copy(cot.at[4:, :, nx - 1], face_up, sems.at[2]),
        pltpu.make_async_copy(cot.at[:4, :, 0], face_down, sems.at[3]),
    ]
    for copy in arriving + leaving:
        copy.start()

    for i in range(1, nx):
        for q in range(8):
            m = i - q // 4

            def put(k, y, rows, i=i, q=q):
                r = slice(q * co + k * GROUP, q * co + (k + 1) * GROUP)
                cots[i - 1, r, y * nz : (y + 1) * nz] = rows
                if y == edge_row(q, ny):
                    cot_edge[i - 1, r] = rows

            tiles = Tiles(
                co // GROUP, lambda k, q=q, m=m: cot[q, k * GROUP : (k + 1) * GROUP, m]
            )
            bring_plane(to_y, tiles, ny, nz, put)

    for copy in arriving:
        copy.wait()
    for tx in range(2):
        for ty in range(2):
            for tz in range(2):
                r = ((2 * tx + ty) * 2 + tz) * co
                for ez in range(2):
                    for ex in range(2):
                        pair = [taps[2 * ex + tx, 2 * ey + ty, 2 * ez + tz] for ey in range(2)]
                        c = (2 * ez + ex) * 2 * ci
                        w[r : r + co, c : c + 2 * ci] = jnp.concatenate(pair, axis=1)
    wt[...] = w[...].T

    for x in range(nx):

        def put(k, y, rows, x=x):
            r = slice(k * GROUP, (k + 1) * GROUP)
            lanes = slice(y * nz, (y + 1) * nz)
            flat[x, r, lanes] = rows
            vm[x, r, lanes] = pltpu.roll(rows.astype(F32), 1, 1).astype(BF16)

        tiles = Tiles(
            ci // GROUP, lambda k, x=x: vol[k * GROUP : (k + 1) * GROUP, x]
        )
        bring_plane(to_y, tiles, ny, nz, put)

    def block(x, y):
        return flat[x - 1, :, (y - 1) * nz : y * nz]

    def rolled(x, y):
        return vm[x - 1, :, (y - 1) * nz : y * nz]

    def cot_at(q, m, n):
        return cots[m + q // 4 - 1, q * co : (q + 1) * co, n * nz : (n + 1) * nz]

    def put_value(q, m, n, value):
        vals[m + q // 4 - 1, q * co : (q + 1) * co, n * nz : (n + 1) * nz] = value

    def wg_add(part, total):
        wg[:, part * half : (part + 1) * half] = total

    def ig_add(m, y, value, fresh):
        lanes = slice(y * nz, (y + 1) * nz)
        ig[m, :, lanes] = value if fresh else ig[m, :, lanes] + value

    def cut_grads(c0, some):
        wide = slice(c0 * nz, (c0 + len(some)) * nz)
        return ga[:, wide], gb[:, wide]

    columns = [(i, j) for i in range(1, nx) for j in range(1, ny)]
    columns_pass(
        dims, chunk, columns, block, rolled, w, cot_at, put_value, None, wg_add, ga, gb
    )
    input_pass(dims, chunk, columns, wt, cut_grads, ig_add)
    leaving.append(pltpu.make_async_copy(vals, vals_out, sems.at[4]))
    leaving.append(pltpu.make_async_copy(ig, ig_out, sems.at[5]))
    for copy in leaving[2:]:
        copy.start()
    for copy in leaving:
        copy.wait()


def outer_kernel(
    dims,
    chunk,
    flat,
    xlo_in,
    xhi_in,
    ylo_in,
    yhi_in,
    w,
    cot,
    cot_edge,
    wg_in,
    wg,
    ga_out,
    gb_out,
    pre_out,
    vals_out,
    val_edge_out,
    xraw,
    yraw,
    vm,
    ga,
    gb,
    pre,
    cots,
    vals,
    val_edge,
    sems,
):
    nx, ny, nz, ci, co = dims
    half = 4 * ci
    to_y = swap_matrix(GROUP, ny)
    arriving = [
        pltpu.make_async_copy(xlo_in.at[: ny * ci], xraw.at[0], sems.at[0]),
        pltpu.make_async_copy(xhi_in.at[: ny * ci], xraw.at[1], sems.at[1]),
        pltpu.make_async_copy(ylo_in.at[: (nx + 2) * ci], yraw.at[0], sems.at[2]),
        pltpu.make_async_copy(yhi_in.at[: (nx + 2) * ci], yraw.at[1], sems.at[3]),
    ]
    for copy in arriving:
        copy.start()

    for side in range(2):
        for q in range(4 * side, 4 * side + 4):

            def put(k, y, rows, q=q):
                r = slice(q * co + k * GROUP, q * co + (k + 1) * GROUP)
                cots[r, y * nz : (y + 1) * nz] = rows

            tiles = Tiles(
                co // GROUP,
                lambda k, q=q, side=side: cot[
                    q, k * GROUP : (k + 1) * GROUP, side * (nx - 1)
                ],
            )
            bring_plane(to_y, tiles, ny, nz, put)

    for copy in arriving:
        copy.wait()

    def block(x, y):
        if y == 0:
            return yraw[0, x * ci : (x + 1) * ci]
        if y == ny + 1:
            return yraw[1, x * ci : (x + 1) * ci]
        if x == 0:
            return xraw[0, (y - 1) * ci : y * ci]
        if x == nx + 1:
            return xraw[1, (y - 1) * ci : y * ci]
        return flat[x - 1, :, (y - 1) * nz : y * nz]

    for x in range(nx + 2):
        for y in range(ny + 2):
            vm[x, :, y * nz : (y + 1) * nz] = pltpu.roll(block(x, y).astype(F32), 1, 1).astype(
                BF16
            )

    def rolled(x, y):
        return vm[x, :, y * nz : (y + 1) * nz]

    def cot_at(q, m, n):
        r = slice(q * co, (q + 1) * co)
        if is_inner(q, m, nx):
            return cot_edge[m + q // 4 - 1, r]
        return cots[r, n * nz : (n + 1) * nz]

    def put_value(q, m, n, value):
        r = slice(q * co, (q + 1) * co)
        if is_inner(q, m, nx):
            val_edge[m + q // 4 - 1, r] = value
        else:
            vals[r, n * nz : (n + 1) * nz] = value

    spots = foreign_spots(nx, ny)

    def put_foreign(key, tz, value):
        pre[spots[key], tz * co : (tz + 1) * co] = value

    leaving = []

    def leave():
        for k, (src, dst) in enumerate(
            ((ga, ga_out), (gb, gb_out), (pre, pre_out), (vals, vals_out), (val_edge, val_edge_out))
        ):
            leaving.append(pltpu.make_async_copy(src, dst, sems.at[4 + k]))
            leaving[-1].start()

    def wg_add(part, total):
        if part == 0:
            leave()
        total = total + wg_in[:, part * half : (part + 1) * half]
        for ex in range(2):
            for row in range(8):
                tx, ty, tz = row // 4, row // 2 % 2, row % 2
                index = ((tx * 2 + ty) * 2 + part) * 2 + tz
                wg[ex * 16 + index] = total[
                    row * co : (row + 1) * co, ex * 2 * ci : (ex + 1) * 2 * ci
                ].astype(BF16)

    columns_pass(
        dims,
        chunk,
        outer_columns(nx, ny),
        block,
        rolled,
        w,
        cot_at,
        put_value,
        put_foreign,
        wg_add,
        ga,
        gb,
    )
    for copy in leaving:
        copy.wait()


def last_kernel(
    dims,
    chunk,
    ga_in,
    gb_in,
    pre_in,
    vals_in,
    val_edge_in,
    xlo_in,
    xhi_in,
    ylo_in,
    yhi_in,
    wt_in,
    inner_vals_in,
    ig_in,
    act_out,
    ig_out,
    ga,
    gb,
    pre,
    vals,
    val_edge,
    xraw,
    yraw,
    wt,
    inner_vals,
    ig,
    cots,
    staged,
    ig_staged,
    sems,
):
    nx, ny, nz, ci, co = dims
    to_y = swap_matrix(GROUP, ny)
    to_c = swap_matrix(ny, GROUP)
    skip = (nx + 2) * ci
    early = [(vals_in, vals), (val_edge_in, val_edge), (inner_vals_in, inner_vals)]
    late = [
        (xlo_in, xraw.at[0]),
        (xhi_in, xraw.at[1]),
        (ylo_in.at[skip:], yraw.at[0]),
        (yhi_in.at[skip:], yraw.at[1]),
        (ga_in, ga),
        (gb_in, gb),
        (pre_in, pre),
        (wt_in, wt),
        (ig_in, ig),
    ]
    copies = [
        pltpu.make_async_copy(src, dst, sems.at[k]) for k, (src, dst) in enumerate(early + late)
    ]
    for copy in copies:
        copy.start()
    spot = len(copies)
    for copy in copies[: len(early)]:
        copy.wait()
    leaving = []

    for m in range(nx):
        for q in range(8):
            tiles = []
            for k in range(co // GROUP):
                r = slice(q * co + k * GROUP, q * co + (k + 1) * GROUP)
                rows = []
                for y in range(ny):
                    lanes = slice(y * nz, (y + 1) * nz)
                    if not is_inner(q, m, nx):
                        rows.append(vals[r, lanes])
                    elif y == edge_row(q, ny):
                        rows.append(val_edge[m + q // 4 - 1, r])
                    else:
                        rows.append(inner_vals[m + q // 4 - 1, r, lanes])
                tiles.append(jnp.concatenate(rows, axis=0).reshape(ny, GROUP, nz))
            moved = turn(to_c, tiles, nz)
            index = m * 8 + q
            for k in range(co // GROUP):
                staged[index, k * GROUP : (k + 1) * GROUP] = moved[
                    :, k * nz : (k + 1) * nz
                ].reshape(GROUP, ny, nz)
            leaving.append(
                pltpu.make_async_copy(
                    staged.at[index], act_out.at[q, :, m], sems.at[spot + index]
                )
            )
            leaving[-1].start()

    for copy in copies[len(early) :]:
        copy.wait()
    for side in range(2):
        for p in range(4):

            def put(k, y, rows, side=side, p=p):
                r = slice(p * co + k * GROUP, p * co + (k + 1) * GROUP)
                cots[side, r, y * nz : (y + 1) * nz] = rows

            tiles = Tiles(
                co // GROUP,
                lambda k, side=side, p=p: xraw[side, p, k * GROUP : (k + 1) * GROUP],
            )
            bring_plane(to_y, tiles, ny, nz, put)

    spots = foreign_spots(nx, ny)
    first = lax.broadcasted_iota(jnp.int32, (co, nz), 1) == 0
    corner = 4 * co * nx

    def foreign(i, j, tx, ty, tz):
        sx, sy, sz = 1 - tx, 1 - ty, 1 - tz
        m, n = i - sx, j - sy
        if 0 <= n < ny:
            side = 0 if m < 0 else 1
            r = (2 * sy + sz) * co
            cot = cots[side, r : r + co, n * nz : (n + 1) * nz]
        else:
            end = 0 if n < 0 else 1
            if 0 <= m < nx:
                r = ((m * 2 + sx) * 2 + sz) * co
            else:
                r = corner + ((0 if m < 0 else 2) + sz) * co
            cot = yraw[end, r : r + co]
        cot = cot.astype(F32)
        if sz == 1:
            cot = pltpu.roll(cot, 1, 1)
        before = pre[spots[i, j, tx, ty], tz * co : (tz + 1) * co]
        sig = 0.5 * jnp.tanh(0.5 * before) + 0.5
        grad = cot * (sig + before * sig * (1.0 - sig))
        whole = grad.astype(BF16)
        cut = jnp.where(first, 0.0, grad).astype(BF16)
        return (whole, cut) if sz == 1 else (cut, whole)

    def cut_grads(c0, some):
        lefts, rights = [], []
        for k, (i, j) in enumerate(some):
            wide = slice((c0 + k) * nz, (c0 + k + 1) * nz)
            left, right = [], []
            for tx in range(2):
                for ty in range(2):
                    base = (2 * tx + ty) * 2 * co
                    if (i, j, tx, ty) in spots:
                        for tz in range(2):
                            one, two = foreign(i, j, tx, ty, tz)
                            left.append(one)
                            right.append(two)
                    else:
                        left.append(ga[base : base + 2 * co, wide])
                        right.append(gb[base : base + 2 * co, wide])
            lefts.append(jnp.concatenate(left, axis=0))
            rights.append(jnp.concatenate(right, axis=0))
        return jnp.concatenate(lefts, axis=1), jnp.concatenate(rights, axis=1)

    def ig_add(m, y, value, fresh):
        lanes = slice(y * nz, (y + 1) * nz)
        ig[m, :, lanes] = ig[m, :, lanes] + value

    input_pass(dims, chunk, outer_columns(nx, ny), wt, cut_grads, ig_add)
    for m in range(nx):
        for k in range(0, ci // GROUP, 2):
            tiles = []
            for h in range(2):
                r = slice((k + h) * GROUP, (k + h + 1) * GROUP)
                rows = [
                    ig[m, r, y * nz : (y + 1) * nz].astype(BF16) for y in range(ny)
                ]
                tiles.append(jnp.concatenate(rows, axis=0).reshape(ny, GROUP, nz))
            moved = turn(to_c, tiles, nz)
            for h in range(2):
                ig_staged[(k + h) * GROUP : (k + h + 1) * GROUP, m] = moved[
                    :, h * nz : (h + 1) * nz
                ].reshape(GROUP, ny, nz)
    leaving.append(pltpu.make_async_copy(ig_staged, ig_out, sems.at[spot + 8 * nx]))
    leaving[-1].start()
    for copy in leaving:
        copy.wait()


def unpack_kernel(co, ci, packed, out):
    for ex in range(2):
        for tx in range(2):
            for ty in range(2):
                for ez in range(2):
                    for tz in range(2):
                        index = (((ex * 2 + tx) * 2 + ty) * 2 + ez) * 2 + tz
                        pair = packed[index].astype(F32)
                        for ey in range(2):
                            out[2 * ex + tx, 2 * ey + ty, 2 * ez + tz] = pair[
                                :, ey * ci : (ey + 1) * ci
                            ]


def neighbours(axis):
    count = lax.axis_size(axis)
    up = [(i, i + 1) for i in range(count - 1)]
    return up, [(b, a) for a, b in up]


def on_device(volume, kernel, cotangent):
    ci, nx, ny, nz = volume.shape
    co = kernel.shape[3]
    gx, gy = lax.axis_size("gx"), lax.axis_size("gy")
    gx_up, gx_down = neighbours("gx")
    gy_up, gy_down = neighbours("gy")
    cells = nx * gx * ny * gy * nz
    dims = (nx, ny, nz, ci, co)

    cot = cotangent.reshape(8, co, nx, ny, nz)

    def corner(sx, sy):
        m, n = (nx - 1) * sx, (ny - 1) * sy
        return cotangent[sx, sy, :, :, m, n].reshape(2 * co, nz)

    def x_message(sx):
        plane = volume[:, (nx - 1) * sx].transpose(1, 0, 2).reshape(ny * ci, nz)
        return jnp.concatenate([plane, corner(sx, 0), corner(sx, 1)], axis=0)

    xlo = lax.ppermute(x_message(1), "gx", gx_up)
    xhi = lax.ppermute(x_message(0), "gx", gx_down)

    vmem = pl.BlockSpec(memory_space=pltpu.VMEM)
    smem = pl.BlockSpec(memory_space=pltpu.SMEM)
    anywhere = pl.BlockSpec(memory_space=pl.ANY)
    params = pltpu.CompilerParams(vmem_limit_bytes=28 * 1024 * 1024)
    n_in = (nx - 1) * (ny - 1)
    n_out = 2 * (ny + 1) + 2 * (nx - 1)
    flat, w, wt, vals, cot_edge, wg_part, ig_part, face_up, face_down = pl.pallas_call(
        functools.partial(inner_kernel, dims, 5),
        out_shape=(
            jax.ShapeDtypeStruct((nx, ci, ny * nz), BF16),
            jax.ShapeDtypeStruct((8 * co, 8 * ci), BF16),
            jax.ShapeDtypeStruct((8 * ci, 8 * co), BF16),
            jax.ShapeDtypeStruct((nx - 1, 8 * co, ny * nz), BF16),
            jax.ShapeDtypeStruct((nx - 1, 8 * co, nz), BF16),
            jax.ShapeDtypeStruct((8 * co, 8 * ci), F32),
            jax.ShapeDtypeStruct((nx, ci, ny * nz), F32),
            jax.ShapeDtypeStruct((4, co, ny, nz), BF16),
            jax.ShapeDtypeStruct((4, co, ny, nz), BF16),
        ),
        in_specs=[anywhere, anywhere, vmem],
        out_specs=(vmem,) * 3 + (anywhere,) + (vmem,) * 2 + (anywhere,) * 3,
        scratch_shapes=[
            pltpu.VMEM((nx - 1, 8 * co, ny * nz), BF16),
            pltpu.VMEM((nx, ci, ny * nz), F32),
            pltpu.VMEM(volume.shape, BF16),
            pltpu.VMEM(kernel.shape, BF16),
            pltpu.SemaphoreType.DMA((6,)),
            pltpu.VMEM((nx, ci, ny * nz), BF16),
            pltpu.VMEM((8 * co, n_in * nz), BF16),
            pltpu.VMEM((8 * co, n_in * nz), BF16),
            pltpu.VMEM((nx - 1, 8 * co, ny * nz), BF16),
        ],
        compiler_params=params,
    )(volume, kernel, cot)

    def y_message(sy):
        y = (ny - 1) * sy
        rows = slice(y * ci, (y + 1) * ci)
        own = cotangent[:, sy, :, :, :, y].transpose(3, 0, 1, 2, 4).reshape(4 * co * nx, nz)
        corner = slice((ny * ci + sy * 2 * co), (ny * ci + (sy + 1) * 2 * co))
        return jnp.concatenate(
            [
                xlo[rows],
                flat[:, :, y * nz : (y + 1) * nz].reshape(nx * ci, nz),
                xhi[rows],
                own,
                xlo[corner],
                xhi[corner],
            ],
            axis=0,
        )

    ylo = lax.ppermute(y_message(1), "gy", gy_up)
    yhi = lax.ppermute(y_message(0), "gy", gy_down)
    face_lo = lax.ppermute(face_up, "gx", gx_up)
    face_hi = lax.ppermute(face_down, "gx", gx_down)
    foreign = len(foreign_spots(nx, ny))
    kept = (
        jax.ShapeDtypeStruct((8 * co, n_out * nz), BF16),
        jax.ShapeDtypeStruct((8 * co, n_out * nz), BF16),
        jax.ShapeDtypeStruct((foreign, 2 * co, nz), F32),
        jax.ShapeDtypeStruct((8 * co, ny * nz), BF16),
        jax.ShapeDtypeStruct((nx - 1, 8 * co, nz), BF16),
    )
    held = [pltpu.VMEM(k.shape, k.dtype) for k in kept]
    wg, *passed = pl.pallas_call(
        functools.partial(outer_kernel, dims, 4),
        out_shape=(jax.ShapeDtypeStruct((32, co, 2 * ci), BF16),) + kept,
        in_specs=[vmem] + [anywhere] * 4 + [vmem] * 4,
        out_specs=(vmem,) + (anywhere,) * 5,
        scratch_shapes=[
            pltpu.VMEM((2, ny * ci, nz), BF16),
            pltpu.VMEM((2, (nx + 2) * ci, nz), BF16),
            pltpu.VMEM((nx + 2, ci, (ny + 2) * nz), BF16),
        ]
        + held[:3]
        + [pltpu.VMEM((8 * co, ny * nz), BF16)]
        + held[3:]
        + [pltpu.SemaphoreType.DMA((9,))],
        compiler_params=params,
    )(flat, xlo, xhi, ylo, yhi, w, cot, cot_edge, wg_part)
    act, input_grad = pl.pallas_call(
        functools.partial(last_kernel, dims, 4),
        out_shape=(
            jax.ShapeDtypeStruct(cot.shape, BF16),
            jax.ShapeDtypeStruct(volume.shape, BF16),
        ),
        in_specs=[anywhere] * 12,
        out_specs=(anywhere,) * 2,
        scratch_shapes=held
        + [
            pltpu.VMEM((2, 4, co, ny, nz), BF16),
            pltpu.VMEM((2, 4 * co * nx + 4 * co, nz), BF16),
            pltpu.VMEM((8 * ci, 8 * co), BF16),
            pltpu.VMEM((nx - 1, 8 * co, ny * nz), BF16),
            pltpu.VMEM((nx, ci, ny * nz), F32),
            pltpu.VMEM((2, 4 * co, ny * nz), BF16),
            pltpu.VMEM((8 * nx, co, ny, nz), BF16),
            pltpu.VMEM(volume.shape, BF16),
            pltpu.SemaphoreType.DMA((13 + 8 * nx,)),
        ],
        compiler_params=params,
    )(*passed, face_lo, face_hi, ylo, yhi, wt, vals, ig_part)

    scale = 1.0 / math.sqrt(cells)
    devices = gx * gy
    shares = wg.reshape(devices, 32 * co // devices, 2 * ci)
    shares = lax.all_to_all(shares, ("gx", "gy"), 0, 0, tiled=True)
    piece = (jnp.sum(shares.astype(F32), axis=0) * scale).astype(BF16)
    pieces = jnp.broadcast_to(piece[None], (devices,) + piece.shape)
    pieces = lax.all_to_all(pieces, ("gx", "gy"), 0, 0, tiled=True)
    weight_grad = pl.pallas_call(
        functools.partial(unpack_kernel, co, ci),
        out_shape=jax.ShapeDtypeStruct((4, 4, 4, co, ci), F32),
        in_specs=[vmem],
        out_specs=vmem,
        compiler_params=pltpu.CompilerParams(vmem_limit_bytes=8 * 1024 * 1024),
    )(pieces.reshape(32, co, 2 * ci))

    return act.reshape(cotangent.shape), input_grad, weight_grad


def solution(mesh):
    placed = (P(None, "gx", "gy", None), P(), P(None, None, None, None, "gx", "gy", None))
    return jax.shard_map(
        on_device,
        mesh=mesh,
        in_specs=placed,
        out_specs=(placed[2], placed[0], P()),
        check_vma=False,
    )
```

```python
import functools
import math

import jax
import jax.numpy as jnp
from jax import lax
from jax.experimental import pallas as pl
from jax.experimental.pallas import tpu as pltpu
from jax.sharding import PartitionSpec as P

F32 = jnp.float32
BF16 = jnp.bfloat16
GROUP = 16


def swap_matrix(outer, inner):
    size = outer * inner
    row = lax.broadcasted_iota(jnp.int32, (size, size), 0)
    col = lax.broadcasted_iota(jnp.int32, (size, size), 1)
    return jnp.where(col == (row % outer) * inner + row // outer, 1.0, 0.0).astype(BF16)


def turn(matrix, pieces, nz):
    flat = [p.reshape(p.shape[0] * p.shape[1], nz) for p in pieces]
    moved = jnp.dot(matrix, jnp.concatenate(flat, axis=1), preferred_element_type=F32)
    return moved.astype(BF16)


def bring_plane(to_y, raw, ny, nz, put):
    for k in range(0, raw.count, 2):
        moved = turn(to_y, [raw(k), raw(k + 1)], nz)
        for y in range(ny):
            rows = slice(y * GROUP, (y + 1) * GROUP)
            put(k, y, moved[rows, :nz])
            put(k + 1, y, moved[rows, nz:])


class Tiles:
    def __init__(self, count, get):
        self.count, self.get = count, get

    def __call__(self, k):
        return self.get(k)


def corners(get, some):
    return jnp.concatenate(
        [
            jnp.concatenate([get(i + 1 - ex, j + 1 - ey) for i, j in some], axis=1)
            for ex in range(2)
            for ey in range(2)
        ],
        axis=0,
    )


def forward_pass(dims, chunk, columns, block, rolled, w, cot_at, put_value, put_foreign, ga, gb):
    nx, ny, nz, ci, co = dims
    half = 4 * ci
    first = lax.broadcasted_iota(jnp.int32, (co, nz), 1) == 0
    zeros = jnp.zeros((2 * co, nz), BF16)

    starts = range(0, len(columns), chunk)
    for c0 in starts:
        some = columns[c0 : c0 + chunk]
        back = jnp.dot(w[:, half:], corners(rolled, some), preferred_element_type=F32)
        here = jnp.dot(w[:, :half], corners(block, some), preferred_element_type=F32)
        for k, (i, j) in enumerate(some):
            cols = slice(k * nz, (k + 1) * nz)
            wide = slice((c0 + k) * nz, (c0 + k + 1) * nz)
            for tx in range(2):
                for ty in range(2):
                    sx, sy = 1 - tx, 1 - ty
                    m, n = i - sx, j - sy
                    base = (2 * tx + ty) * 2 * co
                    if not (0 <= m < nx and 0 <= n < ny):
                        ga[base : base + 2 * co, wide] = zeros
                        gb[base : base + 2 * co, wide] = zeros
                        r = slice(base, base + co)
                        put_foreign(
                            (i, j, tx, ty), 0, back[r, cols] + jnp.where(first, 0.0, here[r, cols])
                        )
                        r = slice(base + co, base + 2 * co)
                        put_foreign(
                            (i, j, tx, ty), 1, jnp.where(first, 0.0, back[r, cols]) + here[r, cols]
                        )
                        continue
                    for tz in range(2):
                        sz = 1 - tz
                        r = slice(base + tz * co, base + (tz + 1) * co)
                        low, high = back[r, cols], here[r, cols]
                        if sz == 1:
                            before = low + jnp.where(first, 0.0, high)
                            before = pltpu.roll(before, nz - 1, 1)
                        else:
                            before = jnp.where(first, 0.0, low) + high
                        q = (2 * sx + sy) * 2 + sz
                        sig = 0.5 * jnp.tanh(0.5 * before) + 0.5
                        value = before * sig
                        put_value(q, m, n, value.astype(BF16))
                        slope = sig + value * (1.0 - sig)
                        grad = cot_at(q, m, n).astype(F32) * slope
                        if sz == 1:
                            grad = pltpu.roll(grad, 1, 1)
                        whole = grad.astype(BF16)
                        cut = jnp.where(first, 0.0, grad).astype(BF16)
                        ga[r, wide] = cut if sz == 0 else whole
                        gb[r, wide] = cut if sz == 1 else whole


def weight_pass(columns, block, rolled, ga, gb, wg_add):
    nt = (((1,), (1,)), ((), ()))
    for part, (grads, get) in enumerate(((gb, block), (ga, rolled))):
        wg_add(
            part,
            lax.dot_general(grads[...], corners(get, columns), nt, preferred_element_type=F32),
        )


def input_pass(dims, chunk, columns, wt, cut_grads, ig_add):
    nx, ny, nz, ci, co = dims
    half = 4 * ci
    started = set()
    for c0 in range(0, len(columns), chunk):
        some = columns[c0 : c0 + chunk]
        left, right = cut_grads(c0, some)
        back = jnp.dot(wt[half:], left, preferred_element_type=F32)
        here = jnp.dot(wt[:half], right, preferred_element_type=F32)
        for k, (i, j) in enumerate(some):
            cols = slice(k * nz, (k + 1) * nz)
            both = here[:, cols] + pltpu.roll(back[:, cols], nz - 1, 1)
            for ex in range(2):
                for ey in range(2):
                    m, y = i - ex, j - ey
                    if 0 <= m < nx and 0 <= y < ny:
                        r = (2 * ex + ey) * ci
                        ig_add(m, y, both[r : r + ci], (m, y) not in started)
                        started.add((m, y))
    return started


def outer_columns(nx, ny):
    columns = [(i, j) for i in (0, nx) for j in range(ny + 1)]
    return columns + [(i, j) for i in range(1, nx) for j in (0, ny)]


def foreign_spots(nx, ny):
    spots = {}
    for i, j in outer_columns(nx, ny):
        for tx in range(2):
            for ty in range(2):
                m, n = i - 1 + tx, j - 1 + ty
                if not (0 <= m < nx and 0 <= n < ny):
                    spots[i, j, tx, ty] = len(spots)
    return spots


def is_inner(q, m, nx):
    return 1 <= m + q // 4 < nx


def edge_row(q, ny):
    return (ny - 1) if q // 2 % 2 else 0


def inner_kernel(
    dims,
    chunk,
    vol_in,
    taps_in,
    cot,
    flat,
    w,
    wt,
    vals,
    cot_edge,
    wg,
    ig,
    face_up,
    face_down,
    vol,
    taps,
    sems,
    vm,
    ga,
    gb,
    cots,
):
    nx, ny, nz, ci, co = dims
    half = 4 * ci
    to_y = swap_matrix(GROUP, ny)
    arriving = [
        pltpu.make_async_copy(vol_in, vol, sems.at[0]),
        pltpu.make_async_copy(taps_in, taps, sems.at[1]),
    ]
    leaving = [
        pltpu.make_async_copy(cot.at[4:, :, nx - 1], face_up, sems.at[2]),
        pltpu.make_async_copy(cot.at[:4, :, 0], face_down, sems.at[3]),
    ]
    for copy in arriving + leaving:
        copy.start()

    for i in range(1, nx):
        for q in range(8):
            m = i - q // 4

            def put(k, y, rows, i=i, q=q):
                r = slice(q * co + k * GROUP, q * co + (k + 1) * GROUP)
                cots[i - 1, r, y * nz : (y + 1) * nz] = rows
                if y == edge_row(q, ny):
                    cot_edge[i - 1, r] = rows

            tiles = Tiles(
                co // GROUP, lambda k, q=q, m=m: cot[q, k * GROUP : (k + 1) * GROUP, m]
            )
            bring_plane(to_y, tiles, ny, nz, put)

    for copy in arriving:
        copy.wait()
    for tx in range(2):
        for ty in range(2):
            for tz in range(2):
                r = ((2 * tx + ty) * 2 + tz) * co
                for ez in range(2):
                    for ex in range(2):
                        pair = [taps[2 * ex + tx, 2 * ey + ty, 2 * ez + tz] for ey in range(2)]
                        c = (2 * ez + ex) * 2 * ci
                        w[r : r + co, c : c + 2 * ci] = jnp.concatenate(pair, axis=1)
    wt[...] = w[...].T

    for x in range(nx):

        def put(k, y, rows, x=x):
            r = slice(k * GROUP, (k + 1) * GROUP)
            lanes = slice(y * nz, (y + 1) * nz)
            flat[x, r, lanes] = rows
            vm[x, r, lanes] = pltpu.roll(rows.astype(F32), 1, 1).astype(BF16)

        tiles = Tiles(
            ci // GROUP, lambda k, x=x: vol[k * GROUP : (k + 1) * GROUP, x]
        )
        bring_plane(to_y, tiles, ny, nz, put)

    def block(x, y):
        return flat[x - 1, :, (y - 1) * nz : y * nz]

    def rolled(x, y):
        return vm[x - 1, :, (y - 1) * nz : y * nz]

    def cot_at(q, m, n):
        return cots[m + q // 4 - 1, q * co : (q + 1) * co, n * nz : (n + 1) * nz]

    def put_value(q, m, n, value):
        vals[m + q // 4 - 1, q * co : (q + 1) * co, n * nz : (n + 1) * nz] = value

    def wg_add(part, total):
        wg[:, part * half : (part + 1) * half] = total

    def ig_add(m, y, value, fresh):
        lanes = slice(y * nz, (y + 1) * nz)
        ig[m, :, lanes] = value if fresh else ig[m, :, lanes] + value

    def cut_grads(c0, some):
        wide = slice(c0 * nz, (c0 + len(some)) * nz)
        return ga[:, wide], gb[:, wide]

    columns = [(i, j) for i in range(1, nx) for j in range(1, ny)]
    forward_pass(dims, chunk, columns, block, rolled, w, cot_at, put_value, None, ga, gb)
    weight_pass(columns, block, rolled, ga, gb, wg_add)
    input_pass(dims, chunk, columns, wt, cut_grads, ig_add)
    for copy in leaving:
        copy.wait()


def outer_kernel(
    dims,
    chunk,
    flat,
    xlo_in,
    xhi_in,
    ylo_in,
    yhi_in,
    w,
    cot,
    cot_edge,
    ga,
    gb,
    pre,
    vals,
    val_edge,
    plain,
    vm,
    xraw,
    yraw,
    cots,
    sems,
):
    nx, ny, nz, ci, co = dims
    to_y = swap_matrix(GROUP, ny)
    arriving = [
        pltpu.make_async_copy(xlo_in.at[: ny * ci], xraw.at[0], sems.at[0]),
        pltpu.make_async_copy(xhi_in.at[: ny * ci], xraw.at[1], sems.at[1]),
        pltpu.make_async_copy(ylo_in.at[: (nx + 2) * ci], yraw.at[0], sems.at[2]),
        pltpu.make_async_copy(yhi_in.at[: (nx + 2) * ci], yraw.at[1], sems.at[3]),
    ]
    for copy in arriving:
        copy.start()

    for side in range(2):
        for q in range(4 * side, 4 * side + 4):

            def put(k, y, rows, q=q):
                r = slice(q * co + k * GROUP, q * co + (k + 1) * GROUP)
                cots[r, y * nz : (y + 1) * nz] = rows

            tiles = Tiles(
                co // GROUP,
                lambda k, q=q, side=side: cot[
                    q, k * GROUP : (k + 1) * GROUP, side * (nx - 1)
                ],
            )
            bring_plane(to_y, tiles, ny, nz, put)

    for copy in arriving:
        copy.wait()

    def block(x, y):
        if y == 0:
            return yraw[0, x * ci : (x + 1) * ci]
        if y == ny + 1:
            return yraw[1, x * ci : (x + 1) * ci]
        if x == 0:
            return xraw[0, (y - 1) * ci : y * ci]
        if x == nx + 1:
            return xraw[1, (y - 1) * ci : y * ci]
        return flat[x - 1, :, (y - 1) * nz : y * nz]

    for x in range(nx + 2):
        for y in range(ny + 2):
            lanes = slice(y * nz, (y + 1) * nz)
            plain[x, :, lanes] = block(x, y)
            vm[x, :, lanes] = pltpu.roll(block(x, y).astype(F32), 1, 1).astype(BF16)

    def rolled(x, y):
        return vm[x, :, y * nz : (y + 1) * nz]

    def cot_at(q, m, n):
        r = slice(q * co, (q + 1) * co)
        if is_inner(q, m, nx):
            return cot_edge[m + q // 4 - 1, r]
        return cots[r, n * nz : (n + 1) * nz]

    def put_value(q, m, n, value):
        r = slice(q * co, (q + 1) * co)
        if is_inner(q, m, nx):
            val_edge[m + q // 4 - 1, r] = value
        else:
            vals[r, n * nz : (n + 1) * nz] = value

    spots = foreign_spots(nx, ny)

    def put_foreign(key, tz, value):
        pre[spots[key], tz * co : (tz + 1) * co] = value

    forward_pass(
        dims,
        chunk,
        outer_columns(nx, ny),
        block,
        rolled,
        w,
        cot_at,
        put_value,
        put_foreign,
        ga,
        gb,
    )


def weight_kernel(dims, plain, vm, ga, gb, wg_in, face_lo, face_hi, wg):
    del face_lo, face_hi
    nx, ny, nz, ci, co = dims
    half = 4 * ci

    def wg_add(part, total):
        total = total + wg_in[:, part * half : (part + 1) * half]
        for ex in range(2):
            for row in range(8):
                tx, ty, tz = row // 4, row // 2 % 2, row % 2
                index = ((tx * 2 + ty) * 2 + part) * 2 + tz
                wg[ex * 16 + index] = total[
                    row * co : (row + 1) * co, ex * 2 * ci : (ex + 1) * 2 * ci
                ].astype(BF16)

    weight_pass(
        outer_columns(nx, ny),
        lambda x, y: plain[x, :, y * nz : (y + 1) * nz],
        lambda x, y: vm[x, :, y * nz : (y + 1) * nz],
        ga,
        gb,
        wg_add,
    )


def last_kernel(
    dims,
    chunk,
    ga,
    gb,
    pre,
    vals,
    val_edge,
    xlo_in,
    xhi_in,
    ylo_in,
    yhi_in,
    wt,
    inner_vals,
    ig_in,
    act_out,
    ig_out,
    xraw,
    yraw,
    ig,
    cots,
    staged,
    ig_staged,
    sems,
):
    nx, ny, nz, ci, co = dims
    to_y = swap_matrix(GROUP, ny)
    to_c = swap_matrix(ny, GROUP)
    skip = (nx + 2) * ci
    late = [
        (xlo_in, xraw.at[0]),
        (xhi_in, xraw.at[1]),
        (ylo_in.at[skip:], yraw.at[0]),
        (yhi_in.at[skip:], yraw.at[1]),
    ]
    copies = [pltpu.make_async_copy(src, dst, sems.at[k]) for k, (src, dst) in enumerate(late)]
    for copy in copies:
        copy.start()
    spot = len(copies)
    leaving = []

    for m in range(nx):
        for q in range(8):
            tiles = []
            for k in range(co // GROUP):
                r = slice(q * co + k * GROUP, q * co + (k + 1) * GROUP)
                rows = []
                for y in range(ny):
                    lanes = slice(y * nz, (y + 1) * nz)
                    if not is_inner(q, m, nx):
                        rows.append(vals[r, lanes])
                    elif y == edge_row(q, ny):
                        rows.append(val_edge[m + q // 4 - 1, r])
                    else:
                        rows.append(inner_vals[m + q // 4 - 1, r, lanes])
                tiles.append(jnp.concatenate(rows, axis=0).reshape(ny, GROUP, nz))
            moved = turn(to_c, tiles, nz)
            index = m * 8 + q
            for k in range(co // GROUP):
                staged[index, k * GROUP : (k + 1) * GROUP] = moved[
                    :, k * nz : (k + 1) * nz
                ].reshape(GROUP, ny, nz)
            leaving.append(
                pltpu.make_async_copy(
                    staged.at[index], act_out.at[q, :, m], sems.at[spot + index]
                )
            )
            leaving[-1].start()

    for copy in copies:
        copy.wait()
    for side in range(2):
        for p in range(4):

            def put(k, y, rows, side=side, p=p):
                r = slice(p * co + k * GROUP, p * co + (k + 1) * GROUP)
                cots[side, r, y * nz : (y + 1) * nz] = rows

            tiles = Tiles(
                co // GROUP,
                lambda k, side=side, p=p: xraw[side, p, k * GROUP : (k + 1) * GROUP],
            )
            bring_plane(to_y, tiles, ny, nz, put)

    spots = foreign_spots(nx, ny)
    first = lax.broadcasted_iota(jnp.int32, (co, nz), 1) == 0
    corner = 4 * co * nx

    def foreign(i, j, tx, ty, tz):
        sx, sy, sz = 1 - tx, 1 - ty, 1 - tz
        m, n = i - sx, j - sy
        if 0 <= n < ny:
            side = 0 if m < 0 else 1
            r = (2 * sy + sz) * co
            cot = cots[side, r : r + co, n * nz : (n + 1) * nz]
        else:
            end = 0 if n < 0 else 1
            if 0 <= m < nx:
                r = ((m * 2 + sx) * 2 + sz) * co
            else:
                r = corner + ((0 if m < 0 else 2) + sz) * co
            cot = yraw[end, r : r + co]
        cot = cot.astype(F32)
        if sz == 1:
            cot = pltpu.roll(cot, 1, 1)
        before = pre[spots[i, j, tx, ty], tz * co : (tz + 1) * co]
        sig = 0.5 * jnp.tanh(0.5 * before) + 0.5
        grad = cot * (sig + before * sig * (1.0 - sig))
        whole = grad.astype(BF16)
        cut = jnp.where(first, 0.0, grad).astype(BF16)
        return (whole, cut) if sz == 1 else (cut, whole)

    def cut_grads(c0, some):
        lefts, rights = [], []
        for k, (i, j) in enumerate(some):
            wide = slice((c0 + k) * nz, (c0 + k + 1) * nz)
            left, right = [], []
            for tx in range(2):
                for ty in range(2):
                    base = (2 * tx + ty) * 2 * co
                    if (i, j, tx, ty) in spots:
                        for tz in range(2):
                            one, two = foreign(i, j, tx, ty, tz)
                            left.append(one)
                            right.append(two)
                    else:
                        left.append(ga[base : base + 2 * co, wide])
                        right.append(gb[base : base + 2 * co, wide])
            lefts.append(jnp.concatenate(left, axis=0))
            rights.append(jnp.concatenate(right, axis=0))
        return jnp.concatenate(lefts, axis=1), jnp.concatenate(rights, axis=1)

    def ig_add(m, y, value, fresh):
        lanes = slice(y * nz, (y + 1) * nz)
        ig[m, :, lanes] = (ig_in if fresh else ig)[m, :, lanes] + value

    started = input_pass(dims, chunk, outer_columns(nx, ny), wt, cut_grads, ig_add)
    for m in range(nx):
        for y in range(ny):
            if (m, y) not in started:
                lanes = slice(y * nz, (y + 1) * nz)
                ig[m, :, lanes] = ig_in[m, :, lanes]
    for m in range(nx):
        for k in range(0, ci // GROUP, 2):
            tiles = []
            for h in range(2):
                r = slice((k + h) * GROUP, (k + h + 1) * GROUP)
                rows = [
                    ig[m, r, y * nz : (y + 1) * nz].astype(BF16) for y in range(ny)
                ]
                tiles.append(jnp.concatenate(rows, axis=0).reshape(ny, GROUP, nz))
            moved = turn(to_c, tiles, nz)
            for h in range(2):
                ig_staged[(k + h) * GROUP : (k + h + 1) * GROUP, m] = moved[
                    :, h * nz : (h + 1) * nz
                ].reshape(GROUP, ny, nz)
    leaving.append(pltpu.make_async_copy(ig_staged, ig_out, sems.at[spot + 8 * nx]))
    leaving[-1].start()
    for copy in leaving:
        copy.wait()


def unpack_kernel(co, ci, packed, out):
    for ex in range(2):
        for tx in range(2):
            for ty in range(2):
                for ez in range(2):
                    for tz in range(2):
                        index = (((ex * 2 + tx) * 2 + ty) * 2 + ez) * 2 + tz
                        pair = packed[index].astype(F32)
                        for ey in range(2):
                            out[2 * ex + tx, 2 * ey + ty, 2 * ez + tz] = pair[
                                :, ey * ci : (ey + 1) * ci
                            ]


def held(shape, dtype):
    return pltpu.VMEM(shape, dtype)


def hold(array):
    return pltpu.with_memory_space_constraint(array, pltpu.VMEM)


def neighbours(axis):
    count = lax.axis_size(axis)
    up = [(i, i + 1) for i in range(count - 1)]
    return up, [(b, a) for a, b in up]


def on_device(volume, kernel, cotangent):
    ci, nx, ny, nz = volume.shape
    co = kernel.shape[3]
    gx, gy = lax.axis_size("gx"), lax.axis_size("gy")
    gx_up, gx_down = neighbours("gx")
    gy_up, gy_down = neighbours("gy")
    cells = nx * gx * ny * gy * nz
    dims = (nx, ny, nz, ci, co)

    cot = cotangent.reshape(8, co, nx, ny, nz)

    def corner(sx, sy):
        m, n = (nx - 1) * sx, (ny - 1) * sy
        return cotangent[sx, sy, :, :, m, n].reshape(2 * co, nz)

    def x_message(sx):
        plane = volume[:, (nx - 1) * sx].transpose(1, 0, 2).reshape(ny * ci, nz)
        return jnp.concatenate([plane, corner(sx, 0), corner(sx, 1)], axis=0)

    xlo = lax.ppermute(x_message(1), "gx", gx_up)
    xhi = lax.ppermute(x_message(0), "gx", gx_down)

    vmem = pl.BlockSpec(memory_space=pltpu.VMEM)
    smem = pl.BlockSpec(memory_space=pltpu.SMEM)
    anywhere = pl.BlockSpec(memory_space=pl.ANY)
    params = pltpu.CompilerParams(vmem_limit_bytes=24 * 1024 * 1024)
    n_in = (nx - 1) * (ny - 1)
    n_out = 2 * (ny + 1) + 2 * (nx - 1)
    flat, w, wt, vals, cot_edge, wg_part, ig_part, face_up, face_down = pl.pallas_call(
        functools.partial(inner_kernel, dims, 5),
        out_shape=(
            jax.ShapeDtypeStruct((nx, ci, ny * nz), BF16),
            jax.ShapeDtypeStruct((8 * co, 8 * ci), BF16),
            jax.ShapeDtypeStruct((8 * ci, 8 * co), BF16),
            held((nx - 1, 8 * co, ny * nz), BF16),
            jax.ShapeDtypeStruct((nx - 1, 8 * co, nz), BF16),
            held((8 * co, 8 * ci), F32),
            held((nx, ci, ny * nz), F32),
            jax.ShapeDtypeStruct((4, co, ny, nz), BF16),
            jax.ShapeDtypeStruct((4, co, ny, nz), BF16),
        ),
        in_specs=[anywhere, anywhere, vmem],
        out_specs=(vmem,) * 7 + (anywhere,) * 2,
        scratch_shapes=[
            pltpu.VMEM(volume.shape, BF16),
            pltpu.VMEM(kernel.shape, BF16),
            pltpu.SemaphoreType.DMA((4,)),
            pltpu.VMEM((nx, ci, ny * nz), BF16),
            pltpu.VMEM((8 * co, n_in * nz), BF16),
            pltpu.VMEM((8 * co, n_in * nz), BF16),
            pltpu.VMEM((nx - 1, 8 * co, ny * nz), BF16),
        ],
        compiler_params=params,
    )(volume, kernel, cot)

    def y_message(sy):
        y = (ny - 1) * sy
        rows = slice(y * ci, (y + 1) * ci)
        own = cotangent[:, sy, :, :, :, y].transpose(3, 0, 1, 2, 4).reshape(4 * co * nx, nz)
        corner = slice((ny * ci + sy * 2 * co), (ny * ci + (sy + 1) * 2 * co))
        return jnp.concatenate(
            [
                xlo[rows],
                flat[:, :, y * nz : (y + 1) * nz].reshape(nx * ci, nz),
                xhi[rows],
                own,
                xlo[corner],
                xhi[corner],
            ],
            axis=0,
        )

    ylo = lax.ppermute(y_message(1), "gy", gy_up)
    yhi = lax.ppermute(y_message(0), "gy", gy_down)
    face_lo = lax.ppermute(face_up, "gx", gx_up)
    face_hi = lax.ppermute(face_down, "gx", gx_down)
    foreign = len(foreign_spots(nx, ny))
    *passed, plain, vm = pl.pallas_call(
        functools.partial(outer_kernel, dims, 4),
        out_shape=(
            held((8 * co, n_out * nz), BF16),
            held((8 * co, n_out * nz), BF16),
            held((foreign, 2 * co, nz), F32),
            held((8 * co, ny * nz), BF16),
            held((nx - 1, 8 * co, nz), BF16),
            held((nx + 2, ci, (ny + 2) * nz), BF16),
            held((nx + 2, ci, (ny + 2) * nz), BF16),
        ),
        in_specs=[vmem] + [anywhere] * 4 + [vmem] * 3,
        out_specs=(vmem,) * 7,
        scratch_shapes=[
            pltpu.VMEM((2, ny * ci, nz), BF16),
            pltpu.VMEM((2, (nx + 2) * ci, nz), BF16),
            pltpu.VMEM((8 * co, ny * nz), BF16),
            pltpu.SemaphoreType.DMA((4,)),
        ],
        compiler_params=params,
    )(flat, xlo, xhi, ylo, yhi, w, cot, cot_edge)
    passed = [hold(p) for p in passed]
    wg = pl.pallas_call(
        functools.partial(weight_kernel, dims),
        out_shape=jax.ShapeDtypeStruct((32, co, 2 * ci), BF16),
        in_specs=[vmem] * 5 + [anywhere] * 2,
        out_specs=vmem,
        compiler_params=params,
    )(hold(plain), hold(vm), passed[0], passed[1], hold(wg_part), face_lo, face_hi)
    act, input_grad = pl.pallas_call(
        functools.partial(last_kernel, dims, 4),
        out_shape=(
            jax.ShapeDtypeStruct(cot.shape, BF16),
            jax.ShapeDtypeStruct(volume.shape, BF16),
        ),
        in_specs=[vmem] * 5 + [anywhere] * 4 + [vmem] * 3,
        out_specs=(anywhere,) * 2,
        scratch_shapes=[
            pltpu.VMEM((2, 4, co, ny, nz), BF16),
            pltpu.VMEM((2, 4 * co * nx + 4 * co, nz), BF16),
            pltpu.VMEM((nx, ci, ny * nz), F32),
            pltpu.VMEM((2, 4 * co, ny * nz), BF16),
            pltpu.VMEM((8 * nx, co, ny, nz), BF16),
            pltpu.VMEM(volume.shape, BF16),
            pltpu.SemaphoreType.DMA((5 + 8 * nx,)),
        ],
        compiler_params=params,
    )(*passed, face_lo, face_hi, ylo, yhi, wt, hold(vals), hold(ig_part))

    scale = 1.0 / math.sqrt(cells)
    devices = gx * gy
    shares = wg.reshape(devices, 32 * co // devices, 2 * ci)
    shares = lax.all_to_all(shares, ("gx", "gy"), 0, 0, tiled=True)
    piece = (jnp.sum(shares.astype(F32), axis=0) * scale).astype(BF16)
    pieces = jnp.broadcast_to(piece[None], (devices,) + piece.shape)
    pieces = lax.all_to_all(pieces, ("gx", "gy"), 0, 0, tiled=True)
    weight_grad = pl.pallas_call(
        functools.partial(unpack_kernel, co, ci),
        out_shape=jax.ShapeDtypeStruct((4, 4, 4, co, ci), F32),
        in_specs=[vmem],
        out_specs=vmem,
        compiler_params=pltpu.CompilerParams(vmem_limit_bytes=8 * 1024 * 1024),
    )(pieces.reshape(32, co, 2 * ci))

    return act.reshape(cotangent.shape), input_grad, weight_grad


def solution(mesh):
    placed = (P(None, "gx", "gy", None), P(), P(None, None, None, None, "gx", "gy", None))
    return jax.shard_map(
        on_device,
        mesh=mesh,
        in_specs=placed,
        out_specs=(placed[2], placed[0], P()),
        check_vma=False,
    )
```

```python
import functools
import math

import jax
import jax.numpy as jnp
from jax import lax
from jax.experimental import pallas as pl
from jax.experimental.pallas import tpu as pltpu
from jax.sharding import PartitionSpec as P

F32 = jnp.float32
BF16 = jnp.bfloat16
GROUP = 16


def swap_matrix(outer, inner):
    size = outer * inner
    row = lax.broadcasted_iota(jnp.int32, (size, size), 0)
    col = lax.broadcasted_iota(jnp.int32, (size, size), 1)
    return jnp.where(col == (row % outer) * inner + row // outer, 1.0, 0.0).astype(BF16)


def turn(matrix, pieces, nz):
    flat = [p.reshape(p.shape[0] * p.shape[1], nz) for p in pieces]
    moved = jnp.dot(matrix, jnp.concatenate(flat, axis=1), preferred_element_type=F32)
    return moved.astype(BF16)


def bring_plane(to_y, raw, ny, nz, put):
    for k in range(0, raw.count, 2):
        moved = turn(to_y, [raw(k), raw(k + 1)], nz)
        for y in range(ny):
            rows = slice(y * GROUP, (y + 1) * GROUP)
            put(k, y, moved[rows, :nz])
            put(k + 1, y, moved[rows, nz:])


class Tiles:
    def __init__(self, count, get):
        self.count, self.get = count, get

    def __call__(self, k):
        return self.get(k)


def corners(get, some):
    return jnp.concatenate(
        [
            jnp.concatenate([get(i + 1 - ex, j + 1 - ey) for i, j in some], axis=1)
            for ex in range(2)
            for ey in range(2)
        ],
        axis=0,
    )


def forward_pass(dims, chunk, columns, block, rolled, w, cot_at, put_value, put_foreign, ga, gb, base_column=0):
    nx, ny, nz, ci, co = dims
    half = 4 * ci
    first = lax.broadcasted_iota(jnp.int32, (co, nz), 1) == 0
    zeros = jnp.zeros((2 * co, nz), BF16)

    starts = range(0, len(columns), chunk)
    for c0 in starts:
        some = columns[c0 : c0 + chunk]
        back = jnp.dot(w[:, half:], corners(rolled, some), preferred_element_type=F32)
        here = jnp.dot(w[:, :half], corners(block, some), preferred_element_type=F32)
        for k, (i, j) in enumerate(some):
            cols = slice(k * nz, (k + 1) * nz)
            at = base_column + c0 + k
            wide = slice(at * nz, (at + 1) * nz)
            for tx in range(2):
                for ty in range(2):
                    sx, sy = 1 - tx, 1 - ty
                    m, n = i - sx, j - sy
                    base = (2 * tx + ty) * 2 * co
                    if not (0 <= m < nx and 0 <= n < ny):
                        ga[base : base + 2 * co, wide] = zeros
                        gb[base : base + 2 * co, wide] = zeros
                        r = slice(base, base + co)
                        put_foreign(
                            (i, j, tx, ty), 0, back[r, cols] + jnp.where(first, 0.0, here[r, cols])
                        )
                        r = slice(base + co, base + 2 * co)
                        put_foreign(
                            (i, j, tx, ty), 1, jnp.where(first, 0.0, back[r, cols]) + here[r, cols]
                        )
                        continue
                    for tz in range(2):
                        sz = 1 - tz
                        r = slice(base + tz * co, base + (tz + 1) * co)
                        low, high = back[r, cols], here[r, cols]
                        if sz == 1:
                            before = low + jnp.where(first, 0.0, high)
                            before = pltpu.roll(before, nz - 1, 1)
                        else:
                            before = jnp.where(first, 0.0, low) + high
                        q = (2 * sx + sy) * 2 + sz
                        sig = 0.5 * jnp.tanh(0.5 * before) + 0.5
                        value = before * sig
                        put_value(q, m, n, value.astype(BF16))
                        slope = sig + value * (1.0 - sig)
                        grad = cot_at(q, m, n).astype(F32) * slope
                        if sz == 1:
                            grad = pltpu.roll(grad, 1, 1)
                        whole = grad.astype(BF16)
                        cut = jnp.where(first, 0.0, grad).astype(BF16)
                        ga[r, wide] = cut if sz == 0 else whole
                        gb[r, wide] = cut if sz == 1 else whole


def weight_pass(columns, block, rolled, ga, gb, wg_add):
    nt = (((1,), (1,)), ((), ()))
    for part, (grads, get) in enumerate(((gb, block), (ga, rolled))):
        wg_add(
            part,
            lax.dot_general(grads[...], corners(get, columns), nt, preferred_element_type=F32),
        )


def input_pass(dims, chunk, columns, wt, cut_grads, ig_add):
    nx, ny, nz, ci, co = dims
    half = 4 * ci
    started = set()
    for c0 in range(0, len(columns), chunk):
        some = columns[c0 : c0 + chunk]
        left, right = cut_grads(c0, some)
        back = jnp.dot(wt[half:], left, preferred_element_type=F32)
        here = jnp.dot(wt[:half], right, preferred_element_type=F32)
        for k, (i, j) in enumerate(some):
            cols = slice(k * nz, (k + 1) * nz)
            both = here[:, cols] + pltpu.roll(back[:, cols], nz - 1, 1)
            for ex in range(2):
                for ey in range(2):
                    m, y = i - ex, j - ey
                    if 0 <= m < nx and 0 <= y < ny:
                        r = (2 * ex + ey) * ci
                        ig_add(m, y, both[r : r + ci], (m, y) not in started)
                        started.add((m, y))
    return started


def outer_columns(nx, ny):
    columns = [(i, j) for i in (0, nx) for j in range(ny + 1)]
    return columns + [(i, j) for i in range(1, nx) for j in (0, ny)]


def foreign_spots(nx, ny):
    spots = {}
    for i, j in outer_columns(nx, ny):
        for tx in range(2):
            for ty in range(2):
                m, n = i - 1 + tx, j - 1 + ty
                if not (0 <= m < nx and 0 <= n < ny):
                    spots[i, j, tx, ty] = len(spots)
    return spots


def is_inner(q, m, nx):
    return 1 <= m + q // 4 < nx


def edge_row(q, ny):
    return (ny - 1) if q // 2 % 2 else 0


def inner_kernel(
    dims,
    chunk,
    vol_in,
    taps_in,
    cot,
    flat,
    w,
    wt_out,
    vals_out,
    cot_edge,
    wg,
    ig_out,
    face_up,
    face_down,
    wt,
    vals,
    ig,
    vol,
    taps,
    sems,
    vm,
    ga,
    gb,
    cots,
):
    nx, ny, nz, ci, co = dims
    half = 4 * ci
    to_y = swap_matrix(GROUP, ny)
    arriving = [
        pltpu.make_async_copy(vol_in, vol, sems.at[0]),
        pltpu.make_async_copy(taps_in, taps, sems.at[1]),
    ]
    leaving = [
        pltpu.make_async_copy(cot.at[4:, :, nx - 1], face_up, sems.at[2]),
        pltpu.make_async_copy(cot.at[:4, :, 0], face_down, sems.at[3]),
    ]
    for copy in arriving + leaving:
        copy.start()

    for i in range(1, nx):
        for q in range(8):
            m = i - q // 4

            def put(k, y, rows, i=i, q=q):
                r = slice(q * co + k * GROUP, q * co + (k + 1) * GROUP)
                cots[i - 1, r, y * nz : (y + 1) * nz] = rows
                if y == edge_row(q, ny):
                    cot_edge[i - 1, r] = rows

            tiles = Tiles(
                co // GROUP, lambda k, q=q, m=m: cot[q, k * GROUP : (k + 1) * GROUP, m]
            )
            bring_plane(to_y, tiles, ny, nz, put)

    for copy in arriving:
        copy.wait()
    for tx in range(2):
        for ty in range(2):
            for tz in range(2):
                r = ((2 * tx + ty) * 2 + tz) * co
                for ez in range(2):
                    for ex in range(2):
                        pair = [taps[2 * ex + tx, 2 * ey + ty, 2 * ez + tz] for ey in range(2)]
                        c = (2 * ez + ex) * 2 * ci
                        w[r : r + co, c : c + 2 * ci] = jnp.concatenate(pair, axis=1)
    wt[...] = w[...].T
    leaving.append(pltpu.make_async_copy(wt, wt_out, sems.at[4]))
    leaving[-1].start()

    for x in range(nx):

        def put(k, y, rows, x=x):
            r = slice(k * GROUP, (k + 1) * GROUP)
            lanes = slice(y * nz, (y + 1) * nz)
            flat[x, r, lanes] = rows
            vm[x, r, lanes] = pltpu.roll(rows.astype(F32), 1, 1).astype(BF16)

        tiles = Tiles(
            ci // GROUP, lambda k, x=x: vol[k * GROUP : (k + 1) * GROUP, x]
        )
        bring_plane(to_y, tiles, ny, nz, put)

    def block(x, y):
        return flat[x - 1, :, (y - 1) * nz : y * nz]

    def rolled(x, y):
        return vm[x - 1, :, (y - 1) * nz : y * nz]

    def cot_at(q, m, n):
        return cots[m + q // 4 - 1, q * co : (q + 1) * co, n * nz : (n + 1) * nz]

    def put_value(q, m, n, value):
        vals[m + q // 4 - 1, q * co : (q + 1) * co, n * nz : (n + 1) * nz] = value

    def wg_add(part, total):
        wg[:, part * half : (part + 1) * half] = total

    def ig_add(m, y, value, fresh):
        lanes = slice(y * nz, (y + 1) * nz)
        ig[m, :, lanes] = value if fresh else ig[m, :, lanes] + value

    def cut_grads(c0, some):
        wide = slice(c0 * nz, (c0 + len(some)) * nz)
        return ga[:, wide], gb[:, wide]

    columns = [(i, j) for i in range(1, nx) for j in range(1, ny)]
    forward_pass(dims, chunk, columns, block, rolled, w, cot_at, put_value, None, ga, gb)
    leaving.append(pltpu.make_async_copy(vals, vals_out, sems.at[5]))
    leaving[-1].start()
    input_pass(dims, chunk, columns, wt, cut_grads, ig_add)
    leaving.append(pltpu.make_async_copy(ig, ig_out, sems.at[6]))
    leaving[-1].start()
    weight_pass(columns, block, rolled, ga, gb, wg_add)
    for copy in leaving:
        copy.wait()


def outer_kernel(
    dims,
    chunk,
    flat,
    xlo_in,
    xhi_in,
    ylo_in,
    yhi_in,
    w,
    cot,
    cot_edge,
    pre_out,
    vals_out,
    val_edge_out,
    ga,
    gb,
    plain,
    vm,
    pre,
    vals,
    val_edge,
    xraw,
    yraw,
    cots,
    sems,
):
    nx, ny, nz, ci, co = dims
    to_y = swap_matrix(GROUP, ny)
    arriving = [
        pltpu.make_async_copy(xlo_in.at[: ny * ci], xraw.at[0], sems.at[0]),
        pltpu.make_async_copy(xhi_in.at[: ny * ci], xraw.at[1], sems.at[1]),
        pltpu.make_async_copy(ylo_in.at[: (nx + 2) * ci], yraw.at[0], sems.at[2]),
        pltpu.make_async_copy(yhi_in.at[: (nx + 2) * ci], yraw.at[1], sems.at[3]),
    ]
    for copy in arriving:
        copy.start()

    for side in range(2):
        for q in range(4 * side, 4 * side + 4):

            def put(k, y, rows, q=q):
                r = slice(q * co + k * GROUP, q * co + (k + 1) * GROUP)
                cots[r, y * nz : (y + 1) * nz] = rows

            tiles = Tiles(
                co // GROUP,
                lambda k, q=q, side=side: cot[
                    q, k * GROUP : (k + 1) * GROUP, side * (nx - 1)
                ],
            )
            bring_plane(to_y, tiles, ny, nz, put)

    for copy in arriving:
        copy.wait()

    def block(x, y):
        if y == 0:
            return yraw[0, x * ci : (x + 1) * ci]
        if y == ny + 1:
            return yraw[1, x * ci : (x + 1) * ci]
        if x == 0:
            return xraw[0, (y - 1) * ci : y * ci]
        if x == nx + 1:
            return xraw[1, (y - 1) * ci : y * ci]
        return flat[x - 1, :, (y - 1) * nz : y * nz]

    for x in range(nx + 2):
        for y in range(ny + 2):
            lanes = slice(y * nz, (y + 1) * nz)
            plain[x, :, lanes] = block(x, y)
            vm[x, :, lanes] = pltpu.roll(block(x, y).astype(F32), 1, 1).astype(BF16)

    def rolled(x, y):
        return vm[x, :, y * nz : (y + 1) * nz]

    def cot_at(q, m, n):
        r = slice(q * co, (q + 1) * co)
        if is_inner(q, m, nx):
            return cot_edge[m + q // 4 - 1, r]
        return cots[r, n * nz : (n + 1) * nz]

    def put_value(q, m, n, value):
        r = slice(q * co, (q + 1) * co)
        if is_inner(q, m, nx):
            val_edge[m + q // 4 - 1, r] = value
        else:
            vals[r, n * nz : (n + 1) * nz] = value

    spots = foreign_spots(nx, ny)

    def put_foreign(key, tz, value):
        pre[spots[key], tz * co : (tz + 1) * co] = value

    leaving = []

    def leave(src, dst):
        leaving.append(pltpu.make_async_copy(src, dst, sems.at[4 + len(leaving)]))
        leaving[-1].start()

    columns = outer_columns(nx, ny)
    sent = 0
    for k, i in enumerate((0, nx, None)):
        c0 = k * (ny + 1)
        some = columns[c0 : c0 + ny + 1] if k < 2 else columns[c0:]
        forward_pass(
            dims, chunk, some, block, rolled, w, cot_at, put_value, put_foreign, ga, gb, c0
        )
        upto = sent + sum(spot[:2] in some for spot in spots)
        leave(pre.at[sent:upto], pre_out.at[sent:upto])
        sent = upto
        if k < 2:
            rows = pl.ds(4 * k * co, 4 * co)
            leave(vals.at[rows], vals_out.at[rows])
        else:
            leave(val_edge, val_edge_out)
    for copy in leaving:
        copy.wait()


def weight_kernel(
    dims, plain, vm, ga, gb, wg_in, face_lo, face_hi, wg, ga_out, gb_out, sems
):
    del face_lo, face_hi
    leaving = [
        pltpu.make_async_copy(ga, ga_out, sems.at[0]),
        pltpu.make_async_copy(gb, gb_out, sems.at[1]),
    ]
    for copy in leaving:
        copy.start()
    nx, ny, nz, ci, co = dims
    half = 4 * ci

    def wg_add(part, total):
        total = total + wg_in[:, part * half : (part + 1) * half]
        for ex in range(2):
            for row in range(8):
                tx, ty, tz = row // 4, row // 2 % 2, row % 2
                index = ((tx * 2 + ty) * 2 + part) * 2 + tz
                wg[ex * 16 + index] = total[
                    row * co : (row + 1) * co, ex * 2 * ci : (ex + 1) * 2 * ci
                ].astype(BF16)

    weight_pass(
        outer_columns(nx, ny),
        lambda x, y: plain[x, :, y * nz : (y + 1) * nz],
        lambda x, y: vm[x, :, y * nz : (y + 1) * nz],
        ga,
        gb,
        wg_add,
    )
    for copy in leaving:
        copy.wait()


def last_kernel(
    dims,
    chunk,
    ga_in,
    gb_in,
    pre_in,
    vals_in,
    val_edge_in,
    xlo_in,
    xhi_in,
    ylo_in,
    yhi_in,
    wt_in,
    inner_vals_in,
    ig_in,
    act_out,
    ig_out,
    ga,
    gb,
    pre,
    vals,
    val_edge,
    xraw,
    yraw,
    wt,
    inner_vals,
    ig,
    cots,
    staged,
    ig_staged,
    sems,
):
    nx, ny, nz, ci, co = dims
    to_y = swap_matrix(GROUP, ny)
    to_c = swap_matrix(ny, GROUP)
    skip = (nx + 2) * ci
    early = [(vals_in, vals), (val_edge_in, val_edge), (inner_vals_in, inner_vals)]
    late = [
        (xlo_in, xraw.at[0]),
        (xhi_in, xraw.at[1]),
        (ylo_in.at[skip:], yraw.at[0]),
        (yhi_in.at[skip:], yraw.at[1]),
        (ga_in, ga),
        (gb_in, gb),
        (pre_in, pre),
        (wt_in, wt),
        (ig_in, ig),
    ]
    copies = [
        pltpu.make_async_copy(src, dst, sems.at[k]) for k, (src, dst) in enumerate(early + late)
    ]
    for copy in copies:
        copy.start()
    spot = len(copies)
    for copy in copies[: len(early)]:
        copy.wait()
    leaving = []

    for m in range(nx):
        for q in range(8):
            tiles = []
            for k in range(co // GROUP):
                r = slice(q * co + k * GROUP, q * co + (k + 1) * GROUP)
                rows = []
                for y in range(ny):
                    lanes = slice(y * nz, (y + 1) * nz)
                    if not is_inner(q, m, nx):
                        rows.append(vals[r, lanes])
                    elif y == edge_row(q, ny):
                        rows.append(val_edge[m + q // 4 - 1, r])
                    else:
                        rows.append(inner_vals[m + q // 4 - 1, r, lanes])
                tiles.append(jnp.concatenate(rows, axis=0).reshape(ny, GROUP, nz))
            moved = turn(to_c, tiles, nz)
            index = m * 8 + q
            for k in range(co // GROUP):
                staged[index, k * GROUP : (k + 1) * GROUP] = moved[
                    :, k * nz : (k + 1) * nz
                ].reshape(GROUP, ny, nz)
            leaving.append(
                pltpu.make_async_copy(
                    staged.at[index], act_out.at[q, :, m], sems.at[spot + index]
                )
            )
            leaving[-1].start()

    for copy in copies[len(early) :]:
        copy.wait()
    for side in range(2):
        for p in range(4):

            def put(k, y, rows, side=side, p=p):
                r = slice(p * co + k * GROUP, p * co + (k + 1) * GROUP)
                cots[side, r, y * nz : (y + 1) * nz] = rows

            tiles = Tiles(
                co // GROUP,
                lambda k, side=side, p=p: xraw[side, p, k * GROUP : (k + 1) * GROUP],
            )
            bring_plane(to_y, tiles, ny, nz, put)

    spots = foreign_spots(nx, ny)
    first = lax.broadcasted_iota(jnp.int32, (co, nz), 1) == 0
    corner = 4 * co * nx

    def foreign(i, j, tx, ty, tz):
        sx, sy, sz = 1 - tx, 1 - ty, 1 - tz
        m, n = i - sx, j - sy
        if 0 <= n < ny:
            side = 0 if m < 0 else 1
            r = (2 * sy + sz) * co
            cot = cots[side, r : r + co, n * nz : (n + 1) * nz]
        else:
            end = 0 if n < 0 else 1
            if 0 <= m < nx:
                r = ((m * 2 + sx) * 2 + sz) * co
            else:
                r = corner + ((0 if m < 0 else 2) + sz) * co
            cot = yraw[end, r : r + co]
        cot = cot.astype(F32)
        if sz == 1:
            cot = pltpu.roll(cot, 1, 1)
        before = pre[spots[i, j, tx, ty], tz * co : (tz + 1) * co]
        sig = 0.5 * jnp.tanh(0.5 * before) + 0.5
        grad = cot * (sig + before * sig * (1.0 - sig))
        whole = grad.astype(BF16)
        cut = jnp.where(first, 0.0, grad).astype(BF16)
        return (whole, cut) if sz == 1 else (cut, whole)

    def cut_grads(c0, some):
        lefts, rights = [], []
        for k, (i, j) in enumerate(some):
            wide = slice((c0 + k) * nz, (c0 + k + 1) * nz)
            left, right = [], []
            for tx in range(2):
                for ty in range(2):
                    base = (2 * tx + ty) * 2 * co
                    if (i, j, tx, ty) in spots:
                        for tz in range(2):
                            one, two = foreign(i, j, tx, ty, tz)
                            left.append(one)
                            right.append(two)
                    else:
                        left.append(ga[base : base + 2 * co, wide])
                        right.append(gb[base : base + 2 * co, wide])
            lefts.append(jnp.concatenate(left, axis=0))
            rights.append(jnp.concatenate(right, axis=0))
        return jnp.concatenate(lefts, axis=1), jnp.concatenate(rights, axis=1)

    def ig_add(m, y, value, fresh):
        lanes = slice(y * nz, (y + 1) * nz)
        ig[m, :, lanes] = ig[m, :, lanes] + value

    input_pass(dims, chunk, outer_columns(nx, ny), wt, cut_grads, ig_add)
    for m in range(nx):
        for k in range(0, ci // GROUP, 2):
            tiles = []
            for h in range(2):
                r = slice((k + h) * GROUP, (k + h + 1) * GROUP)
                rows = [
                    ig[m, r, y * nz : (y + 1) * nz].astype(BF16) for y in range(ny)
                ]
                tiles.append(jnp.concatenate(rows, axis=0).reshape(ny, GROUP, nz))
            moved = turn(to_c, tiles, nz)
            for h in range(2):
                ig_staged[(k + h) * GROUP : (k + h + 1) * GROUP, m] = moved[
                    :, h * nz : (h + 1) * nz
                ].reshape(GROUP, ny, nz)
    leaving.append(pltpu.make_async_copy(ig_staged, ig_out, sems.at[spot + 8 * nx]))
    leaving[-1].start()
    for copy in leaving:
        copy.wait()


def unpack_kernel(co, ci, packed, out):
    for ex in range(2):
        for tx in range(2):
            for ty in range(2):
                for ez in range(2):
                    for tz in range(2):
                        index = (((ex * 2 + tx) * 2 + ty) * 2 + ez) * 2 + tz
                        pair = packed[index].astype(F32)
                        for ey in range(2):
                            out[2 * ex + tx, 2 * ey + ty, 2 * ez + tz] = pair[
                                :, ey * ci : (ey + 1) * ci
                            ]


def far(shape, dtype):
    return pltpu.HBM(shape, dtype)


def stay(array):
    return pltpu.with_memory_space_constraint(array, pltpu.HBM)


def neighbours(axis):
    count = lax.axis_size(axis)
    up = [(i, i + 1) for i in range(count - 1)]
    return up, [(b, a) for a, b in up]


def on_device(volume, kernel, cotangent):
    ci, nx, ny, nz = volume.shape
    co = kernel.shape[3]
    gx, gy = lax.axis_size("gx"), lax.axis_size("gy")
    gx_up, gx_down = neighbours("gx")
    gy_up, gy_down = neighbours("gy")
    cells = nx * gx * ny * gy * nz
    dims = (nx, ny, nz, ci, co)

    cot = cotangent.reshape(8, co, nx, ny, nz)

    def corner(sx, sy):
        m, n = (nx - 1) * sx, (ny - 1) * sy
        return cotangent[sx, sy, :, :, m, n].reshape(2 * co, nz)

    def x_message(sx):
        plane = volume[:, (nx - 1) * sx].transpose(1, 0, 2).reshape(ny * ci, nz)
        return jnp.concatenate([plane, corner(sx, 0), corner(sx, 1)], axis=0)

    xlo = lax.ppermute(x_message(1), "gx", gx_up)
    xhi = lax.ppermute(x_message(0), "gx", gx_down)

    vmem = pl.BlockSpec(memory_space=pltpu.VMEM)
    smem = pl.BlockSpec(memory_space=pltpu.SMEM)
    anywhere = pl.BlockSpec(memory_space=pl.ANY)
    hbm = pl.BlockSpec(memory_space=pltpu.HBM)
    params = pltpu.CompilerParams(vmem_limit_bytes=24 * 1024 * 1024)
    n_in = (nx - 1) * (ny - 1)
    n_out = 2 * (ny + 1) + 2 * (nx - 1)
    flat, w, wt, inner_vals, cot_edge, wg_part, ig_part, face_up, face_down = pl.pallas_call(
        functools.partial(inner_kernel, dims, 5),
        out_shape=(
            jax.ShapeDtypeStruct((nx, ci, ny * nz), BF16),
            jax.ShapeDtypeStruct((8 * co, 8 * ci), BF16),
            far((8 * ci, 8 * co), BF16),
            far((nx - 1, 8 * co, ny * nz), BF16),
            jax.ShapeDtypeStruct((nx - 1, 8 * co, nz), BF16),
            jax.ShapeDtypeStruct((8 * co, 8 * ci), F32),
            far((nx, ci, ny * nz), F32),
            far((4, co, ny, nz), BF16),
            far((4, co, ny, nz), BF16),
        ),
        in_specs=[anywhere, anywhere, vmem],
        out_specs=(vmem, vmem, hbm, hbm, vmem, vmem, hbm, hbm, hbm),
        scratch_shapes=[
            pltpu.VMEM((8 * ci, 8 * co), BF16),
            pltpu.VMEM((nx - 1, 8 * co, ny * nz), BF16),
            pltpu.VMEM((nx, ci, ny * nz), F32),
            pltpu.VMEM(volume.shape, BF16),
            pltpu.VMEM(kernel.shape, BF16),
            pltpu.SemaphoreType.DMA((7,)),
            pltpu.VMEM((nx, ci, ny * nz), BF16),
            pltpu.VMEM((8 * co, n_in * nz), BF16),
            pltpu.VMEM((8 * co, n_in * nz), BF16),
            pltpu.VMEM((nx - 1, 8 * co, ny * nz), BF16),
        ],
        compiler_params=params,
    )(volume, kernel, cot)

    def y_message(sy):
        y = (ny - 1) * sy
        rows = slice(y * ci, (y + 1) * ci)
        own = cotangent[:, sy, :, :, :, y].transpose(3, 0, 1, 2, 4).reshape(4 * co * nx, nz)
        corner = slice((ny * ci + sy * 2 * co), (ny * ci + (sy + 1) * 2 * co))
        return jnp.concatenate(
            [
                xlo[rows],
                flat[:, :, y * nz : (y + 1) * nz].reshape(nx * ci, nz),
                xhi[rows],
                own,
                xlo[corner],
                xhi[corner],
            ],
            axis=0,
        )

    ylo = lax.ppermute(y_message(1), "gy", gy_up)
    yhi = lax.ppermute(y_message(0), "gy", gy_down)
    face_lo = lax.ppermute(face_up, "gx", gx_up)
    face_hi = lax.ppermute(face_down, "gx", gx_down)
    foreign = len(foreign_spots(nx, ny))
    pre_shape = (foreign, 2 * co, nz)
    pre, vals, val_edge, ga, gb, plain, vm = pl.pallas_call(
        functools.partial(outer_kernel, dims, 4),
        out_shape=(
            far(pre_shape, F32),
            far((8 * co, ny * nz), BF16),
            far((nx - 1, 8 * co, nz), BF16),
            jax.ShapeDtypeStruct((8 * co, n_out * nz), BF16),
            jax.ShapeDtypeStruct((8 * co, n_out * nz), BF16),
            jax.ShapeDtypeStruct((nx + 2, ci, (ny + 2) * nz), BF16),
            jax.ShapeDtypeStruct((nx + 2, ci, (ny + 2) * nz), BF16),
        ),
        in_specs=[vmem] + [anywhere] * 4 + [vmem] * 3,
        out_specs=(hbm,) * 3 + (vmem,) * 4,
        scratch_shapes=[
            pltpu.VMEM(pre_shape, F32),
            pltpu.VMEM((8 * co, ny * nz), BF16),
            pltpu.VMEM((nx - 1, 8 * co, nz), BF16),
            pltpu.VMEM((2, ny * ci, nz), BF16),
            pltpu.VMEM((2, (nx + 2) * ci, nz), BF16),
            pltpu.VMEM((8 * co, ny * nz), BF16),
            pltpu.SemaphoreType.DMA((10,)),
        ],
        compiler_params=params,
    )(flat, xlo, xhi, ylo, yhi, w, cot, cot_edge)
    wg, ga, gb = pl.pallas_call(
        functools.partial(weight_kernel, dims),
        out_shape=(
            jax.ShapeDtypeStruct((32, co, 2 * ci), BF16),
            far((8 * co, n_out * nz), BF16),
            far((8 * co, n_out * nz), BF16),
        ),
        in_specs=[vmem] * 5 + [anywhere] * 2,
        out_specs=(vmem, hbm, hbm),
        scratch_shapes=[pltpu.SemaphoreType.DMA((2,))],
        compiler_params=params,
    )(plain, vm, ga, gb, wg_part, face_lo, face_hi)
    passed = [
        stay(array)
        for array in (ga, gb, pre, vals, val_edge, face_lo, face_hi, ylo, yhi, wt, inner_vals, ig_part)
    ]
    act, input_grad = pl.pallas_call(
        functools.partial(last_kernel, dims, 4),
        out_shape=(
            jax.ShapeDtypeStruct(cot.shape, BF16),
            jax.ShapeDtypeStruct(volume.shape, BF16),
        ),
        in_specs=[hbm] * 12,
        out_specs=(anywhere,) * 2,
        scratch_shapes=[
            pltpu.VMEM((8 * co, n_out * nz), BF16),
            pltpu.VMEM((8 * co, n_out * nz), BF16),
            pltpu.VMEM(pre_shape, F32),
            pltpu.VMEM((8 * co, ny * nz), BF16),
            pltpu.VMEM((nx - 1, 8 * co, nz), BF16),
            pltpu.VMEM((2, 4, co, ny, nz), BF16),
            pltpu.VMEM((2, 4 * co * nx + 4 * co, nz), BF16),
            pltpu.VMEM((8 * ci, 8 * co), BF16),
            pltpu.VMEM((nx - 1, 8 * co, ny * nz), BF16),
            pltpu.VMEM((nx, ci, ny * nz), F32),
            pltpu.VMEM((2, 4 * co, ny * nz), BF16),
            pltpu.VMEM((8 * nx, co, ny, nz), BF16),
            pltpu.VMEM(volume.shape, BF16),
            pltpu.SemaphoreType.DMA((13 + 8 * nx,)),
        ],
        compiler_params=params,
    )(*passed)

    scale = 1.0 / math.sqrt(cells)
    devices = gx * gy
    shares = wg.reshape(devices, 32 * co // devices, 2 * ci)
    shares = lax.all_to_all(shares, ("gx", "gy"), 0, 0, tiled=True)
    piece = (jnp.sum(shares.astype(F32), axis=0) * scale).astype(BF16)
    pieces = jnp.broadcast_to(piece[None], (devices,) + piece.shape)
    pieces = lax.all_to_all(pieces, ("gx", "gy"), 0, 0, tiled=True)
    weight_grad = pl.pallas_call(
        functools.partial(unpack_kernel, co, ci),
        out_shape=jax.ShapeDtypeStruct((4, 4, 4, co, ci), F32),
        in_specs=[vmem],
        out_specs=vmem,
        compiler_params=pltpu.CompilerParams(vmem_limit_bytes=8 * 1024 * 1024),
    )(pieces.reshape(32, co, 2 * ci))

    return act.reshape(cotangent.shape), input_grad, weight_grad


def solution(mesh):
    placed = (P(None, "gx", "gy", None), P(), P(None, None, None, None, "gx", "gy", None))
    return jax.shard_map(
        on_device,
        mesh=mesh,
        in_specs=placed,
        out_specs=(placed[2], placed[0], P()),
        check_vma=False,
    )
```

```python
import functools
import math

import jax
import jax.numpy as jnp
from jax import lax
from jax.experimental import pallas as pl
from jax.experimental.pallas import tpu as pltpu
from jax.sharding import PartitionSpec as P

F32 = jnp.float32
BF16 = jnp.bfloat16
GROUP = 16


def swap_matrix(outer, inner):
    size = outer * inner
    row = lax.broadcasted_iota(jnp.int32, (size, size), 0)
    col = lax.broadcasted_iota(jnp.int32, (size, size), 1)
    return jnp.where(col == (row % outer) * inner + row // outer, 1.0, 0.0).astype(BF16)


def turn(matrix, pieces, nz):
    flat = [p.reshape(p.shape[0] * p.shape[1], nz) for p in pieces]
    moved = jnp.dot(matrix, jnp.concatenate(flat, axis=1), preferred_element_type=F32)
    return moved.astype(BF16)


def bring_plane(to_y, raw, ny, nz, put):
    for k in range(0, raw.count, 2):
        moved = turn(to_y, [raw(k), raw(k + 1)], nz)
        for y in range(ny):
            rows = slice(y * GROUP, (y + 1) * GROUP)
            put(k, y, moved[rows, :nz])
            put(k + 1, y, moved[rows, nz:])


class Tiles:
    def __init__(self, count, get):
        self.count, self.get = count, get

    def __call__(self, k):
        return self.get(k)


def corners(get, some):
    return jnp.concatenate(
        [
            jnp.concatenate([get(i + 1 - ex, j + 1 - ey) for i, j in some], axis=1)
            for ex in range(2)
            for ey in range(2)
        ],
        axis=0,
    )


def forward_pass(dims, chunk, columns, block, rolled, w, cot_at, put_value, put_foreign, ga, gb, base_column=0):
    nx, ny, nz, ci, co = dims
    half = 4 * ci
    first = lax.broadcasted_iota(jnp.int32, (co, nz), 1) == 0
    zeros = jnp.zeros((2 * co, nz), BF16)

    starts = range(0, len(columns), chunk)
    for c0 in starts:
        some = columns[c0 : c0 + chunk]
        back = jnp.dot(w[:, half:], corners(rolled, some), preferred_element_type=F32)
        here = jnp.dot(w[:, :half], corners(block, some), preferred_element_type=F32)
        for k, (i, j) in enumerate(some):
            cols = slice(k * nz, (k + 1) * nz)
            at = base_column + c0 + k
            wide = slice(at * nz, (at + 1) * nz)
            for tx in range(2):
                for ty in range(2):
                    sx, sy = 1 - tx, 1 - ty
                    m, n = i - sx, j - sy
                    base = (2 * tx + ty) * 2 * co
                    if not (0 <= m < nx and 0 <= n < ny):
                        ga[base : base + 2 * co, wide] = zeros
                        gb[base : base + 2 * co, wide] = zeros
                        r = slice(base, base + co)
                        put_foreign(
                            (i, j, tx, ty), 0, back[r, cols] + jnp.where(first, 0.0, here[r, cols])
                        )
                        r = slice(base + co, base + 2 * co)
                        put_foreign(
                            (i, j, tx, ty), 1, jnp.where(first, 0.0, back[r, cols]) + here[r, cols]
                        )
                        continue
                    for tz in range(2):
                        sz = 1 - tz
                        r = slice(base + tz * co, base + (tz + 1) * co)
                        low, high = back[r, cols], here[r, cols]
                        if sz == 1:
                            before = low + jnp.where(first, 0.0, high)
                            before = pltpu.roll(before, nz - 1, 1)
                        else:
                            before = jnp.where(first, 0.0, low) + high
                        q = (2 * sx + sy) * 2 + sz
                        sig = 0.5 * jnp.tanh(0.5 * before) + 0.5
                        value = before * sig
                        put_value(q, m, n, value.astype(BF16))
                        slope = sig + value * (1.0 - sig)
                        grad = cot_at(q, m, n).astype(F32) * slope
                        if sz == 1:
                            grad = pltpu.roll(grad, 1, 1)
                        whole = grad.astype(BF16)
                        cut = jnp.where(first, 0.0, grad).astype(BF16)
                        ga[r, wide] = cut if sz == 0 else whole
                        gb[r, wide] = cut if sz == 1 else whole


def weight_pass(columns, block, rolled, ga, gb, wg_add):
    nt = (((1,), (1,)), ((), ()))
    for part, (grads, get) in enumerate(((gb, block), (ga, rolled))):
        wg_add(
            part,
            lax.dot_general(grads[...], corners(get, columns), nt, preferred_element_type=F32),
        )


def input_pass(dims, chunk, columns, wt, cut_grads, ig_add):
    nx, ny, nz, ci, co = dims
    half = 4 * ci
    started = set()
    for c0 in range(0, len(columns), chunk):
        some = columns[c0 : c0 + chunk]
        left, right = cut_grads(c0, some)
        back = jnp.dot(wt[half:], left, preferred_element_type=F32)
        here = jnp.dot(wt[:half], right, preferred_element_type=F32)
        for k, (i, j) in enumerate(some):
            cols = slice(k * nz, (k + 1) * nz)
            both = here[:, cols] + pltpu.roll(back[:, cols], nz - 1, 1)
            for ex in range(2):
                for ey in range(2):
                    m, y = i - ex, j - ey
                    if 0 <= m < nx and 0 <= y < ny:
                        r = (2 * ex + ey) * ci
                        ig_add(m, y, both[r : r + ci], (m, y) not in started)
                        started.add((m, y))
    return started


def outer_columns(nx, ny):
    columns = [(i, j) for i in (0, nx) for j in range(ny + 1)]
    return columns + [(i, j) for i in range(1, nx) for j in (0, ny)]


def foreign_spots(nx, ny):
    spots = {}
    for i, j in outer_columns(nx, ny):
        for tx in range(2):
            for ty in range(2):
                m, n = i - 1 + tx, j - 1 + ty
                if not (0 <= m < nx and 0 <= n < ny):
                    spots[i, j, tx, ty] = len(spots)
    return spots


def is_inner(q, m, nx):
    return 1 <= m + q // 4 < nx


def edge_row(q, ny):
    return (ny - 1) if q // 2 % 2 else 0


def inner_kernel(
    dims,
    chunk,
    vol_in,
    taps_in,
    cot,
    flat,
    w,
    wt_out,
    vals_out,
    cot_edge,
    wg,
    ig_out,
    face_up,
    face_down,
    wt,
    vals,
    ig,
    vol,
    taps,
    sems,
    vm,
    ga,
    gb,
    cots,
):
    nx, ny, nz, ci, co = dims
    half = 4 * ci
    to_y = swap_matrix(GROUP, ny)
    arriving = [
        pltpu.make_async_copy(vol_in, vol, sems.at[0]),
        pltpu.make_async_copy(taps_in, taps, sems.at[1]),
    ]
    leaving = [
        pltpu.make_async_copy(cot.at[4:, :, nx - 1], face_up, sems.at[2]),
        pltpu.make_async_copy(cot.at[:4, :, 0], face_down, sems.at[3]),
    ]
    for copy in arriving + leaving:
        copy.start()

    for i in range(1, nx):
        for q in range(8):
            m = i - q // 4

            def put(k, y, rows, i=i, q=q):
                r = slice(q * co + k * GROUP, q * co + (k + 1) * GROUP)
                cots[i - 1, r, y * nz : (y + 1) * nz] = rows
                if y == edge_row(q, ny):
                    cot_edge[i - 1, r] = rows

            tiles = Tiles(
                co // GROUP, lambda k, q=q, m=m: cot[q, k * GROUP : (k + 1) * GROUP, m]
            )
            bring_plane(to_y, tiles, ny, nz, put)

    for copy in arriving:
        copy.wait()
    for tx in range(2):
        for ty in range(2):
            for tz in range(2):
                r = ((2 * tx + ty) * 2 + tz) * co
                for ez in range(2):
                    for ex in range(2):
                        pair = [taps[2 * ex + tx, 2 * ey + ty, 2 * ez + tz] for ey in range(2)]
                        c = (2 * ez + ex) * 2 * ci
                        w[r : r + co, c : c + 2 * ci] = jnp.concatenate(pair, axis=1)
    wt[...] = w[...].T
    leaving.append(pltpu.make_async_copy(wt, wt_out, sems.at[4]))
    leaving[-1].start()

    for x in range(nx):

        def put(k, y, rows, x=x):
            r = slice(k * GROUP, (k + 1) * GROUP)
            lanes = slice(y * nz, (y + 1) * nz)
            flat[x, r, lanes] = rows
            vm[x, r, lanes] = pltpu.roll(rows.astype(F32), 1, 1).astype(BF16)

        tiles = Tiles(
            ci // GROUP, lambda k, x=x: vol[k * GROUP : (k + 1) * GROUP, x]
        )
        bring_plane(to_y, tiles, ny, nz, put)

    def block(x, y):
        return flat[x - 1, :, (y - 1) * nz : y * nz]

    def rolled(x, y):
        return vm[x - 1, :, (y - 1) * nz : y * nz]

    def cot_at(q, m, n):
        return cots[m + q // 4 - 1, q * co : (q + 1) * co, n * nz : (n + 1) * nz]

    def put_value(q, m, n, value):
        vals[m + q // 4 - 1, q * co : (q + 1) * co, n * nz : (n + 1) * nz] = value

    def wg_add(part, total):
        wg[:, part * half : (part + 1) * half] = total

    def ig_add(m, y, value, fresh):
        lanes = slice(y * nz, (y + 1) * nz)
        ig[m, :, lanes] = value if fresh else ig[m, :, lanes] + value

    def cut_grads(c0, some):
        wide = slice(c0 * nz, (c0 + len(some)) * nz)
        return ga[:, wide], gb[:, wide]

    columns = [(i, j) for i in range(1, nx) for j in range(1, ny)]
    forward_pass(dims, chunk, columns, block, rolled, w, cot_at, put_value, None, ga, gb)
    leaving.append(pltpu.make_async_copy(vals, vals_out, sems.at[5]))
    leaving[-1].start()
    input_pass(dims, chunk, columns, wt, cut_grads, ig_add)
    leaving.append(pltpu.make_async_copy(ig, ig_out, sems.at[6]))
    leaving[-1].start()
    weight_pass(columns, block, rolled, ga, gb, wg_add)
    for copy in leaving:
        copy.wait()


def outer_kernel(
    dims,
    chunk,
    flat,
    xlo_in,
    xhi_in,
    ylo_in,
    yhi_in,
    w,
    cot,
    cot_edge,
    wg_in,
    pre_out,
    vals_out,
    val_edge_out,
    ga_out,
    gb_out,
    wg,
    ga,
    gb,
    vm,
    pre,
    vals,
    val_edge,
    xraw,
    yraw,
    cots,
    sems,
):
    nx, ny, nz, ci, co = dims
    to_y = swap_matrix(GROUP, ny)
    arriving = [
        pltpu.make_async_copy(xlo_in.at[: ny * ci], xraw.at[0], sems.at[0]),
        pltpu.make_async_copy(xhi_in.at[: ny * ci], xraw.at[1], sems.at[1]),
        pltpu.make_async_copy(ylo_in.at[: (nx + 2) * ci], yraw.at[0], sems.at[2]),
        pltpu.make_async_copy(yhi_in.at[: (nx + 2) * ci], yraw.at[1], sems.at[3]),
    ]
    for copy in arriving:
        copy.start()

    for side in range(2):
        for q in range(4 * side, 4 * side + 4):

            def put(k, y, rows, q=q):
                r = slice(q * co + k * GROUP, q * co + (k + 1) * GROUP)
                cots[r, y * nz : (y + 1) * nz] = rows

            tiles = Tiles(
                co // GROUP,
                lambda k, q=q, side=side: cot[
                    q, k * GROUP : (k + 1) * GROUP, side * (nx - 1)
                ],
            )
            bring_plane(to_y, tiles, ny, nz, put)

    for copy in arriving:
        copy.wait()

    def block(x, y):
        if y == 0:
            return yraw[0, x * ci : (x + 1) * ci]
        if y == ny + 1:
            return yraw[1, x * ci : (x + 1) * ci]
        if x == 0:
            return xraw[0, (y - 1) * ci : y * ci]
        if x == nx + 1:
            return xraw[1, (y - 1) * ci : y * ci]
        return flat[x - 1, :, (y - 1) * nz : y * nz]

    for x in range(nx + 2):
        for y in range(ny + 2):
            lanes = slice(y * nz, (y + 1) * nz)
            vm[x, :, lanes] = pltpu.roll(block(x, y).astype(F32), 1, 1).astype(BF16)

    def rolled(x, y):
        return vm[x, :, y * nz : (y + 1) * nz]

    def cot_at(q, m, n):
        r = slice(q * co, (q + 1) * co)
        if is_inner(q, m, nx):
            return cot_edge[m + q // 4 - 1, r]
        return cots[r, n * nz : (n + 1) * nz]

    def put_value(q, m, n, value):
        r = slice(q * co, (q + 1) * co)
        if is_inner(q, m, nx):
            val_edge[m + q // 4 - 1, r] = value
        else:
            vals[r, n * nz : (n + 1) * nz] = value

    spots = foreign_spots(nx, ny)

    def put_foreign(key, tz, value):
        pre[spots[key], tz * co : (tz + 1) * co] = value

    leaving = []

    def leave(src, dst):
        leaving.append(pltpu.make_async_copy(src, dst, sems.at[4 + len(leaving)]))
        leaving[-1].start()

    columns = outer_columns(nx, ny)
    sent = 0
    for k, i in enumerate((0, nx, None)):
        c0 = k * (ny + 1)
        some = columns[c0 : c0 + ny + 1] if k < 2 else columns[c0:]
        forward_pass(
            dims, chunk, some, block, rolled, w, cot_at, put_value, put_foreign, ga, gb, c0
        )
        upto = sent + sum(spot[:2] in some for spot in spots)
        leave(pre.at[sent:upto], pre_out.at[sent:upto])
        sent = upto
        if k < 2:
            rows = pl.ds(4 * k * co, 4 * co)
            leave(vals.at[rows], vals_out.at[rows])
        else:
            leave(val_edge, val_edge_out)
    leave(ga, ga_out)
    leave(gb, gb_out)

    def wg_add(part, total):
        total = total + wg_in[:, part * 4 * ci : (part + 1) * 4 * ci]
        for ex in range(2):
            for row in range(8):
                tx, ty, tz = row // 4, row // 2 % 2, row % 2
                index = ((tx * 2 + ty) * 2 + part) * 2 + tz
                wg[ex * 16 + index] = total[
                    row * co : (row + 1) * co, ex * 2 * ci : (ex + 1) * 2 * ci
                ].astype(BF16)

    weight_pass(columns, block, rolled, ga, gb, wg_add)
    for copy in leaving:
        copy.wait()


def last_kernel(
    dims,
    chunk,
    ga_in,
    gb_in,
    pre_in,
    vals_in,
    val_edge_in,
    xlo_in,
    xhi_in,
    ylo_in,
    yhi_in,
    wt_in,
    inner_vals_in,
    ig_in,
    act_out,
    ig_out,
    ga,
    gb,
    pre,
    vals,
    val_edge,
    xraw,
    yraw,
    wt,
    inner_vals,
    ig,
    cots,
    staged,
    ig_staged,
    sems,
):
    nx, ny, nz, ci, co = dims
    to_y = swap_matrix(GROUP, ny)
    to_c = swap_matrix(ny, GROUP)
    skip = (nx + 2) * ci
    early = [(vals_in, vals), (val_edge_in, val_edge), (inner_vals_in, inner_vals)]
    late = [
        (xlo_in, xraw.at[0]),
        (xhi_in, xraw.at[1]),
        (ylo_in.at[skip:], yraw.at[0]),
        (yhi_in.at[skip:], yraw.at[1]),
        (ga_in, ga),
        (gb_in, gb),
        (pre_in, pre),
        (wt_in, wt),
        (ig_in, ig),
    ]
    copies = [
        pltpu.make_async_copy(src, dst, sems.at[k]) for k, (src, dst) in enumerate(early + late)
    ]
    for copy in copies:
        copy.start()
    spot = len(copies)
    for copy in copies[: len(early)]:
        copy.wait()
    leaving = []

    for m in range(nx):
        for q in range(8):
            tiles = []
            for k in range(co // GROUP):
                r = slice(q * co + k * GROUP, q * co + (k + 1) * GROUP)
                rows = []
                for y in range(ny):
                    lanes = slice(y * nz, (y + 1) * nz)
                    if not is_inner(q, m, nx):
                        rows.append(vals[r, lanes])
                    elif y == edge_row(q, ny):
                        rows.append(val_edge[m + q // 4 - 1, r])
                    else:
                        rows.append(inner_vals[m + q // 4 - 1, r, lanes])
                tiles.append(jnp.concatenate(rows, axis=0).reshape(ny, GROUP, nz))
            moved = turn(to_c, tiles, nz)
            index = m * 8 + q
            for k in range(co // GROUP):
                staged[index, k * GROUP : (k + 1) * GROUP] = moved[
                    :, k * nz : (k + 1) * nz
                ].reshape(GROUP, ny, nz)
            leaving.append(
                pltpu.make_async_copy(
                    staged.at[index], act_out.at[q, :, m], sems.at[spot + index]
                )
            )
            leaving[-1].start()

    for copy in copies[len(early) :]:
        copy.wait()
    for side in range(2):
        for p in range(4):

            def put(k, y, rows, side=side, p=p):
                r = slice(p * co + k * GROUP, p * co + (k + 1) * GROUP)
                cots[side, r, y * nz : (y + 1) * nz] = rows

            tiles = Tiles(
                co // GROUP,
                lambda k, side=side, p=p: xraw[side, p, k * GROUP : (k + 1) * GROUP],
            )
            bring_plane(to_y, tiles, ny, nz, put)

    spots = foreign_spots(nx, ny)
    first = lax.broadcasted_iota(jnp.int32, (co, nz), 1) == 0
    corner = 4 * co * nx

    def foreign(i, j, tx, ty, tz):
        sx, sy, sz = 1 - tx, 1 - ty, 1 - tz
        m, n = i - sx, j - sy
        if 0 <= n < ny:
            side = 0 if m < 0 else 1
            r = (2 * sy + sz) * co
            cot = cots[side, r : r + co, n * nz : (n + 1) * nz]
        else:
            end = 0 if n < 0 else 1
            if 0 <= m < nx:
                r = ((m * 2 + sx) * 2 + sz) * co
            else:
                r = corner + ((0 if m < 0 else 2) + sz) * co
            cot = yraw[end, r : r + co]
        cot = cot.astype(F32)
        if sz == 1:
            cot = pltpu.roll(cot, 1, 1)
        before = pre[spots[i, j, tx, ty], tz * co : (tz + 1) * co]
        sig = 0.5 * jnp.tanh(0.5 * before) + 0.5
        grad = cot * (sig + before * sig * (1.0 - sig))
        whole = grad.astype(BF16)
        cut = jnp.where(first, 0.0, grad).astype(BF16)
        return (whole, cut) if sz == 1 else (cut, whole)

    def cut_grads(c0, some):
        lefts, rights = [], []
        for k, (i, j) in enumerate(some):
            wide = slice((c0 + k) * nz, (c0 + k + 1) * nz)
            left, right = [], []
            for tx in range(2):
                for ty in range(2):
                    base = (2 * tx + ty) * 2 * co
                    if (i, j, tx, ty) in spots:
                        for tz in range(2):
                            one, two = foreign(i, j, tx, ty, tz)
                            left.append(one)
                            right.append(two)
                    else:
                        left.append(ga[base : base + 2 * co, wide])
                        right.append(gb[base : base + 2 * co, wide])
            lefts.append(jnp.concatenate(left, axis=0))
            rights.append(jnp.concatenate(right, axis=0))
        return jnp.concatenate(lefts, axis=1), jnp.concatenate(rights, axis=1)

    def ig_add(m, y, value, fresh):
        lanes = slice(y * nz, (y + 1) * nz)
        ig[m, :, lanes] = ig[m, :, lanes] + value

    input_pass(dims, chunk, outer_columns(nx, ny), wt, cut_grads, ig_add)
    for m in range(nx):
        for k in range(0, ci // GROUP, 2):
            tiles = []
            for h in range(2):
                r = slice((k + h) * GROUP, (k + h + 1) * GROUP)
                rows = [
                    ig[m, r, y * nz : (y + 1) * nz].astype(BF16) for y in range(ny)
                ]
                tiles.append(jnp.concatenate(rows, axis=0).reshape(ny, GROUP, nz))
            moved = turn(to_c, tiles, nz)
            for h in range(2):
                ig_staged[(k + h) * GROUP : (k + h + 1) * GROUP, m] = moved[
                    :, h * nz : (h + 1) * nz
                ].reshape(GROUP, ny, nz)
    leaving.append(pltpu.make_async_copy(ig_staged, ig_out, sems.at[spot + 8 * nx]))
    leaving[-1].start()
    for copy in leaving:
        copy.wait()


def unpack_kernel(co, ci, packed, out):
    for ex in range(2):
        for tx in range(2):
            for ty in range(2):
                for ez in range(2):
                    for tz in range(2):
                        index = (((ex * 2 + tx) * 2 + ty) * 2 + ez) * 2 + tz
                        pair = packed[index].astype(F32)
                        for ey in range(2):
                            out[2 * ex + tx, 2 * ey + ty, 2 * ez + tz] = pair[
                                :, ey * ci : (ey + 1) * ci
                            ]


def far(shape, dtype):
    return pltpu.HBM(shape, dtype)


def stay(array):
    return pltpu.with_memory_space_constraint(array, pltpu.HBM)


def neighbours(axis):
    count = lax.axis_size(axis)
    up = [(i, i + 1) for i in range(count - 1)]
    return up, [(b, a) for a, b in up]


def on_device(volume, kernel, cotangent):
    ci, nx, ny, nz = volume.shape
    co = kernel.shape[3]
    gx, gy = lax.axis_size("gx"), lax.axis_size("gy")
    gx_up, gx_down = neighbours("gx")
    gy_up, gy_down = neighbours("gy")
    cells = nx * gx * ny * gy * nz
    dims = (nx, ny, nz, ci, co)

    cot = cotangent.reshape(8, co, nx, ny, nz)

    def corner(sx, sy):
        m, n = (nx - 1) * sx, (ny - 1) * sy
        return cotangent[sx, sy, :, :, m, n].reshape(2 * co, nz)

    def x_message(sx):
        plane = volume[:, (nx - 1) * sx].transpose(1, 0, 2).reshape(ny * ci, nz)
        return jnp.concatenate([plane, corner(sx, 0), corner(sx, 1)], axis=0)

    xlo = lax.ppermute(x_message(1), "gx", gx_up)
    xhi = lax.ppermute(x_message(0), "gx", gx_down)

    vmem = pl.BlockSpec(memory_space=pltpu.VMEM)
    smem = pl.BlockSpec(memory_space=pltpu.SMEM)
    anywhere = pl.BlockSpec(memory_space=pl.ANY)
    hbm = pl.BlockSpec(memory_space=pltpu.HBM)
    params = pltpu.CompilerParams(vmem_limit_bytes=24 * 1024 * 1024)
    n_in = (nx - 1) * (ny - 1)
    n_out = 2 * (ny + 1) + 2 * (nx - 1)
    flat, w, wt, inner_vals, cot_edge, wg_part, ig_part, face_up, face_down = pl.pallas_call(
        functools.partial(inner_kernel, dims, 5),
        out_shape=(
            jax.ShapeDtypeStruct((nx, ci, ny * nz), BF16),
            jax.ShapeDtypeStruct((8 * co, 8 * ci), BF16),
            far((8 * ci, 8 * co), BF16),
            far((nx - 1, 8 * co, ny * nz), BF16),
            jax.ShapeDtypeStruct((nx - 1, 8 * co, nz), BF16),
            jax.ShapeDtypeStruct((8 * co, 8 * ci), F32),
            far((nx, ci, ny * nz), F32),
            far((4, co, ny, nz), BF16),
            far((4, co, ny, nz), BF16),
        ),
        in_specs=[anywhere, anywhere, vmem],
        out_specs=(vmem, vmem, hbm, hbm, vmem, vmem, hbm, hbm, hbm),
        scratch_shapes=[
            pltpu.VMEM((8 * ci, 8 * co), BF16),
            pltpu.VMEM((nx - 1, 8 * co, ny * nz), BF16),
            pltpu.VMEM((nx, ci, ny * nz), F32),
            pltpu.VMEM(volume.shape, BF16),
            pltpu.VMEM(kernel.shape, BF16),
            pltpu.SemaphoreType.DMA((7,)),
            pltpu.VMEM((nx, ci, ny * nz), BF16),
            pltpu.VMEM((8 * co, n_in * nz), BF16),
            pltpu.VMEM((8 * co, n_in * nz), BF16),
            pltpu.VMEM((nx - 1, 8 * co, ny * nz), BF16),
        ],
        compiler_params=params,
    )(volume, kernel, cot)

    def y_message(sy):
        y = (ny - 1) * sy
        rows = slice(y * ci, (y + 1) * ci)
        own = cotangent[:, sy, :, :, :, y].transpose(3, 0, 1, 2, 4).reshape(4 * co * nx, nz)
        corner = slice((ny * ci + sy * 2 * co), (ny * ci + (sy + 1) * 2 * co))
        return jnp.concatenate(
            [
                xlo[rows],
                flat[:, :, y * nz : (y + 1) * nz].reshape(nx * ci, nz),
                xhi[rows],
                own,
                xlo[corner],
                xhi[corner],
            ],
            axis=0,
        )

    ylo = lax.ppermute(y_message(1), "gy", gy_up)
    yhi = lax.ppermute(y_message(0), "gy", gy_down)
    face_lo = lax.ppermute(face_up, "gx", gx_up)
    face_hi = lax.ppermute(face_down, "gx", gx_down)
    foreign = len(foreign_spots(nx, ny))
    pre_shape = (foreign, 2 * co, nz)
    pre, vals, val_edge, ga, gb, wg = pl.pallas_call(
        functools.partial(outer_kernel, dims, 4),
        out_shape=(
            far(pre_shape, F32),
            far((8 * co, ny * nz), BF16),
            far((nx - 1, 8 * co, nz), BF16),
            far((8 * co, n_out * nz), BF16),
            far((8 * co, n_out * nz), BF16),
            jax.ShapeDtypeStruct((32, co, 2 * ci), BF16),
        ),
        in_specs=[vmem] + [anywhere] * 4 + [vmem] * 4,
        out_specs=(hbm,) * 5 + (vmem,),
        scratch_shapes=[
            pltpu.VMEM((8 * co, n_out * nz), BF16),
            pltpu.VMEM((8 * co, n_out * nz), BF16),
            pltpu.VMEM((nx + 2, ci, (ny + 2) * nz), BF16),
            pltpu.VMEM(pre_shape, F32),
            pltpu.VMEM((8 * co, ny * nz), BF16),
            pltpu.VMEM((nx - 1, 8 * co, nz), BF16),
            pltpu.VMEM((2, ny * ci, nz), BF16),
            pltpu.VMEM((2, (nx + 2) * ci, nz), BF16),
            pltpu.VMEM((8 * co, ny * nz), BF16),
            pltpu.SemaphoreType.DMA((12,)),
        ],
        compiler_params=params,
    )(flat, xlo, xhi, ylo, yhi, w, cot, cot_edge, wg_part)
    passed = [
        stay(array)
        for array in (ga, gb, pre, vals, val_edge, face_lo, face_hi, ylo, yhi, wt, inner_vals, ig_part)
    ]
    act, input_grad = pl.pallas_call(
        functools.partial(last_kernel, dims, 4),
        out_shape=(
            jax.ShapeDtypeStruct(cot.shape, BF16),
            jax.ShapeDtypeStruct(volume.shape, BF16),
        ),
        in_specs=[hbm] * 12,
        out_specs=(anywhere,) * 2,
        scratch_shapes=[
            pltpu.VMEM((8 * co, n_out * nz), BF16),
            pltpu.VMEM((8 * co, n_out * nz), BF16),
            pltpu.VMEM(pre_shape, F32),
            pltpu.VMEM((8 * co, ny * nz), BF16),
            pltpu.VMEM((nx - 1, 8 * co, nz), BF16),
            pltpu.VMEM((2, 4, co, ny, nz), BF16),
            pltpu.VMEM((2, 4 * co * nx + 4 * co, nz), BF16),
            pltpu.VMEM((8 * ci, 8 * co), BF16),
            pltpu.VMEM((nx - 1, 8 * co, ny * nz), BF16),
            pltpu.VMEM((nx, ci, ny * nz), F32),
            pltpu.VMEM((2, 4 * co, ny * nz), BF16),
            pltpu.VMEM((8 * nx, co, ny, nz), BF16),
            pltpu.VMEM(volume.shape, BF16),
            pltpu.SemaphoreType.DMA((13 + 8 * nx,)),
        ],
        compiler_params=params,
    )(*passed)

    scale = 1.0 / math.sqrt(cells)
    devices = gx * gy
    shares = wg.reshape(devices, 32 * co // devices, 2 * ci)
    shares = lax.all_to_all(shares, ("gx", "gy"), 0, 0, tiled=True)
    piece = (jnp.sum(shares.astype(F32), axis=0) * scale).astype(BF16)
    pieces = jnp.broadcast_to(piece[None], (devices,) + piece.shape)
    pieces = lax.all_to_all(pieces, ("gx", "gy"), 0, 0, tiled=True)
    weight_grad = pl.pallas_call(
        functools.partial(unpack_kernel, co, ci),
        out_shape=jax.ShapeDtypeStruct((4, 4, 4, co, ci), F32),
        in_specs=[vmem],
        out_specs=vmem,
        compiler_params=pltpu.CompilerParams(vmem_limit_bytes=8 * 1024 * 1024),
    )(pieces.reshape(32, co, 2 * ci))

    return act.reshape(cotangent.shape), input_grad, weight_grad


def solution(mesh):
    placed = (P(None, "gx", "gy", None), P(), P(None, None, None, None, "gx", "gy", None))
    return jax.shard_map(
        on_device,
        mesh=mesh,
        in_specs=placed,
        out_specs=(placed[2], placed[0], P()),
        check_vma=False,
    )
```

```python
import functools
import math

import jax
import jax.numpy as jnp
from jax import lax
from jax.experimental import pallas as pl
from jax.experimental.pallas import tpu as pltpu
from jax.sharding import PartitionSpec as P

F32 = jnp.float32
BF16 = jnp.bfloat16
GROUP = 16


def swap_matrix(outer, inner):
    size = outer * inner
    row = lax.broadcasted_iota(jnp.int32, (size, size), 0)
    col = lax.broadcasted_iota(jnp.int32, (size, size), 1)
    return jnp.where(col == (row % outer) * inner + row // outer, 1.0, 0.0).astype(BF16)


def turn(matrix, pieces, nz):
    flat = [p.reshape(p.shape[0] * p.shape[1], nz) for p in pieces]
    moved = jnp.dot(matrix, jnp.concatenate(flat, axis=1), preferred_element_type=F32)
    return moved.astype(BF16)


def bring_plane(to_y, raw, ny, nz, put):
    for k in range(0, raw.count, 2):
        moved = turn(to_y, [raw(k), raw(k + 1)], nz)
        for y in range(ny):
            rows = slice(y * GROUP, (y + 1) * GROUP)
            put(k, y, moved[rows, :nz])
            put(k + 1, y, moved[rows, nz:])


class Tiles:
    def __init__(self, count, get):
        self.count, self.get = count, get

    def __call__(self, k):
        return self.get(k)


def corners(get, some):
    return jnp.concatenate(
        [
            jnp.concatenate([get(i + 1 - ex, j + 1 - ey) for i, j in some], axis=1)
            for ex in range(2)
            for ey in range(2)
        ],
        axis=0,
    )


def forward_pass(dims, chunk, columns, block, rolled, w, cot_at, put_value, put_foreign, ga, gb, base_column=0):
    nx, ny, nz, ci, co = dims
    half = 4 * ci
    first = lax.broadcasted_iota(jnp.int32, (co, nz), 1) == 0
    zeros = jnp.zeros((2 * co, nz), BF16)

    starts = range(0, len(columns), chunk)
    for c0 in starts:
        some = columns[c0 : c0 + chunk]
        back = jnp.dot(w[:, half:], corners(rolled, some), preferred_element_type=F32)
        here = jnp.dot(w[:, :half], corners(block, some), preferred_element_type=F32)
        for k, (i, j) in enumerate(some):
            cols = slice(k * nz, (k + 1) * nz)
            at = base_column + c0 + k
            wide = slice(at * nz, (at + 1) * nz)
            for tx in range(2):
                for ty in range(2):
                    sx, sy = 1 - tx, 1 - ty
                    m, n = i - sx, j - sy
                    base = (2 * tx + ty) * 2 * co
                    if not (0 <= m < nx and 0 <= n < ny):
                        ga[base : base + 2 * co, wide] = zeros
                        gb[base : base + 2 * co, wide] = zeros
                        r = slice(base, base + co)
                        put_foreign(
                            (i, j, tx, ty), 0, back[r, cols] + jnp.where(first, 0.0, here[r, cols])
                        )
                        r = slice(base + co, base + 2 * co)
                        put_foreign(
                            (i, j, tx, ty), 1, jnp.where(first, 0.0, back[r, cols]) + here[r, cols]
                        )
                        continue
                    for tz in range(2):
                        sz = 1 - tz
                        r = slice(base + tz * co, base + (tz + 1) * co)
                        low, high = back[r, cols], here[r, cols]
                        if sz == 1:
                            before = low + jnp.where(first, 0.0, high)
                            before = pltpu.roll(before, nz - 1, 1)
                        else:
                            before = jnp.where(first, 0.0, low) + high
                        q = (2 * sx + sy) * 2 + sz
                        sig = 0.5 * jnp.tanh(0.5 * before) + 0.5
                        value = before * sig
                        put_value(q, m, n, value.astype(BF16))
                        slope = sig + value * (1.0 - sig)
                        grad = cot_at(q, m, n).astype(F32) * slope
                        if sz == 1:
                            grad = pltpu.roll(grad, 1, 1)
                        whole = grad.astype(BF16)
                        cut = jnp.where(first, 0.0, grad).astype(BF16)
                        ga[r, wide] = cut if sz == 0 else whole
                        gb[r, wide] = cut if sz == 1 else whole


def weight_pass(columns, block, rolled, ga, gb, wg_add):
    nt = (((1,), (1,)), ((), ()))
    for part, (grads, get) in enumerate(((gb, block), (ga, rolled))):
        wg_add(
            part,
            lax.dot_general(grads[...], corners(get, columns), nt, preferred_element_type=F32),
        )


def input_pass(dims, chunk, columns, wt, cut_grads, ig_add):
    nx, ny, nz, ci, co = dims
    half = 4 * ci
    started = set()
    for c0 in range(0, len(columns), chunk):
        some = columns[c0 : c0 + chunk]
        left, right = cut_grads(c0, some)
        back = jnp.dot(wt[half:], left, preferred_element_type=F32)
        here = jnp.dot(wt[:half], right, preferred_element_type=F32)
        for k, (i, j) in enumerate(some):
            cols = slice(k * nz, (k + 1) * nz)
            both = here[:, cols] + pltpu.roll(back[:, cols], nz - 1, 1)
            for ex in range(2):
                for ey in range(2):
                    m, y = i - ex, j - ey
                    if 0 <= m < nx and 0 <= y < ny:
                        r = (2 * ex + ey) * ci
                        ig_add(m, y, both[r : r + ci], (m, y) not in started)
                        started.add((m, y))
    return started


def outer_columns(nx, ny):
    columns = [(i, j) for i in (0, nx) for j in range(ny + 1)]
    return columns + [(i, j) for i in range(1, nx) for j in (0, ny)]


def foreign_spots(nx, ny):
    spots = {}
    for i, j in outer_columns(nx, ny):
        for tx in range(2):
            for ty in range(2):
                m, n = i - 1 + tx, j - 1 + ty
                if not (0 <= m < nx and 0 <= n < ny):
                    spots[i, j, tx, ty] = len(spots)
    return spots


def is_inner(q, m, nx):
    return 1 <= m + q // 4 < nx


def edge_row(q, ny):
    return (ny - 1) if q // 2 % 2 else 0


def inner_kernel(
    dims,
    chunk,
    vol_in,
    taps_in,
    cot,
    flat,
    w,
    wt_out,
    vals_out,
    cot_edge,
    wg,
    ig_out,
    face_up,
    face_down,
    wt,
    vals,
    ig,
    vol,
    taps,
    sems,
    vm,
    ga,
    gb,
    cots,
):
    nx, ny, nz, ci, co = dims
    half = 4 * ci
    to_y = swap_matrix(GROUP, ny)
    arriving = [
        pltpu.make_async_copy(vol_in, vol, sems.at[0]),
        pltpu.make_async_copy(taps_in, taps, sems.at[1]),
    ]
    leaving = [
        pltpu.make_async_copy(cot.at[4:, :, nx - 1], face_up, sems.at[2]),
        pltpu.make_async_copy(cot.at[:4, :, 0], face_down, sems.at[3]),
    ]
    for copy in arriving + leaving:
        copy.start()

    for i in range(1, nx):
        for q in range(8):
            m = i - q // 4

            def put(k, y, rows, i=i, q=q):
                r = slice(q * co + k * GROUP, q * co + (k + 1) * GROUP)
                cots[i - 1, r, y * nz : (y + 1) * nz] = rows
                if y == edge_row(q, ny):
                    cot_edge[i - 1, r] = rows

            tiles = Tiles(
                co // GROUP, lambda k, q=q, m=m: cot[q, k * GROUP : (k + 1) * GROUP, m]
            )
            bring_plane(to_y, tiles, ny, nz, put)

    for copy in arriving:
        copy.wait()
    for tx in range(2):
        for ty in range(2):
            for tz in range(2):
                r = ((2 * tx + ty) * 2 + tz) * co
                for ez in range(2):
                    for ex in range(2):
                        pair = [taps[2 * ex + tx, 2 * ey + ty, 2 * ez + tz] for ey in range(2)]
                        c = (2 * ez + ex) * 2 * ci
                        w[r : r + co, c : c + 2 * ci] = jnp.concatenate(pair, axis=1)
    wt[...] = w[...].T
    leaving.append(pltpu.make_async_copy(wt, wt_out, sems.at[4]))
    leaving[-1].start()

    for x in range(nx):

        def put(k, y, rows, x=x):
            r = slice(k * GROUP, (k + 1) * GROUP)
            lanes = slice(y * nz, (y + 1) * nz)
            flat[x, r, lanes] = rows
            vm[x, r, lanes] = pltpu.roll(rows.astype(F32), 1, 1).astype(BF16)

        tiles = Tiles(
            ci // GROUP, lambda k, x=x: vol[k * GROUP : (k + 1) * GROUP, x]
        )
        bring_plane(to_y, tiles, ny, nz, put)

    def block(x, y):
        return flat[x - 1, :, (y - 1) * nz : y * nz]

    def rolled(x, y):
        return vm[x - 1, :, (y - 1) * nz : y * nz]

    def cot_at(q, m, n):
        return cots[m + q // 4 - 1, q * co : (q + 1) * co, n * nz : (n + 1) * nz]

    def put_value(q, m, n, value):
        vals[m + q // 4 - 1, q * co : (q + 1) * co, n * nz : (n + 1) * nz] = value

    def wg_add(part, total):
        wg[:, part * half : (part + 1) * half] = total

    def ig_add(m, y, value, fresh):
        lanes = slice(y * nz, (y + 1) * nz)
        ig[m, :, lanes] = value if fresh else ig[m, :, lanes] + value

    def cut_grads(c0, some):
        wide = slice(c0 * nz, (c0 + len(some)) * nz)
        return ga[:, wide], gb[:, wide]

    columns = [(i, j) for i in range(1, nx) for j in range(1, ny)]
    forward_pass(dims, chunk, columns, block, rolled, w, cot_at, put_value, None, ga, gb)
    leaving.append(pltpu.make_async_copy(vals, vals_out, sems.at[5]))
    leaving[-1].start()
    input_pass(dims, chunk, columns, wt, cut_grads, ig_add)
    leaving.append(pltpu.make_async_copy(ig, ig_out, sems.at[6]))
    leaving[-1].start()
    weight_pass(columns, block, rolled, ga, gb, wg_add)
    for copy in leaving:
        copy.wait()


def outer_kernel(
    dims,
    chunk,
    flat,
    xlo_in,
    xhi_in,
    ylo_in,
    yhi_in,
    w,
    cot,
    cot_edge,
    wg_in,
    pre_out,
    vals_out,
    val_edge_out,
    ga_out,
    gb_out,
    wg,
    ga,
    gb,
    vm,
    pre,
    vals,
    val_edge,
    xraw,
    yraw,
    cots,
    sems,
):
    nx, ny, nz, ci, co = dims
    to_y = swap_matrix(GROUP, ny)
    arriving = [
        pltpu.make_async_copy(xlo_in.at[: ny * ci], xraw.at[0], sems.at[0]),
        pltpu.make_async_copy(xhi_in.at[: ny * ci], xraw.at[1], sems.at[1]),
        pltpu.make_async_copy(ylo_in.at[: (nx + 2) * ci], yraw.at[0], sems.at[2]),
        pltpu.make_async_copy(yhi_in.at[: (nx + 2) * ci], yraw.at[1], sems.at[3]),
    ]
    for copy in arriving:
        copy.start()

    for side in range(2):
        for q in range(4 * side, 4 * side + 4):

            def put(k, y, rows, q=q):
                r = slice(q * co + k * GROUP, q * co + (k + 1) * GROUP)
                cots[r, y * nz : (y + 1) * nz] = rows

            tiles = Tiles(
                co // GROUP,
                lambda k, q=q, side=side: cot[
                    q, k * GROUP : (k + 1) * GROUP, side * (nx - 1)
                ],
            )
            bring_plane(to_y, tiles, ny, nz, put)

    for copy in arriving:
        copy.wait()

    def block(x, y):
        if y == 0:
            return yraw[0, x * ci : (x + 1) * ci]
        if y == ny + 1:
            return yraw[1, x * ci : (x + 1) * ci]
        if x == 0:
            return xraw[0, (y - 1) * ci : y * ci]
        if x == nx + 1:
            return xraw[1, (y - 1) * ci : y * ci]
        return flat[x - 1, :, (y - 1) * nz : y * nz]

    for x in range(nx + 2):
        for y in range(ny + 2):
            lanes = slice(y * nz, (y + 1) * nz)
            vm[x, :, lanes] = pltpu.roll(block(x, y).astype(F32), 1, 1).astype(BF16)

    def rolled(x, y):
        return vm[x, :, y * nz : (y + 1) * nz]

    def cot_at(q, m, n):
        r = slice(q * co, (q + 1) * co)
        if is_inner(q, m, nx):
            return cot_edge[m + q // 4 - 1, r]
        return cots[r, n * nz : (n + 1) * nz]

    def put_value(q, m, n, value):
        r = slice(q * co, (q + 1) * co)
        if is_inner(q, m, nx):
            val_edge[m + q // 4 - 1, r] = value
        else:
            vals[r, n * nz : (n + 1) * nz] = value

    spots = foreign_spots(nx, ny)

    def put_foreign(key, tz, value):
        pre[spots[key], tz * co : (tz + 1) * co] = value

    leaving = []

    def leave(src, dst):
        leaving.append(pltpu.make_async_copy(src, dst, sems.at[4 + len(leaving)]))
        leaving[-1].start()

    columns = outer_columns(nx, ny)
    sent = 0
    for k, i in enumerate((0, nx, None)):
        c0 = k * (ny + 1)
        some = columns[c0 : c0 + ny + 1] if k < 2 else columns[c0:]
        forward_pass(
            dims, chunk, some, block, rolled, w, cot_at, put_value, put_foreign, ga, gb, c0
        )
        upto = sent + sum(spot[:2] in some for spot in spots)
        leave(pre.at[sent:upto], pre_out.at[sent:upto])
        sent = upto
        if k < 2:
            rows = pl.ds(4 * k * co, 4 * co)
            leave(vals.at[rows], vals_out.at[rows])
        else:
            leave(val_edge, val_edge_out)
    leave(ga, ga_out)
    leave(gb, gb_out)

    def wg_add(part, total):
        total = total + wg_in[:, part * 4 * ci : (part + 1) * 4 * ci]
        for ex in range(2):
            for row in range(8):
                tx, ty, tz = row // 4, row // 2 % 2, row % 2
                index = ((tx * 2 + ty) * 2 + part) * 2 + tz
                wg[ex * 16 + index] = total[
                    row * co : (row + 1) * co, ex * 2 * ci : (ex + 1) * 2 * ci
                ].astype(BF16)

    weight_pass(columns, block, rolled, ga, gb, wg_add)
    for copy in leaving:
        copy.wait()


def last_kernel(
    dims,
    chunk,
    ga_in,
    gb_in,
    pre_in,
    vals_in,
    val_edge_in,
    xlo_in,
    xhi_in,
    ylo_in,
    yhi_in,
    wt_in,
    inner_vals_in,
    ig_in,
    act_out,
    ig_out,
    ga,
    gb,
    pre,
    vals,
    val_edge,
    xraw,
    yraw,
    wt,
    inner_vals,
    ig,
    cots,
    staged,
    ig_staged,
    sems,
):
    nx, ny, nz, ci, co = dims
    to_y = swap_matrix(GROUP, ny)
    to_c = swap_matrix(ny, GROUP)
    skip = (nx + 2) * ci
    early = [(vals_in, vals), (val_edge_in, val_edge), (inner_vals_in, inner_vals)]
    late = [
        (xlo_in, xraw.at[0]),
        (xhi_in, xraw.at[1]),
        (ylo_in.at[skip:], yraw.at[0]),
        (yhi_in.at[skip:], yraw.at[1]),
        (ga_in, ga),
        (gb_in, gb),
        (pre_in, pre),
        (wt_in, wt),
        (ig_in, ig),
    ]
    copies = [
        pltpu.make_async_copy(src, dst, sems.at[k]) for k, (src, dst) in enumerate(early + late)
    ]
    for copy in copies:
        copy.start()
    spot = len(copies)
    for copy in copies[: len(early)]:
        copy.wait()
    leaving = []

    for m in range(nx):
        for q in range(8):
            tiles = []
            for k in range(co // GROUP):
                r = slice(q * co + k * GROUP, q * co + (k + 1) * GROUP)
                rows = []
                for y in range(ny):
                    lanes = slice(y * nz, (y + 1) * nz)
                    if not is_inner(q, m, nx):
                        rows.append(vals[r, lanes])
                    elif y == edge_row(q, ny):
                        rows.append(val_edge[m + q // 4 - 1, r])
                    else:
                        rows.append(inner_vals[m + q // 4 - 1, r, lanes])
                tiles.append(jnp.concatenate(rows, axis=0).reshape(ny, GROUP, nz))
            moved = turn(to_c, tiles, nz)
            index = m * 8 + q
            for k in range(co // GROUP):
                staged[index, k * GROUP : (k + 1) * GROUP] = moved[
                    :, k * nz : (k + 1) * nz
                ].reshape(GROUP, ny, nz)
            leaving.append(
                pltpu.make_async_copy(
                    staged.at[index], act_out.at[q, :, m], sems.at[spot + index]
                )
            )
            leaving[-1].start()

    for copy in copies[len(early) :]:
        copy.wait()
    for side in range(2):
        for p in range(4):

            def put(k, y, rows, side=side, p=p):
                r = slice(p * co + k * GROUP, p * co + (k + 1) * GROUP)
                cots[side, r, y * nz : (y + 1) * nz] = rows

            tiles = Tiles(
                co // GROUP,
                lambda k, side=side, p=p: xraw[side, p, k * GROUP : (k + 1) * GROUP],
            )
            bring_plane(to_y, tiles, ny, nz, put)

    spots = foreign_spots(nx, ny)
    first = lax.broadcasted_iota(jnp.int32, (co, nz), 1) == 0
    corner = 4 * co * nx

    def foreign(i, j, tx, ty, tz):
        sx, sy, sz = 1 - tx, 1 - ty, 1 - tz
        m, n = i - sx, j - sy
        if 0 <= n < ny:
            side = 0 if m < 0 else 1
            r = (2 * sy + sz) * co
            cot = cots[side, r : r + co, n * nz : (n + 1) * nz]
        else:
            end = 0 if n < 0 else 1
            if 0 <= m < nx:
                r = ((m * 2 + sx) * 2 + sz) * co
            else:
                r = corner + ((0 if m < 0 else 2) + sz) * co
            cot = yraw[end, r : r + co]
        cot = cot.astype(F32)
        if sz == 1:
            cot = pltpu.roll(cot, 1, 1)
        before = pre[spots[i, j, tx, ty], tz * co : (tz + 1) * co]
        sig = 0.5 * jnp.tanh(0.5 * before) + 0.5
        grad = cot * (sig + before * sig * (1.0 - sig))
        whole = grad.astype(BF16)
        cut = jnp.where(first, 0.0, grad).astype(BF16)
        return (whole, cut) if sz == 1 else (cut, whole)

    def cut_grads(c0, some):
        lefts, rights = [], []
        for k, (i, j) in enumerate(some):
            wide = slice((c0 + k) * nz, (c0 + k + 1) * nz)
            left, right = [], []
            for tx in range(2):
                for ty in range(2):
                    base = (2 * tx + ty) * 2 * co
                    if (i, j, tx, ty) in spots:
                        for tz in range(2):
                            one, two = foreign(i, j, tx, ty, tz)
                            left.append(one)
                            right.append(two)
                    else:
                        left.append(ga[base : base + 2 * co, wide])
                        right.append(gb[base : base + 2 * co, wide])
            lefts.append(jnp.concatenate(left, axis=0))
            rights.append(jnp.concatenate(right, axis=0))
        return jnp.concatenate(lefts, axis=1), jnp.concatenate(rights, axis=1)

    def ig_add(m, y, value, fresh):
        lanes = slice(y * nz, (y + 1) * nz)
        ig[m, :, lanes] = ig[m, :, lanes] + value

    input_pass(dims, chunk, outer_columns(nx, ny), wt, cut_grads, ig_add)
    for m in range(nx):
        for k in range(0, ci // GROUP, 2):
            tiles = []
            for h in range(2):
                r = slice((k + h) * GROUP, (k + h + 1) * GROUP)
                rows = [
                    ig[m, r, y * nz : (y + 1) * nz].astype(BF16) for y in range(ny)
                ]
                tiles.append(jnp.concatenate(rows, axis=0).reshape(ny, GROUP, nz))
            moved = turn(to_c, tiles, nz)
            for h in range(2):
                ig_staged[(k + h) * GROUP : (k + h + 1) * GROUP, m] = moved[
                    :, h * nz : (h + 1) * nz
                ].reshape(GROUP, ny, nz)
    leaving.append(pltpu.make_async_copy(ig_staged, ig_out, sems.at[spot + 8 * nx]))
    leaving[-1].start()
    for copy in leaving:
        copy.wait()


def unpack_kernel(co, ci, packed, out):
    for ex in range(2):
        for tx in range(2):
            for ty in range(2):
                for ez in range(2):
                    for tz in range(2):
                        index = (((ex * 2 + tx) * 2 + ty) * 2 + ez) * 2 + tz
                        pair = packed[index].astype(F32)
                        for ey in range(2):
                            out[2 * ex + tx, 2 * ey + ty, 2 * ez + tz] = pair[
                                :, ey * ci : (ey + 1) * ci
                            ]


def far(shape, dtype):
    return pltpu.HBM(shape, dtype)


def stay(array):
    return pltpu.with_memory_space_constraint(array, pltpu.HBM)


def neighbours(axis):
    count = lax.axis_size(axis)
    up = [(i, i + 1) for i in range(count - 1)]
    return up, [(b, a) for a, b in up]


def on_device(volume, kernel, cotangent):
    ci, nx, ny, nz = volume.shape
    co = kernel.shape[3]
    gx, gy = lax.axis_size("gx"), lax.axis_size("gy")
    gx_up, gx_down = neighbours("gx")
    gy_up, gy_down = neighbours("gy")
    cells = nx * gx * ny * gy * nz
    dims = (nx, ny, nz, ci, co)

    cot = cotangent.reshape(8, co, nx, ny, nz)

    def corner(sx, sy):
        m, n = (nx - 1) * sx, (ny - 1) * sy
        return cotangent[sx, sy, :, :, m, n].reshape(2 * co, nz)

    def x_message(sx):
        plane = volume[:, (nx - 1) * sx].transpose(1, 0, 2).reshape(ny * ci, nz)
        return jnp.concatenate([plane, corner(sx, 0), corner(sx, 1)], axis=0)

    xlo = lax.ppermute(x_message(1), "gx", gx_up)
    xhi = lax.ppermute(x_message(0), "gx", gx_down)

    vmem = pl.BlockSpec(memory_space=pltpu.VMEM)
    smem = pl.BlockSpec(memory_space=pltpu.SMEM)
    anywhere = pl.BlockSpec(memory_space=pl.ANY)
    hbm = pl.BlockSpec(memory_space=pltpu.HBM)
    params = pltpu.CompilerParams(vmem_limit_bytes=24 * 1024 * 1024)
    n_in = (nx - 1) * (ny - 1)
    n_out = 2 * (ny + 1) + 2 * (nx - 1)
    flat, w, wt, inner_vals, cot_edge, wg_part, ig_part, face_up, face_down = pl.pallas_call(
        functools.partial(inner_kernel, dims, 5),
        out_shape=(
            jax.ShapeDtypeStruct((nx, ci, ny * nz), BF16),
            jax.ShapeDtypeStruct((8 * co, 8 * ci), BF16),
            far((8 * ci, 8 * co), BF16),
            far((nx - 1, 8 * co, ny * nz), BF16),
            jax.ShapeDtypeStruct((nx - 1, 8 * co, nz), BF16),
            jax.ShapeDtypeStruct((8 * co, 8 * ci), F32),
            far((nx, ci, ny * nz), F32),
            far((4, co, ny, nz), BF16),
            far((4, co, ny, nz), BF16),
        ),
        in_specs=[anywhere, anywhere, vmem],
        out_specs=(vmem, vmem, hbm, hbm, vmem, vmem, hbm, hbm, hbm),
        scratch_shapes=[
            pltpu.VMEM((8 * ci, 8 * co), BF16),
            pltpu.VMEM((nx - 1, 8 * co, ny * nz), BF16),
            pltpu.VMEM((nx, ci, ny * nz), F32),
            pltpu.VMEM(volume.shape, BF16),
            pltpu.VMEM(kernel.shape, BF16),
            pltpu.SemaphoreType.DMA((7,)),
            pltpu.VMEM((nx, ci, ny * nz), BF16),
            pltpu.VMEM((8 * co, n_in * nz), BF16),
            pltpu.VMEM((8 * co, n_in * nz), BF16),
            pltpu.VMEM((nx - 1, 8 * co, ny * nz), BF16),
        ],
        compiler_params=params,
    )(volume, kernel, cot)

    def y_message(sy):
        y = (ny - 1) * sy
        rows = slice(y * ci, (y + 1) * ci)
        own = cotangent[:, sy, :, :, :, y].transpose(3, 0, 1, 2, 4).reshape(4 * co * nx, nz)
        corner = slice((ny * ci + sy * 2 * co), (ny * ci + (sy + 1) * 2 * co))
        return jnp.concatenate(
            [
                xlo[rows],
                flat[:, :, y * nz : (y + 1) * nz].reshape(nx * ci, nz),
                xhi[rows],
                own,
                xlo[corner],
                xhi[corner],
            ],
            axis=0,
        )

    ylo = lax.ppermute(y_message(1), "gy", gy_up)
    yhi = lax.ppermute(y_message(0), "gy", gy_down)
    face_lo = lax.ppermute(face_up, "gx", gx_up)
    face_hi = lax.ppermute(face_down, "gx", gx_down)
    foreign = len(foreign_spots(nx, ny))
    pre_shape = (foreign, 2 * co, nz)
    pre, vals, val_edge, ga, gb, wg = pl.pallas_call(
        functools.partial(outer_kernel, dims, 4),
        out_shape=(
            far(pre_shape, F32),
            far((8 * co, ny * nz), BF16),
            far((nx - 1, 8 * co, nz), BF16),
            far((8 * co, n_out * nz), BF16),
            far((8 * co, n_out * nz), BF16),
            jax.ShapeDtypeStruct((32, co, 2 * ci), BF16),
        ),
        in_specs=[vmem] + [anywhere] * 4 + [vmem] * 4,
        out_specs=(hbm,) * 5 + (vmem,),
        scratch_shapes=[
            pltpu.VMEM((8 * co, n_out * nz), BF16),
            pltpu.VMEM((8 * co, n_out * nz), BF16),
            pltpu.VMEM((nx + 2, ci, (ny + 2) * nz), BF16),
            pltpu.VMEM(pre_shape, F32),
            pltpu.VMEM((8 * co, ny * nz), BF16),
            pltpu.VMEM((nx - 1, 8 * co, nz), BF16),
            pltpu.VMEM((2, ny * ci, nz), BF16),
            pltpu.VMEM((2, (nx + 2) * ci, nz), BF16),
            pltpu.VMEM((8 * co, ny * nz), BF16),
            pltpu.SemaphoreType.DMA((12,)),
        ],
        compiler_params=params,
    )(flat, xlo, xhi, ylo, yhi, w, cot, cot_edge, wg_part)
    passed = [
        stay(array)
        for array in (ga, gb, pre, vals, val_edge, ylo, yhi, wt, inner_vals, ig_part)
    ]
    passed[5:5] = [face_lo, face_hi]
    act, input_grad = pl.pallas_call(
        functools.partial(last_kernel, dims, 4),
        out_shape=(
            jax.ShapeDtypeStruct(cot.shape, BF16),
            jax.ShapeDtypeStruct(volume.shape, BF16),
        ),
        in_specs=[hbm] * 5 + [anywhere] * 2 + [hbm] * 5,
        out_specs=(anywhere,) * 2,
        scratch_shapes=[
            pltpu.VMEM((8 * co, n_out * nz), BF16),
            pltpu.VMEM((8 * co, n_out * nz), BF16),
            pltpu.VMEM(pre_shape, F32),
            pltpu.VMEM((8 * co, ny * nz), BF16),
            pltpu.VMEM((nx - 1, 8 * co, nz), BF16),
            pltpu.VMEM((2, 4, co, ny, nz), BF16),
            pltpu.VMEM((2, 4 * co * nx + 4 * co, nz), BF16),
            pltpu.VMEM((8 * ci, 8 * co), BF16),
            pltpu.VMEM((nx - 1, 8 * co, ny * nz), BF16),
            pltpu.VMEM((nx, ci, ny * nz), F32),
            pltpu.VMEM((2, 4 * co, ny * nz), BF16),
            pltpu.VMEM((8 * nx, co, ny, nz), BF16),
            pltpu.VMEM(volume.shape, BF16),
            pltpu.SemaphoreType.DMA((13 + 8 * nx,)),
        ],
        compiler_params=params,
    )(*passed)

    scale = 1.0 / math.sqrt(cells)
    devices = gx * gy
    shares = wg.reshape(devices, 32 * co // devices, 2 * ci)
    shares = lax.all_to_all(shares, ("gx", "gy"), 0, 0, tiled=True)
    piece = (jnp.sum(shares.astype(F32), axis=0) * scale).astype(BF16)
    pieces = jnp.broadcast_to(piece[None], (devices,) + piece.shape)
    pieces = lax.all_to_all(pieces, ("gx", "gy"), 0, 0, tiled=True)
    weight_grad = pl.pallas_call(
        functools.partial(unpack_kernel, co, ci),
        out_shape=jax.ShapeDtypeStruct((4, 4, 4, co, ci), F32),
        in_specs=[vmem],
        out_specs=vmem,
        compiler_params=pltpu.CompilerParams(vmem_limit_bytes=8 * 1024 * 1024),
    )(pieces.reshape(32, co, 2 * ci))

    return act.reshape(cotangent.shape), input_grad, weight_grad


def solution(mesh):
    placed = (P(None, "gx", "gy", None), P(), P(None, None, None, None, "gx", "gy", None))
    return jax.shard_map(
        on_device,
        mesh=mesh,
        in_specs=placed,
        out_specs=(placed[2], placed[0], P()),
        check_vma=False,
    )
```
